32 devices in a mesh: dp: 16 (over z, y, core), seq: 2 (over x).
Axes of the slice: x: 2, y: 2, z: 4, core: 2. Of those that a mesh axis runs over, the one named last changes fastest.
Arguments:
- inputs: bfloat16 [16, 1024, 768], P('dp', 'seq'), may hold values from -6 to 6
- vectors: bfloat16 [768, 8], P('dp'), may hold values from -2 to 2, as said below
- w_qkv: bfloat16 [768, 2304], P('dp', 'seq'), may hold values from -0.21875 to 0.21875
- w_out: bfloat16 [768, 768], P('dp', 'seq'), may hold values from -1.25 to 1.25
- w_up: bfloat16 [768, 3072], P('dp', 'seq'), may hold values from -0.21875 to 0.21875
- w_down: bfloat16 [768, 3072], P('dp', 'seq'), may hold values from -0.109375 to 0.109375
- up_bias: bfloat16 [3072], P(('dp', 'seq')), may hold values from -3 to 3
- cotangent: bfloat16 [16, 1024, 768], P('dp', 'seq'), may hold values from -6 to 6
Outputs:
- result: bfloat16 [16, 1024, 768], P('dp', 'seq')
- input_grad: float32 [16, 1024, 768], P('dp', 'seq')
- grad_qkv: float32 [768, 2304], P('dp', 'seq')
- grad_out: float32 [768, 768], P('dp', 'seq')
- grad_up: float32 [768, 3072], P('dp', 'seq')
- grad_down: float32 [768, 3072], P('dp', 'seq')
- grad_up_bias: float32 [3072], P(('dp', 'seq'))
- grad_vectors: float32 [768, 8], P('dp')
The draws below stay inside these ranges and needn't reach their ends.
Inputs may be any that keep to these rules, and one draw needn't show every extreme that they name: `vectors`: columns 0 and 5 are the two norms' scales, between 0.5 and 1.5; the other columns are shifts and biases.
All inputs are finite; a program needn't handle non-finite values.
Results may differ from the reference program's by a relative error of at most 0.018.
Values may be sent and summed in bfloat16 or wider, within the bound.
No kernel may reach another device: no remote copies, remote signals or barrier semaphores. Data moves between devices by JAX's collectives and lax.ppermute only.
A program may use at most 192 MiB of HBM per device.

```python
import jax
import jax.numpy as jnp
from jax import lax

D = 768
HEADS = 12
HEAD_DIM = 64
FF = 3072
LENGTH = 1024
SEQS = 16


def draw_vectors(key, part):
    key = jax.random.fold_in(key, 11)
    scale_draw = jax.random.uniform(jax.random.fold_in(key, 1), (D, 8), jnp.float32, 0.5, 1.5)
    shift_draw = jnp.clip(0.5 * jax.random.normal(jax.random.fold_in(key, 2), (D, 8), jnp.float32), -2.0, 2.0)
    column = jnp.arange(8)
    chosen = (column == 0) | (column == 5)
    return jnp.where(chosen[None, :], scale_draw, shift_draw).astype(jnp.bfloat16)


def block_levels(stream_key, dims, split, low, largest):
    gain = 1.0
    for axis_at, shards_of in split:
        heights = jax.random.uniform(jax.random.fold_in(jax.random.fold_in(stream_key, 6), axis_at), (shards_of,), jnp.float32, low / len(split), largest / len(split))
        gain = gain * jnp.repeat(jnp.exp(heights), dims[axis_at] // shards_of).reshape((-1,) + (1,) * (len(dims) - 1 - axis_at))
    return gain


def noise(own_key, extent, width, limit, split=(), held_as=jnp.bfloat16):
    drawn = width * jax.random.normal(own_key, extent, jnp.float32)
    if split:
        drawn = drawn * block_levels(own_key, extent, split, -0.22, 0.18)
    return jnp.clip(drawn, -limit, limit).astype(held_as)


def setup_inputs(seed: int = 0) -> dict:
    seeds = jax.random.split(jax.random.key(seed), 9)
    inputs = noise(seeds[0], (SEQS, LENGTH, D), 1.0, 6.0, ((0, 16), (1, 2)))
    vectors = draw_vectors(jax.random.fold_in(seeds[8], 71), 0)
    w_qkv = noise(seeds[2], (D, 3 * D), D ** -0.5, 0.21875, ((0, 16), (1, 2)))
    w_out = noise(seeds[3], (D, D), (D // 32) ** -0.5, 1.25, ((0, 16), (1, 2)))
    w_up = noise(seeds[4], (D, FF), D ** -0.5, 0.21875, ((0, 16), (1, 2)))
    w_down = noise(seeds[5], (D, FF), FF ** -0.5, 0.109375, ((0, 16), (1, 2)))
    up_bias = noise(seeds[6], (FF,), 0.5, 3.0, ((0, 32),))
    cotangent = noise(seeds[7], (SEQS, LENGTH, D), 1.0, 6.0, ((0, 16), (1, 2)))
    return {"inputs": inputs, "vectors": vectors, "w_qkv": w_qkv, "w_out": w_out, "w_up": w_up, "w_down": w_down, "up_bias": up_bias, "cotangent": cotangent}


@jax.custom_vjp
def low(v):
    return lax.optimization_barrier(v.astype(jnp.bfloat16)).astype(jnp.float32)

@jax.custom_vjp
def low_back(v):
    return v

def low_keep(v):
    return (low(v), None)

def low_pass(kept, grad):
    return (grad,)

def back_keep(v):
    return (v, None)

def back_low(kept, grad):
    return (low(grad),)
low.defvjp(low_keep, low_pass)
low_back.defvjp(back_keep, back_low)
EPSILON = 1e-05
PRECISE = lax.Precision.HIGHEST
MASKED = -1e+30

def norm_rows(values, scale_row, shift_row):
    row_mean = lax.optimization_barrier(jnp.mean(values, axis=-1, keepdims=True))
    centered = values - row_mean
    variance = lax.optimization_barrier(jnp.mean(centered * centered, axis=-1, keepdims=True))
    return centered * lax.rsqrt(variance + EPSILON) * scale_row + shift_row

def gelu_tanh(values):
    return 0.5 * values * (1.0 + jnp.tanh(0.7978845608028654 * (values + 0.044715 * values * values * values)))

def attend_sequence(qkv_rows):
    queries = qkv_rows[:, :D].reshape(LENGTH, HEADS, HEAD_DIM)
    keys_all = qkv_rows[:, D:2 * D].reshape(LENGTH, HEADS, HEAD_DIM)
    values_all = qkv_rows[:, 2 * D:].reshape(LENGTH, HEADS, HEAD_DIM)
    scores = jnp.einsum('qhd,khd->hqk', queries, keys_all, precision=PRECISE) * HEAD_DIM ** (-0.5)
    scores = low_back(scores)
    positions = jnp.arange(LENGTH)
    causal = positions[None, :] <= positions[:, None]
    scores = jnp.where(causal[None], scores, MASKED)
    row_top = lax.optimization_barrier(jnp.max(scores, axis=-1, keepdims=True))
    exp_scores = jnp.exp(scores - row_top)
    attn_probs = exp_scores / lax.optimization_barrier(jnp.sum(exp_scores, axis=-1, keepdims=True))
    mixed_heads = jnp.einsum('hqk,khd->qhd', low(attn_probs), values_all, precision=PRECISE)
    return mixed_heads.reshape(LENGTH, D)

def forward(resid_in, vectors, w_qkv, w_out, w_up, w_down, up_bias):
    normed_one = low(norm_rows(resid_in, vectors[:, 0], vectors[:, 1]))
    qkv_bias = jnp.concatenate([vectors[:, 2], jnp.zeros_like(vectors[:, 2]), vectors[:, 3]])
    qkv_rows = low(low_back(jnp.dot(normed_one, w_qkv, precision=PRECISE) + qkv_bias))
    attended = lax.map(jax.checkpoint(attend_sequence), qkv_rows.reshape(SEQS, LENGTH, 3 * D))
    attended = low(low_back(attended.reshape(SEQS * LENGTH, D)))
    branch_attn = low_back(jnp.dot(attended, w_out, precision=PRECISE) + vectors[:, 4])
    middle = resid_in + branch_attn
    normed_two = low(norm_rows(middle, vectors[:, 5], vectors[:, 6]))
    up_act = low_back(jnp.dot(normed_two, w_up, precision=PRECISE) + up_bias)
    hidden = low(gelu_tanh(up_act))
    branch_mlp = low_back(jnp.dot(hidden, w_down.T, precision=PRECISE) + vectors[:, 7])
    return middle + branch_mlp

def reference(inputs, vectors, w_qkv, w_out, w_up, w_down, up_bias, cotangent):
    resid_in = inputs.astype(jnp.float32).reshape(SEQS * LENGTH, D)
    result, pull_back = jax.vjp(forward, resid_in, vectors.astype(jnp.float32), w_qkv.astype(jnp.float32), w_out.astype(jnp.float32), w_up.astype(jnp.float32), w_down.astype(jnp.float32), up_bias.astype(jnp.float32))
    grads = pull_back(cotangent.astype(jnp.float32).reshape(SEQS * LENGTH, D))
    return (result.astype(jnp.bfloat16).reshape(SEQS, LENGTH, D), grads[0].reshape(SEQS, LENGTH, D), grads[2], grads[3], grads[4], grads[5], grads[6], grads[1])
```

```python
import functools
import math

import jax
import jax.numpy as jnp
from jax import lax
from jax.experimental import pallas as pl
from jax.experimental.pallas import tpu as pltpu
from jax.sharding import PartitionSpec as P

HEADS = 12
HEAD_DIM = 64
VMEM_LIMIT = 48 * 1024 * 1024


EPSILON = 1e-05
MASKED = -1e30


def norm_rows(values, scale_row, shift_row):
    row_mean = jnp.mean(values, axis=-1, keepdims=True)
    centered = values - row_mean
    variance = jnp.mean(centered * centered, axis=-1, keepdims=True)
    return centered * lax.rsqrt(variance + EPSILON) * scale_row + shift_row


def gelu_tanh(values):
    return (
        0.5
        * values
        * (1.0 + jnp.tanh(0.7978845608028654 * (values + 0.044715 * values * values * values)))
    )


def contract_last(left_side, right_side):
    return lax.dot_general(
        left_side, right_side, (((1,), (1,)), ((), ())), preferred_element_type=jnp.float32
    )


def contract_first(left_side, right_side):
    return lax.dot_general(
        left_side, right_side, (((0,), (0,)), ((), ())), preferred_element_type=jnp.float32
    )


def on_device_general(inputs, vectors, w_qkv, w_out, w_up, w_down, up_bias, cotangent):
    seq_count, piece_len, model_width = inputs.shape
    row_count = seq_count * piece_len
    score_scale = HEAD_DIM ** (-0.5)
    seq_index = lax.axis_index("seq")
    query_pos = seq_index * piece_len + jnp.arange(piece_len)
    qkv_cols, out_cols, up_cols, down_cols, upb_cols = (
        lax.all_gather(w_qkv, "seq", axis=1, tiled=True),
        lax.all_gather(w_out, "seq", axis=1, tiled=True),
        lax.all_gather(w_up, "seq", axis=1, tiled=True),
        lax.all_gather(w_down, "seq", axis=1, tiled=True),
        lax.all_gather(up_bias, "seq", axis=0, tiled=True),
    )
    full_fwd = (
        lax.all_gather(qkv_cols, "dp", axis=0, tiled=True),
        lax.all_gather(out_cols, "dp", axis=0, tiled=True),
        lax.all_gather(up_cols, "dp", axis=0, tiled=True),
        lax.all_gather(down_cols, "dp", axis=0, tiled=True),
        lax.all_gather(upb_cols, "dp", axis=0, tiled=True),
        lax.all_gather(vectors, "dp", axis=0, tiled=True),
    )
    qkv_full, out_full, up_full, down_full, upb_full, vec_full = full_fwd
    vec_values = vec_full.astype(jnp.float32)
    resid_in = inputs.reshape(row_count, model_width).astype(jnp.float32)
    normed_one = norm_rows(resid_in, vec_values[:, 0], vec_values[:, 1]).astype(jnp.bfloat16)
    qkv_bias = jnp.concatenate(
        [vec_values[:, 2], jnp.zeros_like(vec_values[:, 2]), vec_values[:, 3]]
    )
    qkv_rows = (
        jnp.dot(normed_one, qkv_full, preferred_element_type=jnp.float32) + qkv_bias
    ).astype(jnp.bfloat16)
    queries = qkv_rows[:, :model_width].reshape(seq_count, piece_len, HEADS, HEAD_DIM)
    key_vals = qkv_rows[:, model_width:].reshape(seq_count, piece_len, 2 * model_width)

    def block_scores(key_block, first_row):
        key_rows = key_block.shape[1]
        keys_part = key_block[..., :model_width].reshape(seq_count, key_rows, HEADS, HEAD_DIM)
        scores = (
            jnp.einsum("bqhd,bkhd->bhqk", queries, keys_part, preferred_element_type=jnp.float32)
            * score_scale
        )
        causal = (first_row + jnp.arange(key_rows))[None, :] <= query_pos[:, None]
        return jnp.where(causal, scores, MASKED)

    key_block = lax.all_gather(key_vals, "seq", axis=1, tiled=True)
    run_max = jnp.full((seq_count, HEADS, piece_len), MASKED, jnp.float32)
    key_rows = key_block.shape[1]
    values_part = key_block[..., model_width:].reshape(seq_count, key_rows, HEADS, HEAD_DIM)
    scores = block_scores(key_block, jnp.int32(0))
    new_max = jnp.maximum(run_max, jnp.max(scores, axis=-1))
    exp_scores = jnp.exp(scores - new_max[..., None])
    run_total = jnp.sum(exp_scores, axis=-1)
    added_part = jnp.einsum(
        "bhqk,bkhd->bqhd",
        exp_scores.astype(jnp.bfloat16),
        values_part,
        preferred_element_type=jnp.float32,
    )
    run_acc = added_part
    run_max, run_total, run_acc = (new_max, run_total, run_acc)
    attended = run_acc / jnp.transpose(run_total, (0, 2, 1))[..., None]
    log_total = run_max + jnp.log(run_total)
    attended_lo = attended.reshape(row_count, model_width).astype(jnp.bfloat16)
    branch_attn = (
        jnp.dot(attended_lo, out_full, preferred_element_type=jnp.float32) + vec_values[:, 4]
    )
    middle = resid_in + branch_attn
    normed_two = norm_rows(middle, vec_values[:, 5], vec_values[:, 6]).astype(jnp.bfloat16)
    up_act = jnp.dot(normed_two, up_full, preferred_element_type=jnp.float32) + upb_full.astype(
        jnp.float32
    )
    hidden = gelu_tanh(up_act).astype(jnp.bfloat16)
    branch_mlp = contract_last(hidden, down_full) + vec_values[:, 7]
    result = middle + branch_mlp
    qkv_back, out_back, up_back, down_back = (qkv_full, out_full, up_full, down_full)
    out_grad = cotangent.reshape(row_count, model_width).astype(jnp.float32)
    mlp_grad = out_grad.astype(jnp.bfloat16)
    hidden_grad = jnp.dot(mlp_grad, down_back, preferred_element_type=jnp.float32)
    gelu_pull = jax.vjp(gelu_tanh, up_act)[1]
    up_grad = gelu_pull(hidden_grad)[0].astype(jnp.bfloat16)
    norm_two_grad = contract_last(up_grad, up_back)
    ln_two_pull = jax.vjp(norm_rows, middle, vec_values[:, 5], vec_values[:, 6])[1]
    middle_part, scale_two, shift_two = ln_two_pull(norm_two_grad)
    middle_grad = out_grad + middle_part
    attn_out_grad = middle_grad.astype(jnp.bfloat16)
    attended_grad = contract_last(attn_out_grad, out_back).astype(jnp.bfloat16)
    grad_heads = attended_grad.reshape(seq_count, piece_len, HEADS, HEAD_DIM)
    row_delta = jnp.transpose(
        jnp.sum(grad_heads.astype(jnp.float32) * attended, axis=-1), (0, 2, 1)
    )
    key_vals_all = lax.all_gather(key_vals, "seq", axis=1, tiled=True)
    total_len = key_vals_all.shape[1]
    key_block_len = math.gcd(total_len, 512)

    def back_step(query_acc, block_index):
        first_row = block_index * key_block_len
        key_block = lax.dynamic_slice_in_dim(key_vals_all, first_row, key_block_len, 1)
        keys_part = key_block[..., :model_width].reshape(seq_count, key_block_len, HEADS, HEAD_DIM)
        values_part = key_block[..., model_width:].reshape(
            seq_count, key_block_len, HEADS, HEAD_DIM
        )
        scores = block_scores(key_block, first_row)
        attn_probs = jnp.exp(scores - log_total[..., None])
        prob_grad = jnp.einsum(
            "bqhd,bkhd->bhqk", grad_heads, values_part, preferred_element_type=jnp.float32
        )
        score_grad = (attn_probs * (prob_grad - row_delta[..., None])).astype(jnp.bfloat16)
        step_part = jnp.einsum(
            "bhqk,bkhd->bqhd", score_grad, keys_part, preferred_element_type=jnp.float32
        )
        key_grad = (
            jnp.einsum("bhqk,bqhd->bkhd", score_grad, queries, preferred_element_type=jnp.float32)
            * score_scale
        )
        value_grad = jnp.einsum(
            "bhqk,bqhd->bkhd",
            attn_probs.astype(jnp.bfloat16),
            grad_heads,
            preferred_element_type=jnp.float32,
        )
        key_value = jnp.concatenate(
            [
                key_grad.reshape(seq_count, key_block_len, model_width),
                value_grad.reshape(seq_count, key_block_len, model_width),
            ],
            axis=-1,
        )
        return (query_acc + step_part * score_scale, key_value)

    query_grad, kv_blocks = lax.scan(
        back_step,
        jnp.zeros((seq_count, piece_len, HEADS, HEAD_DIM), jnp.float32),
        jnp.arange(total_len // key_block_len),
    )
    kv_terms = jnp.moveaxis(kv_blocks, 0, 1).reshape(seq_count, total_len, 2 * model_width)
    key_val_grad = lax.psum_scatter(
        kv_terms.astype(jnp.bfloat16), "seq", scatter_dimension=1, tiled=True
    ).astype(jnp.float32)
    key_val_grad = key_val_grad.reshape(row_count, 2 * model_width)
    qkv_grad = jnp.concatenate(
        [query_grad.reshape(row_count, model_width), key_val_grad], axis=1
    ).astype(jnp.bfloat16)
    norm_one_grad = contract_last(qkv_grad, qkv_back)
    ln_one_pull = jax.vjp(norm_rows, resid_in, vec_values[:, 0], vec_values[:, 1])[1]
    input_part, scale_one, shift_one = ln_one_pull(norm_one_grad)
    input_grad = middle_grad + input_part
    whole_qkv = contract_first(normed_one, qkv_grad)
    whole_out = contract_first(attended_lo, attn_out_grad)
    whole_up = contract_first(normed_two, up_grad)
    whole_down = contract_first(mlp_grad, hidden)
    row_qkv, row_out, row_up, row_down = (
        lax.psum_scatter(
            whole_qkv.astype(jnp.bfloat16), "dp", scatter_dimension=0, tiled=True
        ).astype(jnp.float32),
        lax.psum_scatter(
            whole_out.astype(jnp.bfloat16), "dp", scatter_dimension=0, tiled=True
        ).astype(jnp.float32),
        lax.psum_scatter(
            whole_up.astype(jnp.bfloat16), "dp", scatter_dimension=0, tiled=True
        ).astype(jnp.float32),
        lax.psum_scatter(
            whole_down.astype(jnp.bfloat16), "dp", scatter_dimension=0, tiled=True
        ).astype(jnp.float32),
    )
    grad_qkv, grad_out, grad_up, grad_down = (
        lax.psum_scatter(
            row_qkv.astype(jnp.bfloat16), "seq", scatter_dimension=1, tiled=True
        ).astype(jnp.float32),
        lax.psum_scatter(
            row_out.astype(jnp.bfloat16), "seq", scatter_dimension=1, tiled=True
        ).astype(jnp.float32),
        lax.psum_scatter(
            row_up.astype(jnp.bfloat16), "seq", scatter_dimension=1, tiled=True
        ).astype(jnp.float32),
        lax.psum_scatter(
            row_down.astype(jnp.bfloat16), "seq", scatter_dimension=1, tiled=True
        ).astype(jnp.float32),
    )
    vec_term = jnp.stack(
        [
            scale_one,
            shift_one,
            jnp.sum(qkv_grad[:, :model_width].astype(jnp.float32), axis=0),
            jnp.sum(qkv_grad[:, 2 * model_width :].astype(jnp.float32), axis=0),
            jnp.sum(attn_out_grad.astype(jnp.float32), axis=0),
            scale_two,
            shift_two,
            jnp.sum(mlp_grad.astype(jnp.float32), axis=0),
        ],
        axis=1,
    )
    upb_term = jnp.sum(up_grad.astype(jnp.float32), axis=0)
    vec_sum, upb_sum = lax.psum((vec_term, upb_term), ("dp", "seq"))
    vec_rows = vectors.shape[0]
    grad_vectors = lax.dynamic_slice_in_dim(vec_sum, lax.axis_index("dp") * vec_rows, vec_rows, 0)
    upb_rows = up_bias.shape[0]
    upb_start = (lax.axis_index("dp") * lax.axis_size("seq") + seq_index) * upb_rows
    grad_up_bias = lax.dynamic_slice_in_dim(upb_sum, upb_start, upb_rows, 0)
    return (
        result.reshape(seq_count, piece_len, model_width).astype(jnp.bfloat16),
        input_grad.reshape(seq_count, piece_len, model_width),
        grad_qkv,
        grad_out,
        grad_up,
        grad_down,
        grad_up_bias,
        grad_vectors,
    )


def bit_masks(count):
    return [1 << k for k in range(count.bit_length() - 1)]


def hops(n_dp, n_seq, seq_first):
    dp_bits = bit_masks(n_dp)
    far = [("dp", mask) for mask in reversed(dp_bits[2:])]
    middle = [("dp", mask) for mask in dp_bits[1:2]]
    across = [("seq", mask) for mask in reversed(bit_masks(n_seq))]
    near = [("dp", mask) for mask in dp_bits[:1]]
    return far + (across + middle if seq_first else middle + across) + near


def exchange(values, hop, sizes):
    axis, mask = hop
    return lax.ppermute(values, axis, [(i, i ^ mask) for i in range(sizes[axis])])


def slot_owner(slot, path):
    offset = {"dp": 0, "seq": 0}
    for k, (axis, mask) in enumerate(path):
        if slot >> k & 1:
            offset[axis] ^= mask
    return offset["dp"], offset["seq"]


def gather_slots(block, path, sizes):
    held = block[None]
    for hop in path[:-1]:
        held = jnp.concatenate([held, exchange(held, hop, sizes)], axis=0)
    return held, exchange(held, path[-1], sizes)


def place_kernel(path, rows, first, cols, stride, me_ref, held_ref, other_ref, out_ref, sem):
    half = 1 << (len(path) - 1)
    copies = []
    for slot in range(2 * half):
        off_dp, off_seq = slot_owner(slot, path)
        row = pl.multiple_of((me_ref[0] ^ off_dp) * rows, 16)
        col = pl.multiple_of((me_ref[1] ^ off_seq) * stride, 128)
        src = (held_ref if slot < half else other_ref).at[slot % half, :, pl.ds(first, cols)]
        dst = out_ref.at[pl.ds(row, rows), pl.ds(col, cols)]
        copies.append(pltpu.make_async_copy(src, dst, sem.at[slot]))
    for copy in copies:
        copy.start()
    for copy in copies:
        copy.wait()


def place(held, other, path, sizes, pair, first, cols):
    half, rows, _ = held.shape
    whole_seq = any(axis == "seq" for axis, _ in path)
    shape = (rows * sizes["dp"], cols * (sizes["seq"] if whole_seq else 1))
    return pl.pallas_call(
        functools.partial(place_kernel, path, rows, first, cols, cols if whole_seq else 0),
        out_shape=jax.ShapeDtypeStruct(shape, held.dtype),
        in_specs=[pl.BlockSpec(memory_space=pltpu.SMEM)] + [pl.BlockSpec(memory_space=pl.ANY)] * 2,
        out_specs=pl.BlockSpec(memory_space=pltpu.VMEM),
        scratch_shapes=[pltpu.SemaphoreType.DMA((2 * half,))],
        compiler_params=pltpu.CompilerParams(vmem_limit_bytes=VMEM_LIMIT),
        cost_estimate=pl.CostEstimate(
            flops=0, bytes_accessed=4 * shape[0] * shape[1], transcendentals=0
        ),
    )(pair, held, other)


def split_kernel(path, rows, widths, strides, me_ref, *refs):
    wholes, keep_ref, send_ref, sem = refs[: len(widths)], refs[-3], refs[-2], refs[-1]
    half = 1 << (len(path) - 1)
    copies = []
    for slot in range(2 * half):
        off_dp, off_seq = slot_owner(slot, path)
        row = pl.multiple_of((me_ref[0] ^ off_dp) * rows, 16)
        at = 0
        for k, (whole_ref, width) in enumerate(zip(wholes, widths)):
            col = pl.multiple_of((me_ref[1] ^ off_seq) * strides[k], 128)
            src = whole_ref.at[pl.ds(row, rows), pl.ds(col, width)]
            target = keep_ref if slot < half else send_ref
            dst = target.at[slot % half, :, pl.ds(at, width)]
            copies.append(pltpu.make_async_copy(src, dst, sem.at[slot, k]))
            at += width
    for copy in copies:
        copy.start()
    for copy in copies:
        copy.wait()


def split(wholes, path, sizes, pair):
    whole_seq = any(axis == "seq" for axis, _ in path)
    rows = wholes[0].shape[0] // sizes["dp"]
    widths = [whole.shape[1] // (sizes["seq"] if whole_seq else 1) for whole in wholes]
    half = 1 << (len(path) - 1)
    shape = jax.ShapeDtypeStruct((half, rows, sum(widths)), wholes[0].dtype)
    size = 2 * half * rows * sum(widths)
    return pl.pallas_call(
        functools.partial(
            split_kernel, path, rows, widths, widths if whole_seq else [0] * len(widths)
        ),
        out_shape=[shape, shape],
        in_specs=[pl.BlockSpec(memory_space=pltpu.SMEM)]
        + [pl.BlockSpec(memory_space=pltpu.VMEM)] * len(wholes),
        out_specs=[pl.BlockSpec(memory_space=pl.ANY)] * 2,
        scratch_shapes=[pltpu.SemaphoreType.DMA((2 * half, len(wholes)))],
        compiler_params=pltpu.CompilerParams(vmem_limit_bytes=VMEM_LIMIT),
        cost_estimate=pl.CostEstimate(flops=0, bytes_accessed=4 * size, transcendentals=0),
    )(pair, *wholes)


def reduce_slots(keep, send, path, sizes):
    for hop in reversed(path):
        other = exchange(send, hop, sizes)
        half = keep.shape[0] // 2
        if half == 0:
            return keep[0].astype(jnp.float32) + other[0].astype(jnp.float32)
        send = (keep[half:].astype(jnp.float32) + other[half:].astype(jnp.float32)).astype(
            jnp.bfloat16
        )
        keep = (keep[:half].astype(jnp.float32) + other[:half].astype(jnp.float32)).astype(
            jnp.bfloat16
        )


def head_lanes(values, head, width):
    lane = lax.broadcasted_iota(jnp.int32, values.shape, 1)
    return jnp.where(lane // width == head, values, jnp.zeros_like(values))


def later_keys(block):
    key_at = lax.broadcasted_iota(jnp.int32, (block, block), 0)
    query_at = lax.broadcasted_iota(jnp.int32, (block, block), 1)
    return key_at > query_at


def scores_of(keys, query, hidden_keys, block):
    scores = contract_last(keys, query)
    last = jnp.where(hidden_keys, MASKED, scores[-block:])
    if scores.shape[0] == block:
        return last
    return jnp.concatenate([scores[:-block], last], axis=0)


def attend_kernel(block, width, q_ref, k_ref, v_ref, out_ref, lse_ref):
    length, lanes = q_ref.shape
    scale = jnp.bfloat16(width ** (-0.5))
    hidden_keys = later_keys(block)
    values_t = v_ref[...].T
    for first in range(0, length, block):
        last = first + block
        queries = q_ref[first:last, :] * scale
        outs = []
        for head in range(lanes // width):
            scores = scores_of(k_ref[:last, :], head_lanes(queries, head, width), hidden_keys, block)
            top = jnp.max(scores, axis=0, keepdims=True)
            probs = jnp.exp(scores - top)
            total = jnp.sum(probs, axis=0, keepdims=True)
            mixed = jnp.dot(
                values_t[head * width : (head + 1) * width, :last],
                probs.astype(jnp.bfloat16),
                preferred_element_type=jnp.float32,
            )
            outs.append(mixed / total)
            lse_ref[head : head + 1, first:last] = top + jnp.log(total)
        out_ref[first:last, :] = jnp.concatenate(outs, axis=0).T.astype(jnp.bfloat16)


def attend_back_kernel(
    block, width, q_ref, k_ref, v_ref, g_ref, o_ref, lse_ref, dq_ref, dk_ref, dv_ref, dk_acc, dv_acc
):
    length, lanes = q_ref.shape
    heads = lanes // width
    scale = jnp.bfloat16(width ** (-0.5))
    hidden_keys = later_keys(block)
    keys_t = k_ref[...].T
    for first in reversed(range(0, length, block)):
        last = first + block
        queries = q_ref[first:last, :] * scale
        grads = g_ref[first:last, :]
        products = (grads.astype(jnp.float32) * o_ref[first:last, :].astype(jnp.float32)).T
        key_part = value_part = None
        query_parts = []
        for head in range(heads):
            query = head_lanes(queries, head, width)
            grad = head_lanes(grads, head, width)
            scores = scores_of(k_ref[:last, :], query, hidden_keys, block)
            probs = jnp.exp(scores - lse_ref[head : head + 1, first:last])
            delta = jnp.sum(products[head * width : (head + 1) * width], axis=0, keepdims=True)
            prob_grad = contract_last(v_ref[:last, :], grad)
            score_grad = (probs * (prob_grad - delta)).astype(jnp.bfloat16)
            key_term = jnp.dot(score_grad, query, preferred_element_type=jnp.float32)
            value_term = jnp.dot(
                probs.astype(jnp.bfloat16), grad, preferred_element_type=jnp.float32
            )
            key_part = key_term if key_part is None else key_part + key_term
            value_part = value_term if value_part is None else value_part + value_term
            query_parts.append(
                jnp.dot(
                    keys_t[head * width : (head + 1) * width, :last],
                    score_grad,
                    preferred_element_type=jnp.float32,
                )
            )
        query_grad = jnp.concatenate(query_parts, axis=0).T * width ** (-0.5)
        dq_ref[first:last, :] = query_grad.astype(jnp.bfloat16)
        if last == length:
            dk_acc[...] = key_part
            dv_acc[...] = value_part
        else:
            dk_acc[:last, :] += key_part
            dv_acc[:last, :] += value_part
    dk_ref[...] = dk_acc[...].astype(jnp.bfloat16)
    dv_ref[...] = dv_acc[...].astype(jnp.bfloat16)


def pair_spec(length, first):
    return pl.BlockSpec((length, 128), lambda pair: (0, first + pair))


def attend(qkv):
    length, cols = qkv.shape
    pairs = cols // 3 // 128
    return pl.pallas_call(
        functools.partial(attend_kernel, 256, HEAD_DIM),
        grid=(pairs,),
        out_shape=[
            jax.ShapeDtypeStruct((length, cols // 3), jnp.bfloat16),
            jax.ShapeDtypeStruct((8 * pairs, length), jnp.float32),
        ],
        in_specs=[pair_spec(length, k * pairs) for k in range(3)],
        out_specs=[pair_spec(length, 0), pl.BlockSpec((8, length), lambda pair: (pair, 0))],
        compiler_params=pltpu.CompilerParams(vmem_limit_bytes=VMEM_LIMIT),
        cost_estimate=pl.CostEstimate(
            flops=2 * length * length * cols // 3,
            bytes_accessed=8 * length * cols // 3,
            transcendentals=length * length * pairs,
        ),
    )(qkv, qkv, qkv)


def attend_back(qkv, grads, attended, lse):
    length, cols = qkv.shape
    pairs = cols // 3 // 128
    shape = jax.ShapeDtypeStruct((length, cols // 3), jnp.bfloat16)
    return pl.pallas_call(
        functools.partial(attend_back_kernel, 256, HEAD_DIM),
        grid=(pairs,),
        out_shape=[shape] * 3,
        in_specs=[pair_spec(length, k * pairs) for k in range(3)]
        + [pair_spec(length, 0)] * 2
        + [pl.BlockSpec((8, length), lambda pair: (pair, 0))],
        out_specs=[pair_spec(length, 0)] * 3,
        scratch_shapes=[pltpu.VMEM((length, 128), jnp.float32)] * 2,
        compiler_params=pltpu.CompilerParams(vmem_limit_bytes=VMEM_LIMIT),
        cost_estimate=pl.CostEstimate(
            flops=5 * length * length * cols // 3,
            bytes_accessed=16 * length * cols // 3,
            transcendentals=length * length * pairs,
        ),
    )(qkv, qkv, qkv, grads, attended, lse)


def in_order(seq_index, mine, other, axis):
    return jnp.where(
        seq_index == 0,
        jnp.concatenate([mine, other], axis=axis),
        jnp.concatenate([other, mine], axis=axis),
    )


def on_device(inputs, vectors, w_qkv, w_out, w_up, w_down, up_bias, cotangent):
    _, piece_len, model_width = inputs.shape
    sizes = {"dp": lax.axis_size("dp"), "seq": lax.axis_size("seq")}
    seq_index = lax.axis_index("seq")
    pair = jnp.stack([lax.axis_index("dp"), seq_index])
    swap = ("seq", 1)
    half_width = model_width // 2
    path_dp = [hop for hop in hops(sizes["dp"], sizes["seq"], True) if hop[0] == "dp"]
    path_a = hops(sizes["dp"], sizes["seq"], True)
    path_b = hops(sizes["dp"], sizes["seq"], False)
    rows = w_qkv.shape[0]
    per_row = up_bias.shape[0] // rows

    bias_cols = up_bias.reshape(per_row, rows).T
    small_own = jnp.concatenate(
        [vectors, bias_cols, jnp.zeros((rows, 128 - 8 - per_row), vectors.dtype)], axis=1
    )
    blocks = [w_qkv[:, k * half_width : (k + 1) * half_width] for k in range(3)]
    arrived = exchange(jnp.concatenate([blocks[1], small_own], axis=1), swap, sizes)
    head_cols = jnp.where(
        seq_index == 0,
        jnp.concatenate([blocks[0], blocks[2], arrived[:, :half_width]], axis=1),
        jnp.concatenate([arrived[:, :half_width], blocks[0], blocks[2]], axis=1),
    )
    bias_other = arrived[:, half_width + 8 : half_width + 8 + per_row]
    small_cols = jnp.concatenate(
        [
            vectors,
            in_order(seq_index, bias_cols, bias_other, 1),
            jnp.zeros((rows, 128 - 8 - 2 * per_row), vectors.dtype),
        ],
        axis=1,
    )
    first_held, first_other = gather_slots(
        jnp.concatenate([head_cols, small_cols], axis=1), path_dp, sizes
    )
    x_own = inputs.reshape(piece_len, model_width)
    x_all = in_order(seq_index, x_own, exchange(x_own, swap, sizes), 0).astype(jnp.float32)
    a_held, a_other = gather_slots(jnp.concatenate([w_out, w_up], axis=1), path_a, sizes)
    b_held, b_other = gather_slots(w_down, path_b, sizes)

    first_whole = place(first_held, first_other, path_dp, sizes, pair, 0, 3 * half_width + 128)
    qkv_full = first_whole[:, : 3 * half_width]
    small = first_whole[:, 3 * half_width :].astype(jnp.float32)
    vec_values = small[:, :8]
    upb_full = jnp.transpose(
        small[:, 8 : 8 + 2 * per_row].reshape(sizes["dp"], rows, 2 * per_row), (0, 2, 1)
    ).reshape(-1)

    def own_heads(vector):
        return lax.dynamic_slice_in_dim(vector, seq_index * half_width, half_width, 0)

    qkv_bias = jnp.concatenate(
        [
            own_heads(vec_values[:, 2]),
            jnp.zeros((half_width,), jnp.float32),
            own_heads(vec_values[:, 3]),
        ]
    )
    normed_one = norm_rows(x_all, vec_values[:, 0], vec_values[:, 1]).astype(jnp.bfloat16)
    qkv_rows = (
        jnp.dot(normed_one, qkv_full, preferred_element_type=jnp.float32) + qkv_bias
    ).astype(jnp.bfloat16)
    attended, lse = attend(qkv_rows)

    def tokens_of(values, index):
        return lax.dynamic_slice_in_dim(values, index * piece_len, piece_len, 0)

    attended_lo = in_order(
        seq_index,
        tokens_of(attended, seq_index),
        exchange(tokens_of(attended, 1 - seq_index), swap, sizes),
        1,
    )
    resid_in = x_own.astype(jnp.float32)
    out_full = place(a_held, a_other, path_a, sizes, pair, 0, w_out.shape[1])
    up_full = place(a_held, a_other, path_a, sizes, pair, w_out.shape[1], w_up.shape[1])
    down_full = place(b_held, b_other, path_b, sizes, pair, 0, w_down.shape[1])
    branch_attn = (
        jnp.dot(attended_lo, out_full, preferred_element_type=jnp.float32) + vec_values[:, 4]
    )
    middle = resid_in + branch_attn
    normed_two = norm_rows(middle, vec_values[:, 5], vec_values[:, 6]).astype(jnp.bfloat16)
    up_act = jnp.dot(normed_two, up_full, preferred_element_type=jnp.float32) + upb_full
    hidden = gelu_tanh(up_act).astype(jnp.bfloat16)
    mlp_grad = cotangent.reshape(piece_len, model_width)
    out_grad = mlp_grad.astype(jnp.float32)

    def reduce(wholes, path):
        keep, send = split([whole.astype(jnp.bfloat16) for whole in wholes], path, sizes, pair)
        return reduce_slots(keep, send, path, sizes)

    grad_down = reduce([contract_first(mlp_grad, hidden)], path_a)
    branch_mlp = contract_last(hidden, down_full) + vec_values[:, 7]
    result = middle + branch_mlp
    hidden_grad = jnp.dot(mlp_grad, down_full, preferred_element_type=jnp.float32)
    gelu_pull = jax.vjp(gelu_tanh, up_act)[1]
    up_grad = gelu_pull(hidden_grad)[0].astype(jnp.bfloat16)
    whole_up = contract_first(normed_two, up_grad)
    norm_two_grad = contract_last(up_grad, up_full)
    ln_two_pull = jax.vjp(norm_rows, middle, vec_values[:, 5], vec_values[:, 6])[1]
    middle_part, scale_two, shift_two = ln_two_pull(norm_two_grad)
    middle_grad = out_grad + middle_part
    attn_out_grad = middle_grad.astype(jnp.bfloat16)
    attended_grad = contract_last(attn_out_grad, out_full).astype(jnp.bfloat16)

    def heads_of(values, index):
        return lax.dynamic_slice_in_dim(values, index * half_width, half_width, 1)

    grad_heads = in_order(
        seq_index,
        heads_of(attended_grad, seq_index),
        exchange(heads_of(attended_grad, 1 - seq_index), swap, sizes),
        0,
    )
    grad_up_out = reduce([whole_up, contract_first(attended_lo, attn_out_grad)], path_b)
    grad_up, grad_out = (
        grad_up_out[:, : w_up.shape[1]],
        grad_up_out[:, w_up.shape[1] :],
    )
    query_grad, key_grad, value_grad = attend_back(qkv_rows, grad_heads, attended, lse)
    qkv_grad = jnp.concatenate([query_grad, key_grad, value_grad], axis=1)
    norm_one_grad = contract_last(qkv_grad, qkv_full)
    norm_one_own = tokens_of(norm_one_grad, seq_index) + exchange(
        tokens_of(norm_one_grad, 1 - seq_index).astype(jnp.bfloat16), swap, sizes
    ).astype(jnp.float32)
    ln_one_pull = jax.vjp(norm_rows, resid_in, vec_values[:, 0], vec_values[:, 1])[1]
    input_part, _, _ = ln_one_pull(norm_one_own)
    input_grad = middle_grad + input_part

    centered = x_all - jnp.mean(x_all, axis=-1, keepdims=True)
    variance = jnp.mean(centered * centered, axis=-1, keepdims=True)
    scale_one = jnp.sum(norm_one_grad * (centered * lax.rsqrt(variance + EPSILON)), axis=0)
    shift_one = jnp.sum(norm_one_grad, axis=0)

    def of_own_heads(sums):
        none = jnp.zeros_like(sums)
        return jnp.where(
            seq_index == 0, jnp.concatenate([sums, none]), jnp.concatenate([none, sums])
        )

    vec_term = jnp.stack(
        [
            scale_one,
            shift_one,
            of_own_heads(jnp.sum(query_grad.astype(jnp.float32), axis=0)),
            of_own_heads(jnp.sum(value_grad.astype(jnp.float32), axis=0)),
            jnp.sum(attn_out_grad.astype(jnp.float32), axis=0),
            scale_two,
            shift_two,
            jnp.sum(mlp_grad.astype(jnp.float32), axis=0),
        ],
        axis=1,
    )
    upb_term = jnp.sum(up_grad.astype(jnp.float32), axis=0)
    upb_cols = jnp.transpose(
        upb_term.reshape(sizes["dp"], 2 * per_row, rows), (0, 2, 1)
    ).reshape(model_width, 2 * per_row)
    small_grads = jnp.concatenate(
        [vec_term, upb_cols, jnp.zeros((model_width, 128 - 8 - 2 * per_row), jnp.float32)], axis=1
    )
    last = reduce([contract_first(normed_one, qkv_grad), small_grads], path_dp)
    small_last = last[:, 3 * half_width :]
    sent = jnp.where(
        seq_index == 0, last[:, 2 * half_width :],
        jnp.concatenate([last[:, :half_width], small_last], axis=1)
    )
    arrived_last = exchange(sent.astype(jnp.bfloat16), swap, sizes).astype(jnp.float32)
    middle_block = arrived_last[:, :half_width]
    kept = jnp.where(seq_index == 0, last[:, : 2 * half_width], last[:, half_width : 3 * half_width])
    grad_qkv = jnp.concatenate([kept[:, :half_width], middle_block, kept[:, half_width:]], axis=1)
    small_sum = small_last + arrived_last[:, half_width:]
    grad_vectors = small_sum[:, :8]
    bias_own = lax.dynamic_slice_in_dim(small_sum, 8 + seq_index * per_row, per_row, 1)
    grad_up_bias = bias_own.T.reshape(-1)
    return (
        result.reshape(1, piece_len, model_width).astype(jnp.bfloat16),
        input_grad.reshape(1, piece_len, model_width),
        grad_qkv,
        grad_out,
        grad_up,
        grad_down,
        grad_up_bias,
        grad_vectors,
    )


def block(*arrays):
    n_dp, n_seq = lax.axis_size("dp"), lax.axis_size("seq")
    rows = arrays[2].shape[0]
    whole_tiles = rows % 16 == 0 and all(weight.shape[1] % 384 == 0 for weight in arrays[2:6])
    powers = n_dp >= 4 and n_dp & (n_dp - 1) == 0
    if n_seq == 2 and powers and whole_tiles and arrays[0].shape[0] == 1:
        return on_device(*arrays)
    return on_device_general(*arrays)


def solution(mesh):
    placed = (
        P("dp", "seq", None),
        P("dp", None),
        P("dp", "seq"),
        P("dp", "seq"),
        P("dp", "seq"),
        P("dp", "seq"),
        P(("dp", "seq")),
        P("dp", "seq", None),
    )
    return jax.shard_map(
        block,
        mesh=mesh,
        in_specs=placed,
        out_specs=(
            P("dp", "seq", None),
            P("dp", "seq", None),
            P("dp", "seq"),
            P("dp", "seq"),
            P("dp", "seq"),
            P("dp", "seq"),
            P(("dp", "seq")),
            P("dp", None),
        ),
        check_vma=False,
    )
```

```python
import functools
import math

import jax
import jax.numpy as jnp
from jax import lax
from jax.experimental import pallas as pl
from jax.experimental.pallas import tpu as pltpu
from jax.sharding import PartitionSpec as P

HEADS = 12
HEAD_DIM = 64
VMEM_LIMIT = 48 * 1024 * 1024


EPSILON = 1e-05
MASKED = -1e30


def norm_rows(values, scale_row, shift_row):
    row_mean = jnp.mean(values, axis=-1, keepdims=True)
    centered = values - row_mean
    variance = jnp.mean(centered * centered, axis=-1, keepdims=True)
    return centered * lax.rsqrt(variance + EPSILON) * scale_row + shift_row


def gelu_tanh(values):
    return (
        0.5
        * values
        * (1.0 + jnp.tanh(0.7978845608028654 * (values + 0.044715 * values * values * values)))
    )


def contract_last(left_side, right_side):
    return lax.dot_general(
        left_side, right_side, (((1,), (1,)), ((), ())), preferred_element_type=jnp.float32
    )


def contract_first(left_side, right_side):
    return lax.dot_general(
        left_side, right_side, (((0,), (0,)), ((), ())), preferred_element_type=jnp.float32
    )


def on_device_general(inputs, vectors, w_qkv, w_out, w_up, w_down, up_bias, cotangent):
    seq_count, piece_len, model_width = inputs.shape
    row_count = seq_count * piece_len
    score_scale = HEAD_DIM ** (-0.5)
    seq_index = lax.axis_index("seq")
    query_pos = seq_index * piece_len + jnp.arange(piece_len)
    qkv_cols, out_cols, up_cols, down_cols, upb_cols = (
        lax.all_gather(w_qkv, "seq", axis=1, tiled=True),
        lax.all_gather(w_out, "seq", axis=1, tiled=True),
        lax.all_gather(w_up, "seq", axis=1, tiled=True),
        lax.all_gather(w_down, "seq", axis=1, tiled=True),
        lax.all_gather(up_bias, "seq", axis=0, tiled=True),
    )
    full_fwd = (
        lax.all_gather(qkv_cols, "dp", axis=0, tiled=True),
        lax.all_gather(out_cols, "dp", axis=0, tiled=True),
        lax.all_gather(up_cols, "dp", axis=0, tiled=True),
        lax.all_gather(down_cols, "dp", axis=0, tiled=True),
        lax.all_gather(upb_cols, "dp", axis=0, tiled=True),
        lax.all_gather(vectors, "dp", axis=0, tiled=True),
    )
    qkv_full, out_full, up_full, down_full, upb_full, vec_full = full_fwd
    vec_values = vec_full.astype(jnp.float32)
    resid_in = inputs.reshape(row_count, model_width).astype(jnp.float32)
    normed_one = norm_rows(resid_in, vec_values[:, 0], vec_values[:, 1]).astype(jnp.bfloat16)
    qkv_bias = jnp.concatenate(
        [vec_values[:, 2], jnp.zeros_like(vec_values[:, 2]), vec_values[:, 3]]
    )
    qkv_rows = (
        jnp.dot(normed_one, qkv_full, preferred_element_type=jnp.float32) + qkv_bias
    ).astype(jnp.bfloat16)
    queries = qkv_rows[:, :model_width].reshape(seq_count, piece_len, HEADS, HEAD_DIM)
    key_vals = qkv_rows[:, model_width:].reshape(seq_count, piece_len, 2 * model_width)

    def block_scores(key_block, first_row):
        key_rows = key_block.shape[1]
        keys_part = key_block[..., :model_width].reshape(seq_count, key_rows, HEADS, HEAD_DIM)
        scores = (
            jnp.einsum("bqhd,bkhd->bhqk", queries, keys_part, preferred_element_type=jnp.float32)
            * score_scale
        )
        causal = (first_row + jnp.arange(key_rows))[None, :] <= query_pos[:, None]
        return jnp.where(causal, scores, MASKED)

    key_block = lax.all_gather(key_vals, "seq", axis=1, tiled=True)
    run_max = jnp.full((seq_count, HEADS, piece_len), MASKED, jnp.float32)
    key_rows = key_block.shape[1]
    values_part = key_block[..., model_width:].reshape(seq_count, key_rows, HEADS, HEAD_DIM)
    scores = block_scores(key_block, jnp.int32(0))
    new_max = jnp.maximum(run_max, jnp.max(scores, axis=-1))
    exp_scores = jnp.exp(scores - new_max[..., None])
    run_total = jnp.sum(exp_scores, axis=-1)
    added_part = jnp.einsum(
        "bhqk,bkhd->bqhd",
        exp_scores.astype(jnp.bfloat16),
        values_part,
        preferred_element_type=jnp.float32,
    )
    run_acc = added_part
    run_max, run_total, run_acc = (new_max, run_total, run_acc)
    attended = run_acc / jnp.transpose(run_total, (0, 2, 1))[..., None]
    log_total = run_max + jnp.log(run_total)
    attended_lo = attended.reshape(row_count, model_width).astype(jnp.bfloat16)
    branch_attn = (
        jnp.dot(attended_lo, out_full, preferred_element_type=jnp.float32) + vec_values[:, 4]
    )
    middle = resid_in + branch_attn
    normed_two = norm_rows(middle, vec_values[:, 5], vec_values[:, 6]).astype(jnp.bfloat16)
    up_act = jnp.dot(normed_two, up_full, preferred_element_type=jnp.float32) + upb_full.astype(
        jnp.float32
    )
    hidden = gelu_tanh(up_act).astype(jnp.bfloat16)
    branch_mlp = contract_last(hidden, down_full) + vec_values[:, 7]
    result = middle + branch_mlp
    qkv_back, out_back, up_back, down_back = (qkv_full, out_full, up_full, down_full)
    out_grad = cotangent.reshape(row_count, model_width).astype(jnp.float32)
    mlp_grad = out_grad.astype(jnp.bfloat16)
    hidden_grad = jnp.dot(mlp_grad, down_back, preferred_element_type=jnp.float32)
    gelu_pull = jax.vjp(gelu_tanh, up_act)[1]
    up_grad = gelu_pull(hidden_grad)[0].astype(jnp.bfloat16)
    norm_two_grad = contract_last(up_grad, up_back)
    ln_two_pull = jax.vjp(norm_rows, middle, vec_values[:, 5], vec_values[:, 6])[1]
    middle_part, scale_two, shift_two = ln_two_pull(norm_two_grad)
    middle_grad = out_grad + middle_part
    attn_out_grad = middle_grad.astype(jnp.bfloat16)
    attended_grad = contract_last(attn_out_grad, out_back).astype(jnp.bfloat16)
    grad_heads = attended_grad.reshape(seq_count, piece_len, HEADS, HEAD_DIM)
    row_delta = jnp.transpose(
        jnp.sum(grad_heads.astype(jnp.float32) * attended, axis=-1), (0, 2, 1)
    )
    key_vals_all = lax.all_gather(key_vals, "seq", axis=1, tiled=True)
    total_len = key_vals_all.shape[1]
    key_block_len = math.gcd(total_len, 512)

    def back_step(query_acc, block_index):
        first_row = block_index * key_block_len
        key_block = lax.dynamic_slice_in_dim(key_vals_all, first_row, key_block_len, 1)
        keys_part = key_block[..., :model_width].reshape(seq_count, key_block_len, HEADS, HEAD_DIM)
        values_part = key_block[..., model_width:].reshape(
            seq_count, key_block_len, HEADS, HEAD_DIM
        )
        scores = block_scores(key_block, first_row)
        attn_probs = jnp.exp(scores - log_total[..., None])
        prob_grad = jnp.einsum(
            "bqhd,bkhd->bhqk", grad_heads, values_part, preferred_element_type=jnp.float32
        )
        score_grad = (attn_probs * (prob_grad - row_delta[..., None])).astype(jnp.bfloat16)
        step_part = jnp.einsum(
            "bhqk,bkhd->bqhd", score_grad, keys_part, preferred_element_type=jnp.float32
        )
        key_grad = (
            jnp.einsum("bhqk,bqhd->bkhd", score_grad, queries, preferred_element_type=jnp.float32)
            * score_scale
        )
        value_grad = jnp.einsum(
            "bhqk,bqhd->bkhd",
            attn_probs.astype(jnp.bfloat16),
            grad_heads,
            preferred_element_type=jnp.float32,
        )
        key_value = jnp.concatenate(
            [
                key_grad.reshape(seq_count, key_block_len, model_width),
                value_grad.reshape(seq_count, key_block_len, model_width),
            ],
            axis=-1,
        )
        return (query_acc + step_part * score_scale, key_value)

    query_grad, kv_blocks = lax.scan(
        back_step,
        jnp.zeros((seq_count, piece_len, HEADS, HEAD_DIM), jnp.float32),
        jnp.arange(total_len // key_block_len),
    )
    kv_terms = jnp.moveaxis(kv_blocks, 0, 1).reshape(seq_count, total_len, 2 * model_width)
    key_val_grad = lax.psum_scatter(
        kv_terms.astype(jnp.bfloat16), "seq", scatter_dimension=1, tiled=True
    ).astype(jnp.float32)
    key_val_grad = key_val_grad.reshape(row_count, 2 * model_width)
    qkv_grad = jnp.concatenate(
        [query_grad.reshape(row_count, model_width), key_val_grad], axis=1
    ).astype(jnp.bfloat16)
    norm_one_grad = contract_last(qkv_grad, qkv_back)
    ln_one_pull = jax.vjp(norm_rows, resid_in, vec_values[:, 0], vec_values[:, 1])[1]
    input_part, scale_one, shift_one = ln_one_pull(norm_one_grad)
    input_grad = middle_grad + input_part
    whole_qkv = contract_first(normed_one, qkv_grad)
    whole_out = contract_first(attended_lo, attn_out_grad)
    whole_up = contract_first(normed_two, up_grad)
    whole_down = contract_first(mlp_grad, hidden)
    row_qkv, row_out, row_up, row_down = (
        lax.psum_scatter(
            whole_qkv.astype(jnp.bfloat16), "dp", scatter_dimension=0, tiled=True
        ).astype(jnp.float32),
        lax.psum_scatter(
            whole_out.astype(jnp.bfloat16), "dp", scatter_dimension=0, tiled=True
        ).astype(jnp.float32),
        lax.psum_scatter(
            whole_up.astype(jnp.bfloat16), "dp", scatter_dimension=0, tiled=True
        ).astype(jnp.float32),
        lax.psum_scatter(
            whole_down.astype(jnp.bfloat16), "dp", scatter_dimension=0, tiled=True
        ).astype(jnp.float32),
    )
    grad_qkv, grad_out, grad_up, grad_down = (
        lax.psum_scatter(
            row_qkv.astype(jnp.bfloat16), "seq", scatter_dimension=1, tiled=True
        ).astype(jnp.float32),
        lax.psum_scatter(
            row_out.astype(jnp.bfloat16), "seq", scatter_dimension=1, tiled=True
        ).astype(jnp.float32),
        lax.psum_scatter(
            row_up.astype(jnp.bfloat16), "seq", scatter_dimension=1, tiled=True
        ).astype(jnp.float32),
        lax.psum_scatter(
            row_down.astype(jnp.bfloat16), "seq", scatter_dimension=1, tiled=True
        ).astype(jnp.float32),
    )
    vec_term = jnp.stack(
        [
            scale_one,
            shift_one,
            jnp.sum(qkv_grad[:, :model_width].astype(jnp.float32), axis=0),
            jnp.sum(qkv_grad[:, 2 * model_width :].astype(jnp.float32), axis=0),
            jnp.sum(attn_out_grad.astype(jnp.float32), axis=0),
            scale_two,
            shift_two,
            jnp.sum(mlp_grad.astype(jnp.float32), axis=0),
        ],
        axis=1,
    )
    upb_term = jnp.sum(up_grad.astype(jnp.float32), axis=0)
    vec_sum, upb_sum = lax.psum((vec_term, upb_term), ("dp", "seq"))
    vec_rows = vectors.shape[0]
    grad_vectors = lax.dynamic_slice_in_dim(vec_sum, lax.axis_index("dp") * vec_rows, vec_rows, 0)
    upb_rows = up_bias.shape[0]
    upb_start = (lax.axis_index("dp") * lax.axis_size("seq") + seq_index) * upb_rows
    grad_up_bias = lax.dynamic_slice_in_dim(upb_sum, upb_start, upb_rows, 0)
    return (
        result.reshape(seq_count, piece_len, model_width).astype(jnp.bfloat16),
        input_grad.reshape(seq_count, piece_len, model_width),
        grad_qkv,
        grad_out,
        grad_up,
        grad_down,
        grad_up_bias,
        grad_vectors,
    )


def bit_masks(count):
    return [1 << k for k in range(count.bit_length() - 1)]


def exchange(values, hop, sizes):
    axis, mask = hop
    return lax.ppermute(values, axis, [(i, i ^ mask) for i in range(sizes[axis])])


def slot_owner(slot, path):
    offset = {"dp": 0, "seq": 0}
    for k, (axis, mask) in enumerate(path):
        if slot >> k & 1:
            offset[axis] ^= mask
    return offset["dp"], offset["seq"]


def after(values, *earlier):
    return lax.optimization_barrier((values, *earlier))[0]


def grow(held, hop, sizes):
    return jnp.concatenate([held, exchange(held, hop, sizes)], axis=0)


def start_place(path, rows, parts, me_ref, targets, sems):
    total = 1 << len(path)
    each = total // len(parts)
    copies = []
    for k, (target, first, cols, stride, at) in enumerate(targets):
        for slot in range(total):
            off_dp, off_seq = slot_owner(slot, path)
            row = pl.multiple_of((me_ref[0] ^ off_dp) * rows, 16)
            col = pl.multiple_of((me_ref[1] ^ off_seq) * stride + at, 128)
            src = parts[slot // each].at[slot % each, :, pl.ds(first, cols)]
            dst = target.at[pl.ds(row, rows), pl.ds(col, cols)]
            copy = pltpu.make_async_copy(src, dst, sems.at[k, slot])
            copy.start()
            copies.append(copy)
    return copies


def start_split(rows, me_ref, pieces, keep_ref, send_ref, sems):
    copies = []
    for k, (path, whole, stride, first, cols, at) in enumerate(pieces):
        half = 1 << (len(path) - 1)
        for slot in range(2 * half):
            off_dp, off_seq = slot_owner(slot, path)
            row = pl.multiple_of((me_ref[0] ^ off_dp) * rows, 16)
            col = pl.multiple_of((me_ref[1] ^ off_seq) * stride + first, 128)
            target = keep_ref if slot < half else send_ref
            copy = pltpu.make_async_copy(
                whole.at[pl.ds(row, rows), pl.ds(col, cols)],
                target.at[slot % half, :, pl.ds(at, cols)],
                sems.at[k, slot],
            )
            copy.start()
            copies.append(copy)
    return copies


def wait_all(copies):
    for copy in copies:
        copy.wait()


def normed(values):
    centered = values - jnp.mean(values, axis=-1, keepdims=True)
    inverse = lax.rsqrt(jnp.mean(centered * centered, axis=-1, keepdims=True) + EPSILON)
    return centered * inverse, inverse


def normed_back(grads, unit, inverse, scale_row):
    scaled = grads * scale_row
    mean_one = jnp.mean(scaled, axis=-1, keepdims=True)
    mean_two = jnp.mean(scaled * unit, axis=-1, keepdims=True)
    return inverse * (scaled - mean_one - unit * mean_two)


def dot(left_side, right_side):
    return jnp.dot(left_side, right_side, preferred_element_type=jnp.float32)


def column_sum(values):
    return jnp.sum(values.astype(jnp.float32), axis=0, keepdims=True)


def project_kernel(path, rows, me_ref, own_ref, other_ref, *refs):
    parts = refs[:2]
    qkv_ref, a_ref, w_ref, vec_ref, small, sems = refs[2:]
    seq = me_ref[1]
    piece, width = own_ref.shape
    third = w_ref.shape[1] // 3
    copies = start_place(
        path,
        rows,
        parts,
        me_ref,
        [(small, 3 * third, 128, 0, 0), (w_ref, 0, 3 * third, 0, 0)],
        sems,
    )
    units = []
    for part in range(2):
        values = jnp.where(seq == part, own_ref[...], other_ref[...]).astype(jnp.float32)
        units.append(normed(values)[0])
    wait_all(copies[: len(copies) // 2])
    vec_ref[...] = small[...].astype(jnp.float32).T[: vec_ref.shape[0]]
    for part in range(2):
        a_ref[part * piece : (part + 1) * piece, :] = (
            units[part] * vec_ref[0:1, :] + vec_ref[1:2, :]
        ).astype(jnp.bfloat16)
    wait_all(copies[len(copies) // 2 :])
    own_cols = pl.ds(pl.multiple_of(seq * third, 128), third)
    for k in range(3):
        cols = slice(k * third, (k + 1) * third)
        for part in range(2):
            at = slice(part * piece, (part + 1) * piece)
            product = dot(a_ref[at, :], w_ref[:, cols])
            if k != 1:
                product = product + vec_ref[2 + k // 2 : 3 + k // 2, own_cols]
            qkv_ref[at, cols] = product.astype(jnp.bfloat16)


def in_vmem(count):
    return [pl.BlockSpec(memory_space=pltpu.VMEM)] * count


def in_any(count):
    return [pl.BlockSpec(memory_space=pl.ANY)] * count


def shaped(dtype, *shape):
    return jax.ShapeDtypeStruct(shape, dtype)


def local_call(kernel, pair, vmem_args, any_args, vmem_outs, any_outs, scratch, flops):
    outs = list(vmem_outs) + list(any_outs)
    moved = sum(a.size * a.dtype.itemsize for a in [*vmem_args, *any_args, *outs])
    return pl.pallas_call(
        kernel,
        out_shape=outs,
        in_specs=[pl.BlockSpec(memory_space=pltpu.SMEM)]
        + in_vmem(len(vmem_args))
        + in_any(len(any_args)),
        out_specs=in_vmem(len(vmem_outs)) + in_any(len(any_outs)),
        scratch_shapes=scratch,
        compiler_params=pltpu.CompilerParams(vmem_limit_bytes=VMEM_LIMIT),
        cost_estimate=pl.CostEstimate(flops=100000000000, bytes_accessed=10**7, transcendentals=0),
    )(pair, *vmem_args, *any_args)


def gelu_both(values):
    square = values * values
    angle = jnp.tanh(0.7978845608028654 * values * (1.0 + 0.044715 * square))
    half = 0.5 * (1.0 + angle)
    slope = half + 0.5 * values * (1.0 - angle * angle) * (
        0.7978845608028654 * (1.0 + 3.0 * 0.044715 * square)
    )
    return values * half, slope


def place_out_up(paths, rows, cut, parts, me_ref, w_out, w_up, sems):
    out_cols, up_cols = w_out.shape[1] // 2, w_up.shape[1] // 2
    left = cut - out_cols
    copies = start_place(
        paths[0],
        rows,
        parts[:4],
        me_ref,
        [(w_out, 0, out_cols, out_cols, 0), (w_up, out_cols, left, up_cols, 0)],
        sems,
    )
    slots = 1 << len(paths[0])
    more = start_place(
        paths[1], rows, parts[4:], me_ref, [(w_up, 0, up_cols - left, up_cols, left)], sems.at[2:3]
    )
    return copies[:slots], copies[slots:] + more


def place_down(paths, rows, cut, parts, me_ref, w_down, sems):
    cols = w_down.shape[1] // 2
    return start_place(
        paths[0], rows, parts[:4], me_ref, [(w_down, 0, cut, cols, 0)], sems
    ) + start_place(
        paths[1], rows, parts[4:], me_ref, [(w_down, 0, cols - cut, cols, cut)], sems.at[1:2]
    )


def hidden_kernel(paths, rows, cut, chunk, me_ref, *refs):
    mine_ref, other_ref, x_ref, vec_ref, bias_ref = refs[:5]
    parts = refs[5:13]
    h_ref, a_ref, g_ref, slope_ref = refs[13:17]
    w_out, w_up, sems = refs[17:]
    left_first = me_ref[1] == 0
    half = mine_ref.shape[1]
    out_copies, up_copies = place_out_up(paths, rows, cut, parts, me_ref, w_out, w_up, sems)
    left = jnp.where(left_first, mine_ref[...], other_ref[...])
    right = jnp.where(left_first, other_ref[...], mine_ref[...])
    wait_all(out_copies)
    branch = dot(left, w_out[:half, :]) + dot(right, w_out[half:, :]) + vec_ref[4:5, :]
    middle = x_ref[...].astype(jnp.float32) + branch
    h_ref[...] = middle
    a_ref[...] = (normed(middle)[0] * vec_ref[5:6, :] + vec_ref[6:7, :]).astype(jnp.bfloat16)
    wait_all(up_copies)

    def step(k, carry):
        cols = pl.ds(pl.multiple_of(k * chunk, chunk), chunk)
        act = dot(a_ref[...], w_up[:, cols]) + bias_ref[:, cols]
        value, slope = gelu_both(act)
        g_ref[:, cols] = value.astype(jnp.bfloat16)
        slope_ref[:, cols] = slope.astype(jnp.bfloat16)
        return carry

    lax.fori_loop(0, w_up.shape[1] // chunk, step, 0)


def down_grad_kernel(paths, rows, cut, chunk, me_ref, *refs):
    g_ref, dy_ref, keep_ref, send_ref, grad, dy_t, sems = refs
    dy_t[...] = dy_ref[...].T

    def step(k, carry):
        cols = pl.ds(pl.multiple_of(k * chunk, chunk), chunk)
        grad[:, cols] = dot(dy_t[...], g_ref[:, cols]).astype(jnp.bfloat16)
        return carry

    lax.fori_loop(0, grad.shape[1] // chunk, step, 0)
    cols = grad.shape[1] // 2
    pieces = [
        (paths[0], grad, cols, 0, cut, 0),
        (paths[1], grad, cols, cut, cols - cut, cut),
    ]
    wait_all(start_split(rows, me_ref, pieces, keep_ref, send_ref, sems))


def mlp_back_kernel(paths, rows, cut, down_cut, chunk, me_ref, *refs):
    slope_ref, dy_ref = refs[:2]
    parts, down_parts = refs[2:10], refs[10:18]
    du_ref, acc, bias_sum_ref = refs[18:21]
    w_out, w_up, w_down, sems, down_sems = refs[21:]
    down_copies = place_down(paths, rows, down_cut, down_parts, me_ref, w_down, down_sems)
    out_copies, up_copies = place_out_up(paths, rows, cut, parts, me_ref, w_out, w_up, sems)
    acc[...] = jnp.zeros_like(acc)
    wait_all(down_copies)
    wait_all(out_copies)
    wait_all(up_copies)

    def step(k, carry):
        cols = pl.ds(pl.multiple_of(k * chunk, chunk), chunk)
        up_grad = (
            dot(dy_ref[...], w_down[:, cols]) * slope_ref[:, cols].astype(jnp.float32)
        ).astype(jnp.bfloat16)
        du_ref[:, cols] = up_grad
        bias_sum_ref[0:1, cols] = column_sum(up_grad)
        acc[...] += contract_last(up_grad, w_up[:, cols])
        return carry

    lax.fori_loop(0, w_up.shape[1] // chunk, step, 0)


def middle_back_kernel(paths, rows, out_cols, me_ref, *refs):
    acc_ref, h_ref, dy_ref, vec_ref = refs[:4]
    parts = refs[4:8]
    dh_ref, dz_ref, do_keep_ref, do_send_ref, sum_ref = refs[8:13]
    w_out, sems = refs[13:]
    left_first = me_ref[1] == 0
    copies = start_place(
        paths[0], rows, parts, me_ref, [(w_out, 0, out_cols, out_cols, 0)], sems
    )
    out_grad = dy_ref[...].astype(jnp.float32)
    unit, inverse = normed(h_ref[...])
    grads = acc_ref[...]
    middle_grad = out_grad + normed_back(grads, unit, inverse, vec_ref[5:6, :])
    dh_ref[...] = middle_grad
    attn_grad = middle_grad.astype(jnp.bfloat16)
    dz_ref[...] = attn_grad
    wait_all(copies)
    half = do_keep_ref.shape[1]
    left = contract_last(attn_grad, w_out[:half, :])
    right = contract_last(attn_grad, w_out[half:, :])
    do_keep_ref[...] = jnp.where(left_first, left, right).astype(jnp.bfloat16)
    do_send_ref[...] = jnp.where(left_first, right, left).astype(jnp.bfloat16)
    sum_ref[...] = jnp.concatenate(
        [
            column_sum(attn_grad),
            column_sum(grads * unit),
            column_sum(grads),
            column_sum(out_grad),
            jnp.zeros((4, out_grad.shape[1]), jnp.float32),
        ],
        axis=0,
    )


def result_kernel(paths, rows, down_cut, me_ref, *refs):
    g_ref, h_ref, vec_ref = refs[:3]
    parts = refs[3:11]
    res_ref, w_down, sems = refs[11:]
    wait_all(place_down(paths, rows, down_cut, parts, me_ref, w_down, sems))
    for first in range(0, w_down.shape[0], 256):
        cols = slice(first, first + 256)
        res_ref[:, cols] = (
            h_ref[:, cols] + contract_last(g_ref[...], w_down[cols, :]) + vec_ref[7:8, cols]
        ).astype(jnp.bfloat16)


def up_grad_kernel(paths, rows, cut, chunk, me_ref, *refs):
    a_ref, du_ref, mine_ref, other_ref, dz_ref, keep_ref, send_ref = refs[:7]
    grad_up, grad_out, left_t, sems = refs[7:]
    left_first = me_ref[1] == 0
    half = mine_ref.shape[1]
    left_t[...] = a_ref[...].T

    def step(k, carry):
        cols = pl.ds(pl.multiple_of(k * chunk, chunk), chunk)
        grad_up[:, cols] = dot(left_t[...], du_ref[:, cols]).astype(jnp.bfloat16)
        return carry

    lax.fori_loop(0, du_ref.shape[1] // chunk, step, 0)
    left = jnp.where(left_first, mine_ref[...], other_ref[...])
    right = jnp.where(left_first, other_ref[...], mine_ref[...])
    grad_out[:half, :] = contract_first(left, dz_ref[...]).astype(jnp.bfloat16)
    grad_out[half:, :] = contract_first(right, dz_ref[...]).astype(jnp.bfloat16)
    up_cols, out_cols = grad_up.shape[1] // 2, grad_out.shape[1] // 2
    pieces = [
        (paths[0], grad_up, up_cols, 0, cut, 0),
        (paths[1], grad_up, up_cols, cut, up_cols - cut, cut),
        (paths[1], grad_out, out_cols, 0, out_cols, up_cols),
    ]
    wait_all(start_split(rows, me_ref, pieces, keep_ref, send_ref, sems))


def project_back_kernel(path, rows, pairs, me_ref, *refs):
    grad_refs = refs[: 3 * pairs]
    w_ref, a_ref, own_ref, other_ref, vec_ref, sum_ref, bias_ref = refs[3 * pairs : 3 * pairs + 7]
    da_own_ref, da_send_ref, keep_ref, send_ref = refs[3 * pairs + 7 : 3 * pairs + 11]
    grads_all, grad, parts, small, a_t, sems = refs[3 * pairs + 11 :]
    seq = me_ref[1]
    piece = own_ref.shape[0]
    third = grads_all.shape[1] // 3
    small[...] = jnp.zeros_like(small)
    a_t[...] = a_ref[...].T
    for k in range(3):
        for pair in range(pairs):
            at = k * third + pair * 128
            grads_all[:, at : at + 128] = grad_refs[3 * pair + k][...]
        cols = slice(k * third, (k + 1) * third)
        grad[:, cols] = dot(a_t[...], grads_all[:, cols]).astype(jnp.bfloat16)
    for part in range(2):
        at = slice(part * piece, (part + 1) * piece)
        grads = contract_last(grads_all[at, :], w_ref[...])
        parts[part] = grads
        values = jnp.where(seq == part, own_ref[...], other_ref[...]).astype(jnp.float32)
        small[0:1, :] += column_sum(grads * normed(values)[0])
        small[1:2, :] += column_sum(grads)
    da_own_ref[...] = parts[seq]
    da_send_ref[...] = parts[1 - seq].astype(jnp.bfloat16)
    own_cols = pl.ds(pl.multiple_of(seq * third, 128), third)
    small[2:3, own_cols] = column_sum(grads_all[:, :third])
    small[3:4, own_cols] = column_sum(grads_all[:, 2 * third :])
    small[4:8, :] = sum_ref[0:4, :]
    bias_rows = bias_ref.shape[0]
    small[8 : 8 + bias_rows, :] = bias_ref[...]
    grad[:, 3 * third :] = small[...].T.astype(jnp.bfloat16)
    pieces = [(path, grad, 0, 0, grad.shape[1], 0)]
    wait_all(start_split(rows, me_ref, pieces, keep_ref, send_ref, sems))


def add_kernel(cuts, count, *refs):
    ins, outs = refs[: 2 * count], refs[2 * count :]
    for pair, first, last, left, right, out, at in cuts:
        keep, other = ins[2 * pair], ins[2 * pair + 1]
        total = keep[first:last, :, left:right].astype(jnp.float32) + other[
            first:last, :, left:right
        ].astype(jnp.float32)
        outs[out][:, :, at : at + right - left] = total.astype(outs[out].dtype)


def add_pairs(pairs, cuts, shapes):
    ins = [array for pair in pairs for array in pair]
    return pl.pallas_call(
        functools.partial(add_kernel, cuts, len(pairs)),
        out_shape=[jax.ShapeDtypeStruct(shape, jnp.bfloat16) for shape in shapes],
        in_specs=in_vmem(len(ins)),
        out_specs=in_vmem(len(shapes)),
        compiler_params=pltpu.CompilerParams(vmem_limit_bytes=VMEM_LIMIT),
    )(*ins)


def halves(pairs):
    cuts, shapes = [], []
    for k, (keep, _) in enumerate(pairs):
        slots, rows, cols = keep.shape
        for part in range(2):
            cuts.append((k, part * slots // 2, (part + 1) * slots // 2, 0, cols, len(shapes), 0))
            shapes.append((slots // 2, rows, cols))
    return add_pairs(pairs, cuts, shapes)


def quarters(keep, other, cut):
    slots, rows, cols = keep.shape
    cuts, shapes = [], []
    for left, right in ((0, cut), (cut, cols)):
        for part in range(2):
            cuts.append(
                (0, part * slots // 2, (part + 1) * slots // 2, left, right, len(shapes), 0)
            )
            shapes.append((slots // 2, rows, right - left))
    return add_pairs([(keep, other)], cuts, shapes)


def rejoin(pairs):
    slots, rows, left_cols = pairs[0][0].shape
    right_cols = pairs[1][0].shape[2]
    cuts, shapes = [], []
    for part in range(2):
        first, last = part * slots // 2, (part + 1) * slots // 2
        cuts.append((0, first, last, 0, left_cols, part, 0))
        cuts.append((1, first, last, 0, right_cols, part, left_cols))
        shapes.append((slots // 2, rows, left_cols + right_cols))
    return add_pairs(pairs, cuts, shapes)


def head_lanes(values, head, width):
    lane = lax.broadcasted_iota(jnp.int32, values.shape, 1)
    return jnp.where(lane // width == head, values, jnp.zeros_like(values))


def later_keys(block):
    key_at = lax.broadcasted_iota(jnp.int32, (block, block), 0)
    query_at = lax.broadcasted_iota(jnp.int32, (block, block), 1)
    return key_at > query_at


def scores_of(keys, query, hidden_keys, block):
    scores = contract_last(keys, query)
    last = jnp.where(hidden_keys, MASKED, scores[-block:])
    if scores.shape[0] == block:
        return last
    return jnp.concatenate([scores[:-block], last], axis=0)


def attend_kernel(block, width, q_ref, k_ref, v_ref, out_ref, lse_ref):
    length, lanes = q_ref.shape
    scale = jnp.bfloat16(width ** (-0.5))
    hidden_keys = later_keys(block)
    values_t = v_ref[...].T
    for first in range(0, length, block):
        last = first + block
        queries = q_ref[first:last, :] * scale
        outs = []
        for head in range(lanes // width):
            scores = scores_of(k_ref[:last, :], head_lanes(queries, head, width), hidden_keys, block)
            top = jnp.max(scores, axis=0, keepdims=True)
            probs = jnp.exp(scores - top)
            total = jnp.sum(probs, axis=0, keepdims=True)
            mixed = jnp.dot(
                values_t[head * width : (head + 1) * width, :last],
                probs.astype(jnp.bfloat16),
                preferred_element_type=jnp.float32,
            )
            outs.append(mixed / total)
            lse_ref[head : head + 1, first:last] = top + jnp.log(total)
        out_ref[first:last, :] = jnp.concatenate(outs, axis=0).T.astype(jnp.bfloat16)


def attend_back_kernel(
    block, width, q_ref, k_ref, v_ref, g_ref, o_ref, lse_ref, dq_ref, dk_ref, dv_ref, dk_acc, dv_acc
):
    length, lanes = q_ref.shape
    heads = lanes // width
    scale = jnp.bfloat16(width ** (-0.5))
    hidden_keys = later_keys(block)
    keys_t = k_ref[...].T
    for first in reversed(range(0, length, block)):
        last = first + block
        queries = q_ref[first:last, :] * scale
        grads = g_ref[first:last, :]
        products = (grads.astype(jnp.float32) * o_ref[first:last, :].astype(jnp.float32)).T
        key_part = value_part = None
        query_parts = []
        for head in range(heads):
            query = head_lanes(queries, head, width)
            grad = head_lanes(grads, head, width)
            scores = scores_of(k_ref[:last, :], query, hidden_keys, block)
            probs = jnp.exp(scores - lse_ref[head : head + 1, first:last])
            delta = jnp.sum(products[head * width : (head + 1) * width], axis=0, keepdims=True)
            prob_grad = contract_last(v_ref[:last, :], grad)
            score_grad = (probs * (prob_grad - delta)).astype(jnp.bfloat16)
            key_term = jnp.dot(score_grad, query, preferred_element_type=jnp.float32)
            value_term = jnp.dot(
                probs.astype(jnp.bfloat16), grad, preferred_element_type=jnp.float32
            )
            key_part = key_term if key_part is None else key_part + key_term
            value_part = value_term if value_part is None else value_part + value_term
            query_parts.append(
                jnp.dot(
                    keys_t[head * width : (head + 1) * width, :last],
                    score_grad,
                    preferred_element_type=jnp.float32,
                )
            )
        query_grad = jnp.concatenate(query_parts, axis=0).T * width ** (-0.5)
        dq_ref[first:last, :] = query_grad.astype(jnp.bfloat16)
        if last == length:
            dk_acc[...] = key_part
            dv_acc[...] = value_part
        else:
            dk_acc[:last, :] += key_part
            dv_acc[:last, :] += value_part
    dk_ref[...] = dk_acc[...].astype(jnp.bfloat16)
    dv_ref[...] = dv_acc[...].astype(jnp.bfloat16)


def pair_spec(length, first):
    return pl.BlockSpec((length, 128), lambda pair: (0, first + pair))


def attend(qkv):
    length, cols = qkv.shape
    pairs = cols // 3 // 128
    return pl.pallas_call(
        functools.partial(attend_kernel, 256, HEAD_DIM),
        grid=(pairs,),
        out_shape=[
            jax.ShapeDtypeStruct((length, cols // 3), jnp.bfloat16),
            jax.ShapeDtypeStruct((8 * pairs, length), jnp.float32),
        ],
        in_specs=[pair_spec(length, k * pairs) for k in range(3)],
        out_specs=[pair_spec(length, 0), pl.BlockSpec((8, length), lambda pair: (pair, 0))],
        compiler_params=pltpu.CompilerParams(vmem_limit_bytes=VMEM_LIMIT),
        cost_estimate=pl.CostEstimate(flops=100000000000, bytes_accessed=10**7, transcendentals=0),
    )(qkv, qkv, qkv)


def attend_back(qkv, grads, attended, lse, pair):
    length, cols = qkv.shape
    pairs = cols // 3 // 128
    column = functools.partial(pair_spec, length)
    return pl.pallas_call(
        functools.partial(attend_back_kernel, 256, HEAD_DIM),
        grid=(1,),
        out_shape=[jax.ShapeDtypeStruct((length, 128), jnp.bfloat16)] * 3,
        in_specs=[column(k * pairs + pair) for k in range(3)]
        + [column(pair)] * 2
        + [pl.BlockSpec((8, length), lambda step: (pair, 0))],
        out_specs=[column(0)] * 3,
        scratch_shapes=[pltpu.VMEM((length, 128), jnp.float32)] * 2,
        compiler_params=pltpu.CompilerParams(vmem_limit_bytes=VMEM_LIMIT),
        cost_estimate=pl.CostEstimate(flops=100000000000, bytes_accessed=10**7, transcendentals=0),
    )(qkv, qkv, qkv, grads, attended, lse)


def in_order(seq_index, mine, other, axis):
    return jnp.where(
        seq_index == 0,
        jnp.concatenate([mine, other], axis=axis),
        jnp.concatenate([other, mine], axis=axis),
    )


def on_device(inputs, vectors, w_qkv, w_out, w_up, w_down, up_bias, cotangent):
    _, piece_len, model_width = inputs.shape
    sizes = {"dp": lax.axis_size("dp"), "seq": lax.axis_size("seq")}
    seq_index = lax.axis_index("seq")
    pair = jnp.stack([lax.axis_index("dp"), seq_index])
    swap = ("seq", 1)
    half_width = model_width // 2
    dp_masks = bit_masks(sizes["dp"])
    core, row_hop = ("dp", dp_masks[0]), ("dp", dp_masks[1])
    far = [("dp", mask) for mask in reversed(dp_masks[2:])]
    path_dp = far + [row_hop, core]
    paths = (far + [swap, row_hop, core], far + [row_hop, swap, core])
    rows = w_qkv.shape[0]
    per_row = up_bias.shape[0] // rows

    bias_cols = up_bias.reshape(per_row, rows).T
    small_own = jnp.concatenate(
        [vectors, bias_cols, jnp.zeros((rows, 128 - 8 - per_row), vectors.dtype)], axis=1
    )
    blocks = [w_qkv[:, k * half_width : (k + 1) * half_width] for k in range(3)]
    arrived = exchange(jnp.concatenate([blocks[1], small_own], axis=1), swap, sizes)
    head_cols = jnp.where(
        seq_index == 0,
        jnp.concatenate([blocks[0], blocks[2], arrived[:, :half_width]], axis=1),
        jnp.concatenate([arrived[:, :half_width], blocks[0], blocks[2]], axis=1),
    )
    bias_other = arrived[:, half_width + 8 : half_width + 8 + per_row]
    small_cols = jnp.concatenate(
        [
            vectors,
            in_order(seq_index, bias_cols, bias_other, 1),
            jnp.zeros((rows, 128 - 8 - 2 * per_row), vectors.dtype),
        ],
        axis=1,
    )
    x_own = inputs.reshape(piece_len, model_width)
    x_other = exchange(x_own, swap, sizes)
    first = jnp.concatenate([head_cols, small_cols], axis=1)[None]
    a_held = jnp.concatenate([w_out, w_up], axis=1)[None]
    b_held = w_down[None]
    up_cols = w_up.shape[1]
    cut, down_cut = 8 * a_held.shape[2] // 15 // 128 * 128, up_cols // 2
    for hop in far:
        a_held = grow(a_held, hop, sizes)
        first = grow(first, hop, sizes)
    b_held = grow(after(b_held, first), far[0], sizes)
    a_halves = [a_held[:, :, :cut], a_held[:, :, cut:]]
    a_next = [exchange(part, paths[k][len(far)], sizes) for k, part in enumerate(a_halves)]
    first = grow(first, row_hop, sizes)
    b_next = exchange(b_held, far[1], sizes)
    first_parts = [first, exchange(first, core, sizes)]

    bf16, f32 = jnp.bfloat16, jnp.float32
    seq_len, ff = 2 * piece_len, 2 * w_up.shape[1]
    head_width = 3 * half_width
    dense = 2 * piece_len * model_width
    dma = pltpu.SemaphoreType.DMA
    qkv_rows, normed_one, qkv_full, vec_rows = local_call(
        functools.partial(project_kernel, path_dp, rows),
        pair,
        [x_own, x_other],
        first_parts,
        [
            shaped(bf16, seq_len, head_width),
            shaped(bf16, seq_len, model_width),
            shaped(bf16, model_width, head_width),
            shaped(f32, 16, model_width),
        ],
        [],
        [pltpu.VMEM((model_width, 128), bf16), dma((2, sizes["dp"]))],
        2 * dense * head_width,
    )
    bias_row = jnp.transpose(
        vec_rows[8 : 8 + 2 * per_row].reshape(2 * per_row, sizes["dp"], rows), (1, 0, 2)
    ).reshape(1, ff)
    a_halves = [
        jnp.concatenate([a_halves[k], after(a_next[k], qkv_rows)], axis=0) for k in range(2)
    ]
    a_more = [exchange(part, paths[k][len(far) + 1], sizes) for k, part in enumerate(a_halves)]
    b_held = jnp.concatenate([b_held, after(b_next, qkv_rows)], axis=0)
    b_halves = [b_held[:, :, :down_cut], b_held[:, :, down_cut:]]
    b_next = [exchange(part, paths[k][len(far)], sizes) for k, part in enumerate(b_halves)]
    attended, lse = attend(after(qkv_rows, *a_halves, *b_halves))

    def crossed(parts, more):
        pieces = []
        for k in range(2):
            both = (parts[k], more[k])
            pieces += [*both, *[exchange(part, core, sizes) for part in both]]
        return pieces

    def tokens_of(values, index):
        return lax.dynamic_slice_in_dim(values, index * piece_len, piece_len, 0)

    attended_own = tokens_of(attended, seq_index)
    attended_other = exchange(tokens_of(attended, 1 - seq_index), swap, sizes)
    a_parts = crossed(a_halves, [after(part, attended) for part in a_more])
    b_halves = [
        jnp.concatenate([b_halves[k], after(b_next[k], attended)], axis=0) for k in range(2)
    ]
    b_more = [exchange(part, paths[k][len(far) + 1], sizes) for k, part in enumerate(b_halves)]
    mlp_grad = cotangent.reshape(piece_len, model_width)
    slots = sizes["dp"] * sizes["seq"]
    chunk = math.gcd(ff, 512)
    weight_scratch = [
        pltpu.VMEM((model_width, model_width), bf16),
        pltpu.VMEM((model_width, ff), bf16),
    ]
    middle, normed_two, hidden, slope = local_call(
        functools.partial(hidden_kernel, paths, rows, cut, chunk),
        pair,
        [attended_own, attended_other, after(x_own, *b_halves), vec_rows, bias_row],
        a_parts,
        [
            shaped(f32, piece_len, model_width),
            shaped(bf16, piece_len, model_width),
            shaped(bf16, piece_len, ff),
            shaped(bf16, piece_len, ff),
        ],
        [],
        weight_scratch + [dma((3, slots))],
        dense * (model_width + ff),
    )
    b_parts = crossed(b_halves, [after(part, hidden) for part in b_more])
    down_keep, down_send = local_call(
        functools.partial(down_grad_kernel, paths, rows, down_cut, chunk),
        pair,
        [hidden, mlp_grad],
        [],
        [],
        [shaped(bf16, slots // 2, rows, ff // 2)] * 2,
        [
            pltpu.VMEM((model_width, ff), bf16),
            pltpu.VMEM((model_width, piece_len), bf16),
            dma((2, slots)),
        ],
        dense * ff,
    )

    down_other = exchange(down_send, core, sizes)
    up_grad, norm_two_grad, bias_sums = local_call(
        functools.partial(mlp_back_kernel, paths, rows, cut, down_cut, chunk),
        pair,
        [slope, after(mlp_grad, down_keep)],
        a_parts + b_parts,
        [
            shaped(bf16, piece_len, ff),
            shaped(f32, piece_len, model_width),
            shaped(f32, 8, ff),
        ],
        [],
        weight_scratch + [pltpu.VMEM((model_width, ff), bf16), dma((3, slots)), dma((2, slots))],
        2 * dense * ff,
    )
    down_keeps, down_sends = [None] * 2, [None] * 2
    down_keeps[0], down_sends[0], down_keeps[1], down_sends[1] = quarters(
        down_keep, after(down_other, norm_two_grad), down_cut
    )
    down_others = [exchange(down_sends[k], (swap, row_hop)[1 - k], sizes) for k in range(2)]
    middle_grad, attn_out_grad, grads_own, grads_send, sums = local_call(
        functools.partial(middle_back_kernel, paths, rows, w_out.shape[1]),
        pair,
        [after(norm_two_grad, *down_keeps), middle, mlp_grad, vec_rows],
        a_parts[:4],
        [
            shaped(f32, piece_len, model_width),
            shaped(bf16, piece_len, model_width),
            shaped(bf16, piece_len, half_width),
            shaped(bf16, piece_len, half_width),
            shaped(f32, 8, model_width),
        ],
        [],
        [weight_scratch[0], dma((1, slots))],
        dense * model_width,
    )
    grads_other = exchange(grads_send, swap, sizes)
    back_cut = 8 * (up_cols + w_out.shape[1]) // 15 // 128 * 128
    up_keep, up_send = local_call(
        functools.partial(up_grad_kernel, paths, rows, back_cut, chunk),
        pair,
        [normed_two, up_grad, attended_own, attended_other, attn_out_grad],
        [],
        [],
        [shaped(bf16, slots // 2, rows, (ff + model_width) // 2)] * 2,
        [
            pltpu.VMEM((model_width, ff), bf16),
            pltpu.VMEM((model_width, model_width), bf16),
            pltpu.VMEM((model_width, piece_len), bf16),
            dma((3, slots)),
        ],
        dense * (model_width + ff),
    )
    up_other = exchange(up_send, core, sizes)
    grad_heads = in_order(seq_index, grads_own, after(grads_other, up_keep), 0)
    down_others = [after(part, up_keep) for part in down_others]
    down_sums = halves([(down_keeps[k], down_others[k]) for k in range(2)])
    down_keeps, down_sends = down_sums[0::2], down_sums[1::2]
    down_others = [exchange(down_sends[k], (swap, row_hop)[k], sizes) for k in range(2)]

    def head_pair_back(at, *earlier):
        return attend_back(after(qkv_rows, *earlier), grad_heads, attended, lse, at)

    pair_grads = [head_pair_back(0)]
    up_keeps, up_sends = [None] * 2, [None] * 2
    up_keeps[0], up_sends[0], up_keeps[1], up_sends[1] = quarters(
        up_keep, after(up_other, pair_grads[0][0]), back_cut
    )
    up_others = [exchange(up_sends[k], (swap, row_hop)[1 - k], sizes) for k in range(2)]
    down_keep, down_send = rejoin(
        [(down_keeps[k], after(down_others[k], pair_grads[0][0])) for k in range(2)]
    )
    down_other = exchange(down_send, far[1], sizes)
    pair_grads.append(head_pair_back(1, up_keeps[0], down_keep))
    down_keep, down_send = halves([(down_keep, after(down_other, pair_grads[1][0]))])
    down_other = exchange(down_send, far[0], sizes)
    pair_grads += [head_pair_back(at, down_keep) for at in range(2, half_width // 128)]
    up_sums = halves(
        [(up_keeps[k], after(up_others[k], pair_grads[-1][0])) for k in range(2)]
    )
    up_keeps, up_sends = up_sums[0::2], up_sums[1::2]
    up_others = [exchange(up_sends[k], (swap, row_hop)[k], sizes) for k in range(2)]
    bias_rows = jnp.transpose(
        bias_sums[0].reshape(sizes["dp"], 2 * per_row, rows), (1, 0, 2)
    ).reshape(2 * per_row, model_width)
    da_own, da_send, last_keep, last_send = local_call(
        functools.partial(project_back_kernel, path_dp, rows, half_width // 128),
        pair,
        [
            *[after(grad, *up_keeps) for group in pair_grads for grad in group],
            qkv_full,
            normed_one,
            x_own,
            x_other,
            vec_rows,
            sums,
            bias_rows,
        ],
        [],
        [shaped(f32, piece_len, model_width), shaped(bf16, piece_len, model_width)],
        [shaped(bf16, sizes["dp"] // 2, rows, head_width + 128)] * 2,
        [
            pltpu.VMEM((seq_len, head_width), bf16),
            pltpu.VMEM((model_width, head_width + 128), bf16),
            pltpu.VMEM((2, piece_len, model_width), f32),
            pltpu.VMEM((128, model_width), f32),
            pltpu.VMEM((model_width, seq_len), bf16),
            dma((1, sizes["dp"])),
        ],
        4 * dense * head_width,
    )
    last_other = exchange(last_send, core, sizes)
    da_other = exchange(da_send, swap, sizes)
    last_keep, last_send = halves([(last_keep, last_other)])
    last_other = exchange(last_send, row_hop, sizes)
    up_keep, up_send = rejoin([(up_keeps[k], after(up_others[k], last_send)) for k in range(2)])
    up_other = exchange(up_send, far[1], sizes)
    grad_down = down_keep[0].astype(f32) + after(down_other, last_send)[0].astype(f32)
    (result,) = local_call(
        functools.partial(result_kernel, paths, rows, down_cut),
        pair,
        [hidden, after(middle, last_send, up_send), vec_rows],
        b_parts,
        [shaped(bf16, piece_len, model_width)],
        [],
        [pltpu.VMEM((model_width, ff), bf16), dma((2, slots))],
        dense * ff,
    )
    last_keep, last_send = halves([(last_keep, after(last_other, result))])
    last_other = exchange(last_send, far[1], sizes)
    up_keep, up_send = halves([(up_keep, after(up_other, last_send))])
    up_other = exchange(up_send, far[0], sizes)
    norm_one_own = da_own + after(da_other, last_send).astype(f32)
    unit, inverse = normed(x_own.astype(f32))
    input_grad = middle_grad + normed_back(norm_one_own, unit, inverse, vec_rows[0:1])
    last_keep, last_send = halves([(last_keep, after(last_other, input_grad))])
    last_other = exchange(last_send, far[0], sizes)
    up_other = after(up_other, last_send)
    grad_up_out = up_keep[0].astype(f32) + up_other[0].astype(f32)
    grad_up, grad_out = grad_up_out[:, :up_cols], grad_up_out[:, up_cols:]
    last = last_keep[0].astype(f32) + last_other[0].astype(f32)
    small_last = last[:, 3 * half_width :]
    sent = jnp.where(
        seq_index == 0, last[:, 2 * half_width :],
        jnp.concatenate([last[:, :half_width], small_last], axis=1)
    )
    arrived_last = exchange(sent.astype(jnp.bfloat16), swap, sizes).astype(jnp.float32)
    middle_block = arrived_last[:, :half_width]
    kept = jnp.where(seq_index == 0, last[:, : 2 * half_width], last[:, half_width : 3 * half_width])
    grad_qkv = jnp.concatenate([kept[:, :half_width], middle_block, kept[:, half_width:]], axis=1)
    small_sum = small_last + arrived_last[:, half_width:]
    grad_vectors = small_sum[:, :8]
    bias_own = lax.dynamic_slice_in_dim(small_sum, 8 + seq_index * per_row, per_row, 1)
    grad_up_bias = bias_own.T.reshape(-1)
    return (
        result.reshape(1, piece_len, model_width),
        input_grad.reshape(1, piece_len, model_width),
        grad_qkv,
        grad_out,
        grad_up,
        grad_down,
        grad_up_bias,
        grad_vectors,
    )


def block(*arrays):
    n_dp, n_seq = lax.axis_size("dp"), lax.axis_size("seq")
    rows = arrays[2].shape[0]
    whole_tiles = rows % 16 == 0 and all(weight.shape[1] % 384 == 0 for weight in arrays[2:6])
    powers = n_dp == 16
    if n_seq == 2 and powers and whole_tiles and arrays[0].shape[0] == 1:
        return on_device(*arrays)
    return on_device_general(*arrays)


def solution(mesh):
    placed = (
        P("dp", "seq", None),
        P("dp", None),
        P("dp", "seq"),
        P("dp", "seq"),
        P("dp", "seq"),
        P("dp", "seq"),
        P(("dp", "seq")),
        P("dp", "seq", None),
    )
    return jax.shard_map(
        block,
        mesh=mesh,
        in_specs=placed,
        out_specs=(
            P("dp", "seq", None),
            P("dp", "seq", None),
            P("dp", "seq"),
            P("dp", "seq"),
            P("dp", "seq"),
            P("dp", "seq"),
            P(("dp", "seq")),
            P("dp", None),
        ),
        check_vma=False,
    )
```

```python
import functools
import math

import jax
import jax.numpy as jnp
from jax import lax
from jax.experimental import pallas as pl
from jax.experimental.pallas import tpu as pltpu
from jax.sharding import PartitionSpec as P

HEADS = 12
HEAD_DIM = 64
VMEM_LIMIT = 28 * 1024 * 1024


EPSILON = 1e-05
MASKED = -1e30


def norm_rows(values, scale_row, shift_row):
    row_mean = jnp.mean(values, axis=-1, keepdims=True)
    centered = values - row_mean
    variance = jnp.mean(centered * centered, axis=-1, keepdims=True)
    return centered * lax.rsqrt(variance + EPSILON) * scale_row + shift_row


def gelu_tanh(values):
    return (
        0.5
        * values
        * (1.0 + jnp.tanh(0.7978845608028654 * (values + 0.044715 * values * values * values)))
    )


def contract_last(left_side, right_side):
    return lax.dot_general(
        left_side, right_side, (((1,), (1,)), ((), ())), preferred_element_type=jnp.float32
    )


def contract_first(left_side, right_side):
    return lax.dot_general(
        left_side, right_side, (((0,), (0,)), ((), ())), preferred_element_type=jnp.float32
    )


def on_device_general(inputs, vectors, w_qkv, w_out, w_up, w_down, up_bias, cotangent):
    seq_count, piece_len, model_width = inputs.shape
    row_count = seq_count * piece_len
    score_scale = HEAD_DIM ** (-0.5)
    seq_index = lax.axis_index("seq")
    query_pos = seq_index * piece_len + jnp.arange(piece_len)
    qkv_cols, out_cols, up_cols, down_cols, upb_cols = (
        lax.all_gather(w_qkv, "seq", axis=1, tiled=True),
        lax.all_gather(w_out, "seq", axis=1, tiled=True),
        lax.all_gather(w_up, "seq", axis=1, tiled=True),
        lax.all_gather(w_down, "seq", axis=1, tiled=True),
        lax.all_gather(up_bias, "seq", axis=0, tiled=True),
    )
    full_fwd = (
        lax.all_gather(qkv_cols, "dp", axis=0, tiled=True),
        lax.all_gather(out_cols, "dp", axis=0, tiled=True),
        lax.all_gather(up_cols, "dp", axis=0, tiled=True),
        lax.all_gather(down_cols, "dp", axis=0, tiled=True),
        lax.all_gather(upb_cols, "dp", axis=0, tiled=True),
        lax.all_gather(vectors, "dp", axis=0, tiled=True),
    )
    qkv_full, out_full, up_full, down_full, upb_full, vec_full = full_fwd
    vec_values = vec_full.astype(jnp.float32)
    resid_in = inputs.reshape(row_count, model_width).astype(jnp.float32)
    normed_one = norm_rows(resid_in, vec_values[:, 0], vec_values[:, 1]).astype(jnp.bfloat16)
    qkv_bias = jnp.concatenate(
        [vec_values[:, 2], jnp.zeros_like(vec_values[:, 2]), vec_values[:, 3]]
    )
    qkv_rows = (
        jnp.dot(normed_one, qkv_full, preferred_element_type=jnp.float32) + qkv_bias
    ).astype(jnp.bfloat16)
    queries = qkv_rows[:, :model_width].reshape(seq_count, piece_len, HEADS, HEAD_DIM)
    key_vals = qkv_rows[:, model_width:].reshape(seq_count, piece_len, 2 * model_width)

    def block_scores(key_block, first_row):
        key_rows = key_block.shape[1]
        keys_part = key_block[..., :model_width].reshape(seq_count, key_rows, HEADS, HEAD_DIM)
        scores = (
            jnp.einsum("bqhd,bkhd->bhqk", queries, keys_part, preferred_element_type=jnp.float32)
            * score_scale
        )
        causal = (first_row + jnp.arange(key_rows))[None, :] <= query_pos[:, None]
        return jnp.where(causal, scores, MASKED)

    key_block = lax.all_gather(key_vals, "seq", axis=1, tiled=True)
    run_max = jnp.full((seq_count, HEADS, piece_len), MASKED, jnp.float32)
    key_rows = key_block.shape[1]
    values_part = key_block[..., model_width:].reshape(seq_count, key_rows, HEADS, HEAD_DIM)
    scores = block_scores(key_block, jnp.int32(0))
    new_max = jnp.maximum(run_max, jnp.max(scores, axis=-1))
    exp_scores = jnp.exp(scores - new_max[..., None])
    run_total = jnp.sum(exp_scores, axis=-1)
    added_part = jnp.einsum(
        "bhqk,bkhd->bqhd",
        exp_scores.astype(jnp.bfloat16),
        values_part,
        preferred_element_type=jnp.float32,
    )
    run_acc = added_part
    run_max, run_total, run_acc = (new_max, run_total, run_acc)
    attended = run_acc / jnp.transpose(run_total, (0, 2, 1))[..., None]
    log_total = run_max + jnp.log(run_total)
    attended_lo = attended.reshape(row_count, model_width).astype(jnp.bfloat16)
    branch_attn = (
        jnp.dot(attended_lo, out_full, preferred_element_type=jnp.float32) + vec_values[:, 4]
    )
    middle = resid_in + branch_attn
    normed_two = norm_rows(middle, vec_values[:, 5], vec_values[:, 6]).astype(jnp.bfloat16)
    up_act = jnp.dot(normed_two, up_full, preferred_element_type=jnp.float32) + upb_full.astype(
        jnp.float32
    )
    hidden = gelu_tanh(up_act).astype(jnp.bfloat16)
    branch_mlp = contract_last(hidden, down_full) + vec_values[:, 7]
    result = middle + branch_mlp
    qkv_back, out_back, up_back, down_back = (qkv_full, out_full, up_full, down_full)
    out_grad = cotangent.reshape(row_count, model_width).astype(jnp.float32)
    mlp_grad = out_grad.astype(jnp.bfloat16)
    hidden_grad = jnp.dot(mlp_grad, down_back, preferred_element_type=jnp.float32)
    gelu_pull = jax.vjp(gelu_tanh, up_act)[1]
    up_grad = gelu_pull(hidden_grad)[0].astype(jnp.bfloat16)
    norm_two_grad = contract_last(up_grad, up_back)
    ln_two_pull = jax.vjp(norm_rows, middle, vec_values[:, 5], vec_values[:, 6])[1]
    middle_part, scale_two, shift_two = ln_two_pull(norm_two_grad)
    middle_grad = out_grad + middle_part
    attn_out_grad = middle_grad.astype(jnp.bfloat16)
    attended_grad = contract_last(attn_out_grad, out_back).astype(jnp.bfloat16)
    grad_heads = attended_grad.reshape(seq_count, piece_len, HEADS, HEAD_DIM)
    row_delta = jnp.transpose(
        jnp.sum(grad_heads.astype(jnp.float32) * attended, axis=-1), (0, 2, 1)
    )
    key_vals_all = lax.all_gather(key_vals, "seq", axis=1, tiled=True)
    total_len = key_vals_all.shape[1]
    key_block_len = math.gcd(total_len, 512)

    def back_step(query_acc, block_index):
        first_row = block_index * key_block_len
        key_block = lax.dynamic_slice_in_dim(key_vals_all, first_row, key_block_len, 1)
        keys_part = key_block[..., :model_width].reshape(seq_count, key_block_len, HEADS, HEAD_DIM)
        values_part = key_block[..., model_width:].reshape(
            seq_count, key_block_len, HEADS, HEAD_DIM
        )
        scores = block_scores(key_block, first_row)
        attn_probs = jnp.exp(scores - log_total[..., None])
        prob_grad = jnp.einsum(
            "bqhd,bkhd->bhqk", grad_heads, values_part, preferred_element_type=jnp.float32
        )
        score_grad = (attn_probs * (prob_grad - row_delta[..., None])).astype(jnp.bfloat16)
        step_part = jnp.einsum(
            "bhqk,bkhd->bqhd", score_grad, keys_part, preferred_element_type=jnp.float32
        )
        key_grad = (
            jnp.einsum("bhqk,bqhd->bkhd", score_grad, queries, preferred_element_type=jnp.float32)
            * score_scale
        )
        value_grad = jnp.einsum(
            "bhqk,bqhd->bkhd",
            attn_probs.astype(jnp.bfloat16),
            grad_heads,
            preferred_element_type=jnp.float32,
        )
        key_value = jnp.concatenate(
            [
                key_grad.reshape(seq_count, key_block_len, model_width),
                value_grad.reshape(seq_count, key_block_len, model_width),
            ],
            axis=-1,
        )
        return (query_acc + step_part * score_scale, key_value)

    query_grad, kv_blocks = lax.scan(
        back_step,
        jnp.zeros((seq_count, piece_len, HEADS, HEAD_DIM), jnp.float32),
        jnp.arange(total_len // key_block_len),
    )
    kv_terms = jnp.moveaxis(kv_blocks, 0, 1).reshape(seq_count, total_len, 2 * model_width)
    key_val_grad = lax.psum_scatter(
        kv_terms.astype(jnp.bfloat16), "seq", scatter_dimension=1, tiled=True
    ).astype(jnp.float32)
    key_val_grad = key_val_grad.reshape(row_count, 2 * model_width)
    qkv_grad = jnp.concatenate(
        [query_grad.reshape(row_count, model_width), key_val_grad], axis=1
    ).astype(jnp.bfloat16)
    norm_one_grad = contract_last(qkv_grad, qkv_back)
    ln_one_pull = jax.vjp(norm_rows, resid_in, vec_values[:, 0], vec_values[:, 1])[1]
    input_part, scale_one, shift_one = ln_one_pull(norm_one_grad)
    input_grad = middle_grad + input_part
    whole_qkv = contract_first(normed_one, qkv_grad)
    whole_out = contract_first(attended_lo, attn_out_grad)
    whole_up = contract_first(normed_two, up_grad)
    whole_down = contract_first(mlp_grad, hidden)
    row_qkv, row_out, row_up, row_down = (
        lax.psum_scatter(
            whole_qkv.astype(jnp.bfloat16), "dp", scatter_dimension=0, tiled=True
        ).astype(jnp.float32),
        lax.psum_scatter(
            whole_out.astype(jnp.bfloat16), "dp", scatter_dimension=0, tiled=True
        ).astype(jnp.float32),
        lax.psum_scatter(
            whole_up.astype(jnp.bfloat16), "dp", scatter_dimension=0, tiled=True
        ).astype(jnp.float32),
        lax.psum_scatter(
            whole_down.astype(jnp.bfloat16), "dp", scatter_dimension=0, tiled=True
        ).astype(jnp.float32),
    )
    grad_qkv, grad_out, grad_up, grad_down = (
        lax.psum_scatter(
            row_qkv.astype(jnp.bfloat16), "seq", scatter_dimension=1, tiled=True
        ).astype(jnp.float32),
        lax.psum_scatter(
            row_out.astype(jnp.bfloat16), "seq", scatter_dimension=1, tiled=True
        ).astype(jnp.float32),
        lax.psum_scatter(
            row_up.astype(jnp.bfloat16), "seq", scatter_dimension=1, tiled=True
        ).astype(jnp.float32),
        lax.psum_scatter(
            row_down.astype(jnp.bfloat16), "seq", scatter_dimension=1, tiled=True
        ).astype(jnp.float32),
    )
    vec_term = jnp.stack(
        [
            scale_one,
            shift_one,
            jnp.sum(qkv_grad[:, :model_width].astype(jnp.float32), axis=0),
            jnp.sum(qkv_grad[:, 2 * model_width :].astype(jnp.float32), axis=0),
            jnp.sum(attn_out_grad.astype(jnp.float32), axis=0),
            scale_two,
            shift_two,
            jnp.sum(mlp_grad.astype(jnp.float32), axis=0),
        ],
        axis=1,
    )
    upb_term = jnp.sum(up_grad.astype(jnp.float32), axis=0)
    vec_sum, upb_sum = lax.psum((vec_term, upb_term), ("dp", "seq"))
    vec_rows = vectors.shape[0]
    grad_vectors = lax.dynamic_slice_in_dim(vec_sum, lax.axis_index("dp") * vec_rows, vec_rows, 0)
    upb_rows = up_bias.shape[0]
    upb_start = (lax.axis_index("dp") * lax.axis_size("seq") + seq_index) * upb_rows
    grad_up_bias = lax.dynamic_slice_in_dim(upb_sum, upb_start, upb_rows, 0)
    return (
        result.reshape(seq_count, piece_len, model_width).astype(jnp.bfloat16),
        input_grad.reshape(seq_count, piece_len, model_width),
        grad_qkv,
        grad_out,
        grad_up,
        grad_down,
        grad_up_bias,
        grad_vectors,
    )


def bit_masks(count):
    return [1 << k for k in range(count.bit_length() - 1)]


def exchange(values, hop, sizes):
    axis, mask = hop
    return lax.ppermute(values, axis, [(i, i ^ mask) for i in range(sizes[axis])])


def slot_owner(slot, path):
    offset = {"dp": 0, "seq": 0}
    for k, (axis, mask) in enumerate(path):
        if slot >> k & 1:
            offset[axis] ^= mask
    return offset["dp"], offset["seq"]


def after(values, *earlier):
    return lax.optimization_barrier((values, *earlier))[0]


def grow(held, hop, sizes):
    return jnp.concatenate([held, exchange(held, hop, sizes)], axis=0)


def start_place(path, rows, parts, me_ref, targets, sems):
    total = 1 << len(path)
    each = total // len(parts)
    copies = []
    for k, (target, first, cols, stride, at) in enumerate(targets):
        for slot in range(total):
            off_dp, off_seq = slot_owner(slot, path)
            row = pl.multiple_of((me_ref[0] ^ off_dp) * rows, 16)
            col = pl.multiple_of((me_ref[1] ^ off_seq) * stride + at, 128)
            src = parts[slot // each].at[slot % each, :, pl.ds(first, cols)]
            dst = target.at[pl.ds(row, rows), pl.ds(col, cols)]
            copy = pltpu.make_async_copy(src, dst, sems.at[k, slot])
            copy.start()
            copies.append(copy)
    return copies


def start_split(rows, me_ref, pieces, keep_ref, send_ref, sems):
    copies = []
    for k, (path, whole, stride, first, cols, at) in enumerate(pieces):
        half = 1 << (len(path) - 1)
        for slot in range(2 * half):
            off_dp, off_seq = slot_owner(slot, path)
            row = pl.multiple_of((me_ref[0] ^ off_dp) * rows, 16)
            col = pl.multiple_of((me_ref[1] ^ off_seq) * stride + first, 128)
            target = keep_ref if slot < half else send_ref
            copy = pltpu.make_async_copy(
                whole.at[pl.ds(row, rows), pl.ds(col, cols)],
                target.at[slot % half, :, pl.ds(at, cols)],
                sems.at[k, slot],
            )
            copy.start()
            copies.append(copy)
    return copies


def wait_all(copies):
    for copy in copies:
        copy.wait()


def normed(values):
    centered = values - jnp.mean(values, axis=-1, keepdims=True)
    inverse = lax.rsqrt(jnp.mean(centered * centered, axis=-1, keepdims=True) + EPSILON)
    return centered * inverse, inverse


def normed_back(grads, unit, inverse, scale_row):
    scaled = grads * scale_row
    mean_one = jnp.mean(scaled, axis=-1, keepdims=True)
    mean_two = jnp.mean(scaled * unit, axis=-1, keepdims=True)
    return inverse * (scaled - mean_one - unit * mean_two)


def dot(left_side, right_side):
    return jnp.dot(left_side, right_side, preferred_element_type=jnp.float32)


def column_sum(values):
    return jnp.sum(values.astype(jnp.float32), axis=0, keepdims=True)


def project_kernel(path, rows, me_ref, own_ref, other_ref, *refs):
    parts = refs[:2]
    qkv_ref, a_ref, w_ref, vec_ref, small, sems = refs[2:]
    seq = me_ref[1]
    piece, width = own_ref.shape
    third = w_ref.shape[1] // 3
    copies = start_place(
        path,
        rows,
        parts,
        me_ref,
        [(small, 3 * third, 128, 0, 0), (w_ref, 0, 3 * third, 0, 0)],
        sems,
    )
    units = []
    for part in range(2):
        values = jnp.where(seq == part, own_ref[...], other_ref[...]).astype(jnp.float32)
        units.append(normed(values)[0])
    wait_all(copies[: len(copies) // 2])
    vec_ref[...] = small[...].astype(jnp.float32).T[: vec_ref.shape[0]]
    for part in range(2):
        a_ref[part * piece : (part + 1) * piece, :] = (
            units[part] * vec_ref[0:1, :] + vec_ref[1:2, :]
        ).astype(jnp.bfloat16)
    wait_all(copies[len(copies) // 2 :])
    own_cols = pl.ds(pl.multiple_of(seq * third, 128), third)
    for k in range(3):
        cols = slice(k * third, (k + 1) * third)
        for part in range(2):
            at = slice(part * piece, (part + 1) * piece)
            product = dot(a_ref[at, :], w_ref[:, cols])
            if k != 1:
                product = product + vec_ref[2 + k // 2 : 3 + k // 2, own_cols]
            qkv_ref[at, cols] = product.astype(jnp.bfloat16)


def in_vmem(count):
    return [pl.BlockSpec(memory_space=pltpu.VMEM)] * count


def in_any(count):
    return [pl.BlockSpec(memory_space=pl.ANY)] * count


def shaped(dtype, *shape):
    return jax.ShapeDtypeStruct(shape, dtype)


def local_call(kernel, pair, vmem_args, any_args, vmem_outs, any_outs, scratch, flops):
    outs = list(vmem_outs) + list(any_outs)
    moved = sum(a.size * a.dtype.itemsize for a in [*vmem_args, *any_args, *outs])
    return pl.pallas_call(
        kernel,
        out_shape=outs,
        in_specs=[pl.BlockSpec(memory_space=pltpu.SMEM)]
        + in_vmem(len(vmem_args))
        + in_any(len(any_args)),
        out_specs=in_vmem(len(vmem_outs)) + in_any(len(any_outs)),
        scratch_shapes=scratch,
        compiler_params=pltpu.CompilerParams(vmem_limit_bytes=VMEM_LIMIT),
        cost_estimate=pl.CostEstimate(flops=100000000000, bytes_accessed=10**7, transcendentals=0),
    )(pair, *vmem_args, *any_args)


def gelu_both(values):
    square = values * values
    angle = jnp.tanh(0.7978845608028654 * values * (1.0 + 0.044715 * square))
    half = 0.5 * (1.0 + angle)
    slope = half + 0.5 * values * (1.0 - angle * angle) * (
        0.7978845608028654 * (1.0 + 3.0 * 0.044715 * square)
    )
    return values * half, slope


def place_out_up(paths, rows, cut, parts, me_ref, w_out, w_up, sems):
    out_cols, up_cols = w_out.shape[1] // 2, w_up.shape[1] // 2
    left = cut - out_cols
    copies = start_place(
        paths[0],
        rows,
        parts[:4],
        me_ref,
        [(w_out, 0, out_cols, out_cols, 0), (w_up, out_cols, left, up_cols, 0)],
        sems,
    )
    slots = 1 << len(paths[0])
    more = start_place(
        paths[1], rows, parts[4:], me_ref, [(w_up, 0, up_cols - left, up_cols, left)], sems.at[2:3]
    )
    return copies[:slots], copies[slots:] + more


def place_down(paths, rows, cut, parts, me_ref, w_down, sems):
    cols = w_down.shape[1] // 2
    return start_place(
        paths[0], rows, parts[:4], me_ref, [(w_down, 0, cut, cols, 0)], sems
    ) + start_place(
        paths[1], rows, parts[4:], me_ref, [(w_down, 0, cols - cut, cols, cut)], sems.at[1:2]
    )


def hidden_kernel(paths, rows, cut, chunk, me_ref, *refs):
    mine_ref, other_ref, x_ref, vec_ref, bias_ref = refs[:5]
    parts = refs[5:13]
    h_ref, a_ref, g_ref, slope_ref = refs[13:17]
    w_out, w_up, sems = refs[17:]
    left_first = me_ref[1] == 0
    half = mine_ref.shape[1]
    out_copies, up_copies = place_out_up(paths, rows, cut, parts, me_ref, w_out, w_up, sems)
    left = jnp.where(left_first, mine_ref[...], other_ref[...])
    right = jnp.where(left_first, other_ref[...], mine_ref[...])
    wait_all(out_copies)
    branch = dot(left, w_out[:half, :]) + dot(right, w_out[half:, :]) + vec_ref[4:5, :]
    middle = x_ref[...].astype(jnp.float32) + branch
    h_ref[...] = middle
    a_ref[...] = (normed(middle)[0] * vec_ref[5:6, :] + vec_ref[6:7, :]).astype(jnp.bfloat16)
    wait_all(up_copies)

    def step(k, carry):
        cols = pl.ds(pl.multiple_of(k * chunk, chunk), chunk)
        act = dot(a_ref[...], w_up[:, cols]) + bias_ref[:, cols]
        value, slope = gelu_both(act)
        g_ref[:, cols] = value.astype(jnp.bfloat16)
        slope_ref[:, cols] = slope.astype(jnp.bfloat16)
        return carry

    lax.fori_loop(0, w_up.shape[1] // chunk, step, 0)


def down_grad_kernel(paths, rows, cut, chunk, me_ref, *refs):
    g_ref, dy_ref, keep_ref, send_ref, grad, dy_t, sems = refs
    dy_t[...] = dy_ref[...].T

    def step(k, carry):
        cols = pl.ds(pl.multiple_of(k * chunk, chunk), chunk)
        grad[:, cols] = dot(dy_t[...], g_ref[:, cols]).astype(jnp.bfloat16)
        return carry

    lax.fori_loop(0, grad.shape[1] // chunk, step, 0)
    cols = grad.shape[1] // 2
    pieces = [
        (paths[0], grad, cols, 0, cut, 0),
        (paths[1], grad, cols, cut, cols - cut, cut),
    ]
    wait_all(start_split(rows, me_ref, pieces, keep_ref, send_ref, sems))


def mlp_back_kernel(paths, rows, cut, down_cut, chunk, me_ref, *refs):
    slope_ref, dy_ref = refs[:2]
    parts, down_parts = refs[2:10], refs[10:18]
    du_ref, acc, bias_sum_ref = refs[18:21]
    w_out, w_up, w_down, sems, down_sems = refs[21:]
    down_copies = place_down(paths, rows, down_cut, down_parts, me_ref, w_down, down_sems)
    out_copies, up_copies = place_out_up(paths, rows, cut, parts, me_ref, w_out, w_up, sems)
    acc[...] = jnp.zeros_like(acc)
    wait_all(down_copies)
    wait_all(out_copies)
    wait_all(up_copies)

    def step(k, carry):
        cols = pl.ds(pl.multiple_of(k * chunk, chunk), chunk)
        up_grad = (
            dot(dy_ref[...], w_down[:, cols]) * slope_ref[:, cols].astype(jnp.float32)
        ).astype(jnp.bfloat16)
        du_ref[:, cols] = up_grad
        bias_sum_ref[0:1, cols] = column_sum(up_grad)
        acc[...] += contract_last(up_grad, w_up[:, cols])
        return carry

    lax.fori_loop(0, w_up.shape[1] // chunk, step, 0)


def middle_back_kernel(paths, rows, out_cols, me_ref, *refs):
    acc_ref, h_ref, dy_ref, vec_ref = refs[:4]
    parts = refs[4:8]
    dh_ref, dz_ref, do_keep_ref, do_send_ref, sum_ref = refs[8:13]
    w_out, sems = refs[13:]
    left_first = me_ref[1] == 0
    copies = start_place(
        paths[0], rows, parts, me_ref, [(w_out, 0, out_cols, out_cols, 0)], sems
    )
    out_grad = dy_ref[...].astype(jnp.float32)
    unit, inverse = normed(h_ref[...])
    grads = acc_ref[...]
    middle_grad = out_grad + normed_back(grads, unit, inverse, vec_ref[5:6, :])
    dh_ref[...] = middle_grad
    attn_grad = middle_grad.astype(jnp.bfloat16)
    dz_ref[...] = attn_grad
    wait_all(copies)
    half = do_keep_ref.shape[1]
    left = contract_last(attn_grad, w_out[:half, :])
    right = contract_last(attn_grad, w_out[half:, :])
    do_keep_ref[...] = jnp.where(left_first, left, right).astype(jnp.bfloat16)
    do_send_ref[...] = jnp.where(left_first, right, left).astype(jnp.bfloat16)
    sum_ref[...] = jnp.concatenate(
        [
            column_sum(attn_grad),
            column_sum(grads * unit),
            column_sum(grads),
            column_sum(out_grad),
            jnp.zeros((4, out_grad.shape[1]), jnp.float32),
        ],
        axis=0,
    )


def result_kernel(paths, rows, down_cut, me_ref, *refs):
    g_ref, h_ref, vec_ref = refs[:3]
    parts = refs[3:11]
    res_ref, w_down, sems = refs[11:]
    wait_all(place_down(paths, rows, down_cut, parts, me_ref, w_down, sems))
    for first in range(0, w_down.shape[0], 256):
        cols = slice(first, first + 256)
        res_ref[:, cols] = (
            h_ref[:, cols] + contract_last(g_ref[...], w_down[cols, :]) + vec_ref[7:8, cols]
        ).astype(jnp.bfloat16)


def up_grad_kernel(paths, rows, cut, chunk, me_ref, *refs):
    a_ref, du_ref, mine_ref, other_ref, dz_ref, keep_ref, send_ref = refs[:7]
    grad_up, grad_out, left_t, sems = refs[7:]
    left_first = me_ref[1] == 0
    half = mine_ref.shape[1]
    left_t[...] = a_ref[...].T

    def step(k, carry):
        cols = pl.ds(pl.multiple_of(k * chunk, chunk), chunk)
        grad_up[:, cols] = dot(left_t[...], du_ref[:, cols]).astype(jnp.bfloat16)
        return carry

    lax.fori_loop(0, du_ref.shape[1] // chunk, step, 0)
    left = jnp.where(left_first, mine_ref[...], other_ref[...])
    right = jnp.where(left_first, other_ref[...], mine_ref[...])
    grad_out[:half, :] = contract_first(left, dz_ref[...]).astype(jnp.bfloat16)
    grad_out[half:, :] = contract_first(right, dz_ref[...]).astype(jnp.bfloat16)
    up_cols, out_cols = grad_up.shape[1] // 2, grad_out.shape[1] // 2
    pieces = [
        (paths[0], grad_up, up_cols, 0, cut, 0),
        (paths[1], grad_up, up_cols, cut, up_cols - cut, cut),
        (paths[1], grad_out, out_cols, 0, out_cols, up_cols),
    ]
    wait_all(start_split(rows, me_ref, pieces, keep_ref, send_ref, sems))


def project_back_kernel(path, rows, pairs, me_ref, *refs):
    grad_refs = refs[: 3 * pairs]
    w_ref, a_ref, own_ref, other_ref, vec_ref, sum_ref, bias_ref = refs[3 * pairs : 3 * pairs + 7]
    da_own_ref, da_send_ref, keep_ref, send_ref = refs[3 * pairs + 7 : 3 * pairs + 11]
    grads_all, grad, parts, small, a_t, sems = refs[3 * pairs + 11 :]
    seq = me_ref[1]
    piece = own_ref.shape[0]
    third = grads_all.shape[1] // 3
    small[...] = jnp.zeros_like(small)
    a_t[...] = a_ref[...].T
    for k in range(3):
        for pair in range(pairs):
            at = k * third + pair * 128
            grads_all[:, at : at + 128] = grad_refs[3 * pair + k][...]
        cols = slice(k * third, (k + 1) * third)
        grad[:, cols] = dot(a_t[...], grads_all[:, cols]).astype(jnp.bfloat16)
    for part in range(2):
        at = slice(part * piece, (part + 1) * piece)
        grads = contract_last(grads_all[at, :], w_ref[...])
        parts[part] = grads
        values = jnp.where(seq == part, own_ref[...], other_ref[...]).astype(jnp.float32)
        small[0:1, :] += column_sum(grads * normed(values)[0])
        small[1:2, :] += column_sum(grads)
    da_own_ref[...] = parts[seq]
    da_send_ref[...] = parts[1 - seq].astype(jnp.bfloat16)
    own_cols = pl.ds(pl.multiple_of(seq * third, 128), third)
    small[2:3, own_cols] = column_sum(grads_all[:, :third])
    small[3:4, own_cols] = column_sum(grads_all[:, 2 * third :])
    small[4:8, :] = sum_ref[0:4, :]
    bias_rows = bias_ref.shape[0]
    small[8 : 8 + bias_rows, :] = bias_ref[...]
    grad[:, 3 * third :] = small[...].T.astype(jnp.bfloat16)
    pieces = [(path, grad, 0, 0, grad.shape[1], 0)]
    wait_all(start_split(rows, me_ref, pieces, keep_ref, send_ref, sems))


def add_kernel(cuts, count, *refs):
    ins, outs = refs[: 2 * count], refs[2 * count :]
    for pair, first, last, left, right, out, at in cuts:
        keep, other = ins[2 * pair], ins[2 * pair + 1]
        total = keep[first:last, :, left:right].astype(jnp.float32) + other[
            first:last, :, left:right
        ].astype(jnp.float32)
        outs[out][:, :, at : at + right - left] = total.astype(outs[out].dtype)


def add_pairs(pairs, cuts, shapes):
    ins = [array for pair in pairs for array in pair]
    return pl.pallas_call(
        functools.partial(add_kernel, cuts, len(pairs)),
        out_shape=[jax.ShapeDtypeStruct(shape, jnp.bfloat16) for shape in shapes],
        in_specs=in_vmem(len(ins)),
        out_specs=in_vmem(len(shapes)),
        compiler_params=pltpu.CompilerParams(vmem_limit_bytes=VMEM_LIMIT),
    )(*ins)


def halves(pairs):
    cuts, shapes = [], []
    for k, (keep, _) in enumerate(pairs):
        slots, rows, cols = keep.shape
        for part in range(2):
            cuts.append((k, part * slots // 2, (part + 1) * slots // 2, 0, cols, len(shapes), 0))
            shapes.append((slots // 2, rows, cols))
    return add_pairs(pairs, cuts, shapes)


def quarters(keep, other, cut):
    slots, rows, cols = keep.shape
    cuts, shapes = [], []
    for left, right in ((0, cut), (cut, cols)):
        for part in range(2):
            cuts.append(
                (0, part * slots // 2, (part + 1) * slots // 2, left, right, len(shapes), 0)
            )
            shapes.append((slots // 2, rows, right - left))
    return add_pairs([(keep, other)], cuts, shapes)


def rejoin(pairs):
    slots, rows, left_cols = pairs[0][0].shape
    right_cols = pairs[1][0].shape[2]
    cuts, shapes = [], []
    for part in range(2):
        first, last = part * slots // 2, (part + 1) * slots // 2
        cuts.append((0, first, last, 0, left_cols, part, 0))
        cuts.append((1, first, last, 0, right_cols, part, left_cols))
        shapes.append((slots // 2, rows, left_cols + right_cols))
    return add_pairs(pairs, cuts, shapes)


def head_lanes(values, head, width):
    lane = lax.broadcasted_iota(jnp.int32, values.shape, 1)
    return jnp.where(lane // width == head, values, jnp.zeros_like(values))


def later_keys(block):
    key_at = lax.broadcasted_iota(jnp.int32, (block, block), 0)
    query_at = lax.broadcasted_iota(jnp.int32, (block, block), 1)
    return key_at > query_at


def scores_of(keys, query, hidden_keys, block):
    scores = contract_last(keys, query)
    last = jnp.where(hidden_keys, MASKED, scores[-block:])
    if scores.shape[0] == block:
        return last
    return jnp.concatenate([scores[:-block], last], axis=0)


def attend_kernel(block, width, q_ref, k_ref, v_ref, out_ref, lse_ref):
    length, lanes = q_ref.shape
    scale = jnp.bfloat16(width ** (-0.5))
    hidden_keys = later_keys(block)
    values_t = v_ref[...].T
    for first in range(0, length, block):
        last = first + block
        queries = q_ref[first:last, :] * scale
        outs = []
        for head in range(lanes // width):
            scores = scores_of(k_ref[:last, :], head_lanes(queries, head, width), hidden_keys, block)
            top = jnp.max(scores, axis=0, keepdims=True)
            probs = jnp.exp(scores - top)
            total = jnp.sum(probs, axis=0, keepdims=True)
            mixed = jnp.dot(
                values_t[head * width : (head + 1) * width, :last],
                probs.astype(jnp.bfloat16),
                preferred_element_type=jnp.float32,
            )
            outs.append(mixed / total)
            lse_ref[head : head + 1, first:last] = top + jnp.log(total)
        out_ref[first:last, :] = jnp.concatenate(outs, axis=0).T.astype(jnp.bfloat16)


def attend_back_kernel(
    block, width, q_ref, k_ref, v_ref, g_ref, o_ref, lse_ref, dq_ref, dk_ref, dv_ref, dk_acc, dv_acc
):
    length, lanes = q_ref.shape
    heads = lanes // width
    scale = jnp.bfloat16(width ** (-0.5))
    hidden_keys = later_keys(block)
    keys_t = k_ref[...].T
    for first in reversed(range(0, length, block)):
        last = first + block
        queries = q_ref[first:last, :] * scale
        grads = g_ref[first:last, :]
        products = (grads.astype(jnp.float32) * o_ref[first:last, :].astype(jnp.float32)).T
        key_part = value_part = None
        query_parts = []
        for head in range(heads):
            query = head_lanes(queries, head, width)
            grad = head_lanes(grads, head, width)
            scores = scores_of(k_ref[:last, :], query, hidden_keys, block)
            probs = jnp.exp(scores - lse_ref[head : head + 1, first:last])
            delta = jnp.sum(products[head * width : (head + 1) * width], axis=0, keepdims=True)
            prob_grad = contract_last(v_ref[:last, :], grad)
            score_grad = (probs * (prob_grad - delta)).astype(jnp.bfloat16)
            key_term = jnp.dot(score_grad, query, preferred_element_type=jnp.float32)
            value_term = jnp.dot(
                probs.astype(jnp.bfloat16), grad, preferred_element_type=jnp.float32
            )
            key_part = key_term if key_part is None else key_part + key_term
            value_part = value_term if value_part is None else value_part + value_term
            query_parts.append(
                jnp.dot(
                    keys_t[head * width : (head + 1) * width, :last],
                    score_grad,
                    preferred_element_type=jnp.float32,
                )
            )
        query_grad = jnp.concatenate(query_parts, axis=0).T * width ** (-0.5)
        dq_ref[first:last, :] = query_grad.astype(jnp.bfloat16)
        if last == length:
            dk_acc[...] = key_part
            dv_acc[...] = value_part
        else:
            dk_acc[:last, :] += key_part
            dv_acc[:last, :] += value_part
    dk_ref[...] = dk_acc[...].astype(jnp.bfloat16)
    dv_ref[...] = dv_acc[...].astype(jnp.bfloat16)


def pair_spec(length, first):
    return pl.BlockSpec((length, 128), lambda pair: (0, first + pair))


def attend(qkv):
    length, cols = qkv.shape
    pairs = cols // 3 // 128
    return pl.pallas_call(
        functools.partial(attend_kernel, 256, HEAD_DIM),
        grid=(pairs,),
        out_shape=[
            jax.ShapeDtypeStruct((length, cols // 3), jnp.bfloat16),
            jax.ShapeDtypeStruct((8 * pairs, length), jnp.float32),
        ],
        in_specs=[pair_spec(length, k * pairs) for k in range(3)],
        out_specs=[pair_spec(length, 0), pl.BlockSpec((8, length), lambda pair: (pair, 0))],
        compiler_params=pltpu.CompilerParams(vmem_limit_bytes=VMEM_LIMIT),
        cost_estimate=pl.CostEstimate(flops=100000000000, bytes_accessed=10**7, transcendentals=0),
    )(qkv, qkv, qkv)


def attend_back(qkv, grads, attended, lse, pair):
    length, cols = qkv.shape
    pairs = cols // 3 // 128
    column = functools.partial(pair_spec, length)
    return pl.pallas_call(
        functools.partial(attend_back_kernel, 256, HEAD_DIM),
        grid=(1,),
        out_shape=[jax.ShapeDtypeStruct((length, 128), jnp.bfloat16)] * 3,
        in_specs=[column(k * pairs + pair) for k in range(3)]
        + [column(pair)] * 2
        + [pl.BlockSpec((8, length), lambda step: (pair, 0))],
        out_specs=[column(0)] * 3,
        scratch_shapes=[pltpu.VMEM((length, 128), jnp.float32)] * 2,
        compiler_params=pltpu.CompilerParams(vmem_limit_bytes=VMEM_LIMIT),
        cost_estimate=pl.CostEstimate(flops=100000000000, bytes_accessed=10**7, transcendentals=0),
    )(qkv, qkv, qkv, grads, attended, lse)


def in_order(seq_index, mine, other, axis):
    return jnp.where(
        seq_index == 0,
        jnp.concatenate([mine, other], axis=axis),
        jnp.concatenate([other, mine], axis=axis),
    )


def on_device(inputs, vectors, w_qkv, w_out, w_up, w_down, up_bias, cotangent):
    _, piece_len, model_width = inputs.shape
    sizes = {"dp": lax.axis_size("dp"), "seq": lax.axis_size("seq")}
    seq_index = lax.axis_index("seq")
    pair = jnp.stack([lax.axis_index("dp"), seq_index])
    swap = ("seq", 1)
    half_width = model_width // 2
    dp_masks = bit_masks(sizes["dp"])
    core, row_hop = ("dp", dp_masks[0]), ("dp", dp_masks[1])
    far = [("dp", mask) for mask in reversed(dp_masks[2:])]
    path_dp = far + [row_hop, core]
    paths = (far + [swap, row_hop, core], far + [row_hop, swap, core])
    rows = w_qkv.shape[0]
    per_row = up_bias.shape[0] // rows

    bias_cols = up_bias.reshape(per_row, rows).T
    small_own = jnp.concatenate(
        [vectors, bias_cols, jnp.zeros((rows, 128 - 8 - per_row), vectors.dtype)], axis=1
    )
    blocks = [w_qkv[:, k * half_width : (k + 1) * half_width] for k in range(3)]
    arrived = exchange(jnp.concatenate([blocks[1], small_own], axis=1), swap, sizes)
    head_cols = jnp.where(
        seq_index == 0,
        jnp.concatenate([blocks[0], blocks[2], arrived[:, :half_width]], axis=1),
        jnp.concatenate([arrived[:, :half_width], blocks[0], blocks[2]], axis=1),
    )
    bias_other = arrived[:, half_width + 8 : half_width + 8 + per_row]
    small_cols = jnp.concatenate(
        [
            vectors,
            in_order(seq_index, bias_cols, bias_other, 1),
            jnp.zeros((rows, 128 - 8 - 2 * per_row), vectors.dtype),
        ],
        axis=1,
    )
    x_own = inputs.reshape(piece_len, model_width)
    x_other = exchange(x_own, swap, sizes)
    first = jnp.concatenate([head_cols, small_cols], axis=1)[None]
    a_held = jnp.concatenate([w_out, w_up], axis=1)[None]
    b_held = w_down[None]
    up_cols = w_up.shape[1]
    cut, down_cut = 8 * a_held.shape[2] // 15 // 128 * 128, up_cols // 2
    for hop in far:
        a_held = grow(a_held, hop, sizes)
        first = grow(first, hop, sizes)
    b_held = grow(after(b_held, first), far[0], sizes)
    a_halves = [a_held[:, :, :cut], a_held[:, :, cut:]]
    a_next = [exchange(part, paths[k][len(far)], sizes) for k, part in enumerate(a_halves)]
    first = grow(first, row_hop, sizes)
    b_next = exchange(b_held, far[1], sizes)
    first_parts = [first, exchange(first, core, sizes)]

    bf16, f32 = jnp.bfloat16, jnp.float32
    seq_len, ff = 2 * piece_len, 2 * w_up.shape[1]
    head_width = 3 * half_width
    dense = 2 * piece_len * model_width
    dma = pltpu.SemaphoreType.DMA
    qkv_rows, normed_one, qkv_full, vec_rows = local_call(
        functools.partial(project_kernel, path_dp, rows),
        pair,
        [x_own, x_other],
        first_parts,
        [
            shaped(bf16, seq_len, head_width),
            shaped(bf16, seq_len, model_width),
            shaped(bf16, model_width, head_width),
            shaped(f32, 16, model_width),
        ],
        [],
        [pltpu.VMEM((model_width, 128), bf16), dma((2, sizes["dp"]))],
        2 * dense * head_width,
    )
    bias_row = jnp.transpose(
        vec_rows[8 : 8 + 2 * per_row].reshape(2 * per_row, sizes["dp"], rows), (1, 0, 2)
    ).reshape(1, ff)
    a_halves = [
        jnp.concatenate([a_halves[k], after(a_next[k], qkv_rows)], axis=0) for k in range(2)
    ]
    a_more = [exchange(part, paths[k][len(far) + 1], sizes) for k, part in enumerate(a_halves)]
    b_held = jnp.concatenate([b_held, after(b_next, qkv_rows)], axis=0)
    b_halves = [b_held[:, :, :down_cut], b_held[:, :, down_cut:]]
    b_next = [exchange(part, paths[k][len(far)], sizes) for k, part in enumerate(b_halves)]
    attended, lse = attend(after(qkv_rows, *a_halves, *b_halves))

    def crossed(parts, more):
        pieces = []
        for k in range(2):
            both = (parts[k], more[k])
            pieces += [*both, *[exchange(part, core, sizes) for part in both]]
        return pieces

    def tokens_of(values, index):
        return lax.dynamic_slice_in_dim(values, index * piece_len, piece_len, 0)

    attended_own = tokens_of(attended, seq_index)
    attended_other = exchange(tokens_of(attended, 1 - seq_index), swap, sizes)
    a_parts = crossed(a_halves, [after(part, attended) for part in a_more])
    b_halves = [
        jnp.concatenate([b_halves[k], after(b_next[k], attended)], axis=0) for k in range(2)
    ]
    b_more = [exchange(part, paths[k][len(far) + 1], sizes) for k, part in enumerate(b_halves)]
    mlp_grad = cotangent.reshape(piece_len, model_width)
    slots = sizes["dp"] * sizes["seq"]
    chunk = math.gcd(ff, 512)
    weight_scratch = [
        pltpu.VMEM((model_width, model_width), bf16),
        pltpu.VMEM((model_width, ff), bf16),
    ]
    middle, normed_two, hidden, slope = local_call(
        functools.partial(hidden_kernel, paths, rows, cut, chunk),
        pair,
        [attended_own, attended_other, after(x_own, *b_halves), vec_rows, bias_row],
        a_parts,
        [
            shaped(f32, piece_len, model_width),
            shaped(bf16, piece_len, model_width),
            shaped(bf16, piece_len, ff),
            shaped(bf16, piece_len, ff),
        ],
        [],
        weight_scratch + [dma((3, slots))],
        dense * (model_width + ff),
    )
    b_parts = crossed(b_halves, [after(part, hidden) for part in b_more])
    down_keep, down_send = local_call(
        functools.partial(down_grad_kernel, paths, rows, down_cut, chunk),
        pair,
        [hidden, mlp_grad],
        [],
        [],
        [shaped(bf16, slots // 2, rows, ff // 2)] * 2,
        [
            pltpu.VMEM((model_width, ff), bf16),
            pltpu.VMEM((model_width, piece_len), bf16),
            dma((2, slots)),
        ],
        dense * ff,
    )

    down_other = exchange(down_send, core, sizes)
    up_grad, norm_two_grad, bias_sums = local_call(
        functools.partial(mlp_back_kernel, paths, rows, cut, down_cut, chunk),
        pair,
        [slope, after(mlp_grad, down_keep)],
        a_parts + b_parts,
        [
            shaped(bf16, piece_len, ff),
            shaped(f32, piece_len, model_width),
            shaped(f32, 8, ff),
        ],
        [],
        weight_scratch + [pltpu.VMEM((model_width, ff), bf16), dma((3, slots)), dma((2, slots))],
        2 * dense * ff,
    )
    down_keeps, down_sends = [None] * 2, [None] * 2
    down_keeps[0], down_sends[0], down_keeps[1], down_sends[1] = quarters(
        down_keep, after(down_other, norm_two_grad), down_cut
    )
    down_others = [exchange(down_sends[k], (swap, row_hop)[1 - k], sizes) for k in range(2)]
    middle_grad, attn_out_grad, grads_own, grads_send, sums = local_call(
        functools.partial(middle_back_kernel, paths, rows, w_out.shape[1]),
        pair,
        [after(norm_two_grad, *down_keeps), middle, mlp_grad, vec_rows],
        a_parts[:4],
        [
            shaped(f32, piece_len, model_width),
            shaped(bf16, piece_len, model_width),
            shaped(bf16, piece_len, half_width),
            shaped(bf16, piece_len, half_width),
            shaped(f32, 8, model_width),
        ],
        [],
        [weight_scratch[0], dma((1, slots))],
        dense * model_width,
    )
    grads_other = exchange(grads_send, swap, sizes)
    back_cut = 8 * (up_cols + w_out.shape[1]) // 15 // 128 * 128
    up_keep, up_send = local_call(
        functools.partial(up_grad_kernel, paths, rows, back_cut, chunk),
        pair,
        [normed_two, up_grad, attended_own, attended_other, attn_out_grad],
        [],
        [],
        [shaped(bf16, slots // 2, rows, (ff + model_width) // 2)] * 2,
        [
            pltpu.VMEM((model_width, ff), bf16),
            pltpu.VMEM((model_width, model_width), bf16),
            pltpu.VMEM((model_width, piece_len), bf16),
            dma((3, slots)),
        ],
        dense * (model_width + ff),
    )
    up_other = exchange(up_send, core, sizes)
    grad_heads = in_order(seq_index, grads_own, after(grads_other, up_keep), 0)
    down_others = [after(part, up_keep) for part in down_others]
    down_sums = halves([(down_keeps[k], down_others[k]) for k in range(2)])
    down_keeps, down_sends = down_sums[0::2], down_sums[1::2]
    down_others = [exchange(down_sends[k], (swap, row_hop)[k], sizes) for k in range(2)]

    def head_pair_back(at, *earlier):
        return attend_back(qkv_rows, grad_heads, attended, lse, at)

    pair_grads = [head_pair_back(0)]
    up_keeps, up_sends = [None] * 2, [None] * 2
    up_keeps[0], up_sends[0], up_keeps[1], up_sends[1] = quarters(
        up_keep, after(up_other, pair_grads[0][0]), back_cut
    )
    down_keep, down_send = rejoin(
        [(down_keeps[k], after(down_others[k], pair_grads[0][0])) for k in range(2)]
    )
    if True:
        up_others = [exchange(up_sends[k], (swap, row_hop)[1 - k], sizes) for k in range(2)]
        down_other = exchange(down_send, far[1], sizes)
        pair_grads += [head_pair_back(at) for at in range(1, half_width // 128)]
    down_keep, down_send = halves([(down_keep, down_other)])
    down_other = exchange(down_send, far[0], sizes)
    bias_rows = jnp.transpose(
        bias_sums[0].reshape(sizes["dp"], 2 * per_row, rows), (1, 0, 2)
    ).reshape(2 * per_row, model_width)
    da_own, da_send, last_keep, last_send = local_call(
        functools.partial(project_back_kernel, path_dp, rows, half_width // 128),
        pair,
        [
            *[grad for group in pair_grads for grad in group],
            qkv_full,
            normed_one,
            x_own,
            x_other,
            vec_rows,
            sums,
            bias_rows,
        ],
        [],
        [shaped(f32, piece_len, model_width), shaped(bf16, piece_len, model_width)],
        [shaped(bf16, sizes["dp"] // 2, rows, head_width + 128)] * 2,
        [
            pltpu.VMEM((seq_len, head_width), bf16),
            pltpu.VMEM((model_width, head_width + 128), bf16),
            pltpu.VMEM((2, piece_len, model_width), f32),
            pltpu.VMEM((128, model_width), f32),
            pltpu.VMEM((model_width, seq_len), bf16),
            dma((1, sizes["dp"])),
        ],
        4 * dense * head_width,
    )
    last_other = exchange(last_send, core, sizes)
    up_sums = halves([(up_keeps[k], after(up_others[k], da_own)) for k in range(2)])
    up_keeps, up_sends = up_sums[0::2], up_sums[1::2]
    up_others = [exchange(up_sends[k], (swap, row_hop)[k], sizes) for k in range(2)]
    da_other = exchange(da_send, swap, sizes)
    last_keep, last_send = halves([(last_keep, last_other)])
    last_other = exchange(last_send, row_hop, sizes)
    up_keep, up_send = rejoin([(up_keeps[k], after(up_others[k], last_send)) for k in range(2)])
    up_other = exchange(up_send, far[1], sizes)
    grad_down = down_keep[0].astype(f32) + after(down_other, last_send)[0].astype(f32)
    (result,) = local_call(
        functools.partial(result_kernel, paths, rows, down_cut),
        pair,
        [hidden, after(middle, last_send, up_send), vec_rows],
        b_parts,
        [shaped(bf16, piece_len, model_width)],
        [],
        [pltpu.VMEM((model_width, ff), bf16), dma((2, slots))],
        dense * ff,
    )
    last_keep, last_send = halves([(last_keep, after(last_other, result))])
    last_other = exchange(last_send, far[1], sizes)
    up_keep, up_send = halves([(up_keep, after(up_other, last_send))])
    up_other = exchange(up_send, far[0], sizes)
    norm_one_own = da_own + after(da_other, last_send).astype(f32)
    unit, inverse = normed(x_own.astype(f32))
    input_grad = middle_grad + normed_back(norm_one_own, unit, inverse, vec_rows[0:1])
    last_keep, last_send = halves([(last_keep, after(last_other, input_grad))])
    last_other = exchange(last_send, far[0], sizes)
    up_other = after(up_other, last_send)
    grad_up_out = up_keep[0].astype(f32) + up_other[0].astype(f32)
    grad_up, grad_out = grad_up_out[:, :up_cols], grad_up_out[:, up_cols:]
    last = last_keep[0].astype(f32) + last_other[0].astype(f32)
    small_last = last[:, 3 * half_width :]
    sent = jnp.where(
        seq_index == 0, last[:, 2 * half_width :],
        jnp.concatenate([last[:, :half_width], small_last], axis=1)
    )
    arrived_last = exchange(sent.astype(jnp.bfloat16), swap, sizes).astype(jnp.float32)
    middle_block = arrived_last[:, :half_width]
    kept = jnp.where(seq_index == 0, last[:, : 2 * half_width], last[:, half_width : 3 * half_width])
    grad_qkv = jnp.concatenate([kept[:, :half_width], middle_block, kept[:, half_width:]], axis=1)
    small_sum = small_last + arrived_last[:, half_width:]
    grad_vectors = small_sum[:, :8]
    bias_own = lax.dynamic_slice_in_dim(small_sum, 8 + seq_index * per_row, per_row, 1)
    grad_up_bias = bias_own.T.reshape(-1)
    return (
        result.reshape(1, piece_len, model_width),
        input_grad.reshape(1, piece_len, model_width),
        grad_qkv,
        grad_out,
        grad_up,
        grad_down,
        grad_up_bias,
        grad_vectors,
    )


def block(*arrays):
    n_dp, n_seq = lax.axis_size("dp"), lax.axis_size("seq")
    rows = arrays[2].shape[0]
    whole_tiles = rows % 16 == 0 and all(weight.shape[1] % 384 == 0 for weight in arrays[2:6])
    powers = n_dp == 16
    if n_seq == 2 and powers and whole_tiles and arrays[0].shape[0] == 1:
        return on_device(*arrays)
    return on_device_general(*arrays)


def solution(mesh):
    placed = (
        P("dp", "seq", None),
        P("dp", None),
        P("dp", "seq"),
        P("dp", "seq"),
        P("dp", "seq"),
        P("dp", "seq"),
        P(("dp", "seq")),
        P("dp", "seq", None),
    )
    return jax.shard_map(
        block,
        mesh=mesh,
        in_specs=placed,
        out_specs=(
            P("dp", "seq", None),
            P("dp", "seq", None),
            P("dp", "seq"),
            P("dp", "seq"),
            P("dp", "seq"),
            P("dp", "seq"),
            P(("dp", "seq")),
            P("dp", None),
        ),
        check_vma=False,
    )
```

```python
import functools
import math

import jax
import jax.numpy as jnp
from jax import lax
from jax.experimental import pallas as pl
from jax.experimental.pallas import tpu as pltpu
from jax.sharding import PartitionSpec as P

HEADS = 12
HEAD_DIM = 64
VMEM_LIMIT = 28 * 1024 * 1024
COST = pl.CostEstimate(flops=10**11, bytes_accessed=10**7, transcendentals=0)


EPSILON = 1e-05
MASKED = -1e30


def norm_rows(values, scale_row, shift_row):
    row_mean = jnp.mean(values, axis=-1, keepdims=True)
    centered = values - row_mean
    variance = jnp.mean(centered * centered, axis=-1, keepdims=True)
    return centered * lax.rsqrt(variance + EPSILON) * scale_row + shift_row


def gelu_tanh(values):
    return (
        0.5
        * values
        * (1.0 + jnp.tanh(0.7978845608028654 * (values + 0.044715 * values * values * values)))
    )


def contract_last(left_side, right_side):
    return lax.dot_general(
        left_side, right_side, (((1,), (1,)), ((), ())), preferred_element_type=jnp.float32
    )


def contract_first(left_side, right_side):
    return lax.dot_general(
        left_side, right_side, (((0,), (0,)), ((), ())), preferred_element_type=jnp.float32
    )


def on_device_general(inputs, vectors, w_qkv, w_out, w_up, w_down, up_bias, cotangent):
    seq_count, piece_len, model_width = inputs.shape
    row_count = seq_count * piece_len
    score_scale = HEAD_DIM ** (-0.5)
    seq_index = lax.axis_index("seq")
    query_pos = seq_index * piece_len + jnp.arange(piece_len)
    qkv_cols, out_cols, up_cols, down_cols, upb_cols = (
        lax.all_gather(w_qkv, "seq", axis=1, tiled=True),
        lax.all_gather(w_out, "seq", axis=1, tiled=True),
        lax.all_gather(w_up, "seq", axis=1, tiled=True),
        lax.all_gather(w_down, "seq", axis=1, tiled=True),
        lax.all_gather(up_bias, "seq", axis=0, tiled=True),
    )
    full_fwd = (
        lax.all_gather(qkv_cols, "dp", axis=0, tiled=True),
        lax.all_gather(out_cols, "dp", axis=0, tiled=True),
        lax.all_gather(up_cols, "dp", axis=0, tiled=True),
        lax.all_gather(down_cols, "dp", axis=0, tiled=True),
        lax.all_gather(upb_cols, "dp", axis=0, tiled=True),
        lax.all_gather(vectors, "dp", axis=0, tiled=True),
    )
    qkv_full, out_full, up_full, down_full, upb_full, vec_full = full_fwd
    vec_values = vec_full.astype(jnp.float32)
    resid_in = inputs.reshape(row_count, model_width).astype(jnp.float32)
    normed_one = norm_rows(resid_in, vec_values[:, 0], vec_values[:, 1]).astype(jnp.bfloat16)
    qkv_bias = jnp.concatenate(
        [vec_values[:, 2], jnp.zeros_like(vec_values[:, 2]), vec_values[:, 3]]
    )
    qkv_rows = (
        jnp.dot(normed_one, qkv_full, preferred_element_type=jnp.float32) + qkv_bias
    ).astype(jnp.bfloat16)
    queries = qkv_rows[:, :model_width].reshape(seq_count, piece_len, HEADS, HEAD_DIM)
    key_vals = qkv_rows[:, model_width:].reshape(seq_count, piece_len, 2 * model_width)

    def block_scores(key_block, first_row):
        key_rows = key_block.shape[1]
        keys_part = key_block[..., :model_width].reshape(seq_count, key_rows, HEADS, HEAD_DIM)
        scores = (
            jnp.einsum("bqhd,bkhd->bhqk", queries, keys_part, preferred_element_type=jnp.float32)
            * score_scale
        )
        causal = (first_row + jnp.arange(key_rows))[None, :] <= query_pos[:, None]
        return jnp.where(causal, scores, MASKED)

    key_block = lax.all_gather(key_vals, "seq", axis=1, tiled=True)
    run_max = jnp.full((seq_count, HEADS, piece_len), MASKED, jnp.float32)
    key_rows = key_block.shape[1]
    values_part = key_block[..., model_width:].reshape(seq_count, key_rows, HEADS, HEAD_DIM)
    scores = block_scores(key_block, jnp.int32(0))
    new_max = jnp.maximum(run_max, jnp.max(scores, axis=-1))
    exp_scores = jnp.exp(scores - new_max[..., None])
    run_total = jnp.sum(exp_scores, axis=-1)
    added_part = jnp.einsum(
        "bhqk,bkhd->bqhd",
        exp_scores.astype(jnp.bfloat16),
        values_part,
        preferred_element_type=jnp.float32,
    )
    run_acc = added_part
    run_max, run_total, run_acc = (new_max, run_total, run_acc)
    attended = run_acc / jnp.transpose(run_total, (0, 2, 1))[..., None]
    log_total = run_max + jnp.log(run_total)
    attended_lo = attended.reshape(row_count, model_width).astype(jnp.bfloat16)
    branch_attn = (
        jnp.dot(attended_lo, out_full, preferred_element_type=jnp.float32) + vec_values[:, 4]
    )
    middle = resid_in + branch_attn
    normed_two = norm_rows(middle, vec_values[:, 5], vec_values[:, 6]).astype(jnp.bfloat16)
    up_act = jnp.dot(normed_two, up_full, preferred_element_type=jnp.float32) + upb_full.astype(
        jnp.float32
    )
    hidden = gelu_tanh(up_act).astype(jnp.bfloat16)
    branch_mlp = contract_last(hidden, down_full) + vec_values[:, 7]
    result = middle + branch_mlp
    qkv_back, out_back, up_back, down_back = (qkv_full, out_full, up_full, down_full)
    out_grad = cotangent.reshape(row_count, model_width).astype(jnp.float32)
    mlp_grad = out_grad.astype(jnp.bfloat16)
    hidden_grad = jnp.dot(mlp_grad, down_back, preferred_element_type=jnp.float32)
    gelu_pull = jax.vjp(gelu_tanh, up_act)[1]
    up_grad = gelu_pull(hidden_grad)[0].astype(jnp.bfloat16)
    norm_two_grad = contract_last(up_grad, up_back)
    ln_two_pull = jax.vjp(norm_rows, middle, vec_values[:, 5], vec_values[:, 6])[1]
    middle_part, scale_two, shift_two = ln_two_pull(norm_two_grad)
    middle_grad = out_grad + middle_part
    attn_out_grad = middle_grad.astype(jnp.bfloat16)
    attended_grad = contract_last(attn_out_grad, out_back).astype(jnp.bfloat16)
    grad_heads = attended_grad.reshape(seq_count, piece_len, HEADS, HEAD_DIM)
    row_delta = jnp.transpose(
        jnp.sum(grad_heads.astype(jnp.float32) * attended, axis=-1), (0, 2, 1)
    )
    key_vals_all = lax.all_gather(key_vals, "seq", axis=1, tiled=True)
    total_len = key_vals_all.shape[1]
    key_block_len = math.gcd(total_len, 512)

    def back_step(query_acc, block_index):
        first_row = block_index * key_block_len
        key_block = lax.dynamic_slice_in_dim(key_vals_all, first_row, key_block_len, 1)
        keys_part = key_block[..., :model_width].reshape(seq_count, key_block_len, HEADS, HEAD_DIM)
        values_part = key_block[..., model_width:].reshape(
            seq_count, key_block_len, HEADS, HEAD_DIM
        )
        scores = block_scores(key_block, first_row)
        attn_probs = jnp.exp(scores - log_total[..., None])
        prob_grad = jnp.einsum(
            "bqhd,bkhd->bhqk", grad_heads, values_part, preferred_element_type=jnp.float32
        )
        score_grad = (attn_probs * (prob_grad - row_delta[..., None])).astype(jnp.bfloat16)
        step_part = jnp.einsum(
            "bhqk,bkhd->bqhd", score_grad, keys_part, preferred_element_type=jnp.float32
        )
        key_grad = (
            jnp.einsum("bhqk,bqhd->bkhd", score_grad, queries, preferred_element_type=jnp.float32)
            * score_scale
        )
        value_grad = jnp.einsum(
            "bhqk,bqhd->bkhd",
            attn_probs.astype(jnp.bfloat16),
            grad_heads,
            preferred_element_type=jnp.float32,
        )
        key_value = jnp.concatenate(
            [
                key_grad.reshape(seq_count, key_block_len, model_width),
                value_grad.reshape(seq_count, key_block_len, model_width),
            ],
            axis=-1,
        )
        return (query_acc + step_part * score_scale, key_value)

    query_grad, kv_blocks = lax.scan(
        back_step,
        jnp.zeros((seq_count, piece_len, HEADS, HEAD_DIM), jnp.float32),
        jnp.arange(total_len // key_block_len),
    )
    kv_terms = jnp.moveaxis(kv_blocks, 0, 1).reshape(seq_count, total_len, 2 * model_width)
    key_val_grad = lax.psum_scatter(
        kv_terms.astype(jnp.bfloat16), "seq", scatter_dimension=1, tiled=True
    ).astype(jnp.float32)
    key_val_grad = key_val_grad.reshape(row_count, 2 * model_width)
    qkv_grad = jnp.concatenate(
        [query_grad.reshape(row_count, model_width), key_val_grad], axis=1
    ).astype(jnp.bfloat16)
    norm_one_grad = contract_last(qkv_grad, qkv_back)
    ln_one_pull = jax.vjp(norm_rows, resid_in, vec_values[:, 0], vec_values[:, 1])[1]
    input_part, scale_one, shift_one = ln_one_pull(norm_one_grad)
    input_grad = middle_grad + input_part
    whole_qkv = contract_first(normed_one, qkv_grad)
    whole_out = contract_first(attended_lo, attn_out_grad)
    whole_up = contract_first(normed_two, up_grad)
    whole_down = contract_first(mlp_grad, hidden)
    row_qkv, row_out, row_up, row_down = (
        lax.psum_scatter(
            whole_qkv.astype(jnp.bfloat16), "dp", scatter_dimension=0, tiled=True
        ).astype(jnp.float32),
        lax.psum_scatter(
            whole_out.astype(jnp.bfloat16), "dp", scatter_dimension=0, tiled=True
        ).astype(jnp.float32),
        lax.psum_scatter(
            whole_up.astype(jnp.bfloat16), "dp", scatter_dimension=0, tiled=True
        ).astype(jnp.float32),
        lax.psum_scatter(
            whole_down.astype(jnp.bfloat16), "dp", scatter_dimension=0, tiled=True
        ).astype(jnp.float32),
    )
    grad_qkv, grad_out, grad_up, grad_down = (
        lax.psum_scatter(
            row_qkv.astype(jnp.bfloat16), "seq", scatter_dimension=1, tiled=True
        ).astype(jnp.float32),
        lax.psum_scatter(
            row_out.astype(jnp.bfloat16), "seq", scatter_dimension=1, tiled=True
        ).astype(jnp.float32),
        lax.psum_scatter(
            row_up.astype(jnp.bfloat16), "seq", scatter_dimension=1, tiled=True
        ).astype(jnp.float32),
        lax.psum_scatter(
            row_down.astype(jnp.bfloat16), "seq", scatter_dimension=1, tiled=True
        ).astype(jnp.float32),
    )
    vec_term = jnp.stack(
        [
            scale_one,
            shift_one,
            jnp.sum(qkv_grad[:, :model_width].astype(jnp.float32), axis=0),
            jnp.sum(qkv_grad[:, 2 * model_width :].astype(jnp.float32), axis=0),
            jnp.sum(attn_out_grad.astype(jnp.float32), axis=0),
            scale_two,
            shift_two,
            jnp.sum(mlp_grad.astype(jnp.float32), axis=0),
        ],
        axis=1,
    )
    upb_term = jnp.sum(up_grad.astype(jnp.float32), axis=0)
    vec_sum, upb_sum = lax.psum((vec_term, upb_term), ("dp", "seq"))
    vec_rows = vectors.shape[0]
    grad_vectors = lax.dynamic_slice_in_dim(vec_sum, lax.axis_index("dp") * vec_rows, vec_rows, 0)
    upb_rows = up_bias.shape[0]
    upb_start = (lax.axis_index("dp") * lax.axis_size("seq") + seq_index) * upb_rows
    grad_up_bias = lax.dynamic_slice_in_dim(upb_sum, upb_start, upb_rows, 0)
    return (
        result.reshape(seq_count, piece_len, model_width).astype(jnp.bfloat16),
        input_grad.reshape(seq_count, piece_len, model_width),
        grad_qkv,
        grad_out,
        grad_up,
        grad_down,
        grad_up_bias,
        grad_vectors,
    )


def bit_masks(count):
    return [1 << k for k in range(count.bit_length() - 1)]


def exchange(values, hop, sizes):
    axis, mask = hop
    return lax.ppermute(values, axis, [(i, i ^ mask) for i in range(sizes[axis])])


def slot_owner(slot, path):
    offset = {"dp": 0, "seq": 0}
    for k, (axis, mask) in enumerate(path):
        if slot >> k & 1:
            offset[axis] ^= mask
    return offset["dp"], offset["seq"]


def after(values, *earlier):
    return lax.optimization_barrier((values, *earlier))[0]


def grow(held, hop, sizes):
    return jnp.concatenate([held, exchange(held, hop, sizes)], axis=0)


def start_place(path, rows, parts, me_ref, targets, sems):
    total = 1 << len(path)
    each = total // len(parts)
    copies = []
    for k, (target, first, cols, stride, at) in enumerate(targets):
        for slot in range(total):
            off_dp, off_seq = slot_owner(slot, path)
            row = pl.multiple_of((me_ref[0] ^ off_dp) * rows, 16)
            col = pl.multiple_of((me_ref[1] ^ off_seq) * stride + at, 128)
            src = parts[slot // each].at[slot % each, :, pl.ds(first, cols)]
            dst = target.at[pl.ds(row, rows), pl.ds(col, cols)]
            copy = pltpu.make_async_copy(src, dst, sems.at[k, slot])
            copy.start()
            copies.append(copy)
    return copies


def start_split(rows, me_ref, pieces, keep_ref, send_ref, sems):
    copies = []
    for k, (path, whole, stride, first, cols, at) in enumerate(pieces):
        half = 1 << (len(path) - 1)
        for slot in range(2 * half):
            off_dp, off_seq = slot_owner(slot, path)
            row = pl.multiple_of((me_ref[0] ^ off_dp) * rows, 16)
            col = pl.multiple_of((me_ref[1] ^ off_seq) * stride + first, 128)
            target = keep_ref if slot < half else send_ref
            copy = pltpu.make_async_copy(
                whole.at[pl.ds(row, rows), pl.ds(col, cols)],
                target.at[slot % half, :, pl.ds(at, cols)],
                sems.at[k, slot],
            )
            copy.start()
            copies.append(copy)
    return copies


def wait_all(copies):
    for copy in copies:
        copy.wait()


def normed(values):
    centered = values - jnp.mean(values, axis=-1, keepdims=True)
    inverse = lax.rsqrt(jnp.mean(centered * centered, axis=-1, keepdims=True) + EPSILON)
    return centered * inverse, inverse


def normed_back(grads, unit, inverse, scale_row):
    scaled = grads * scale_row
    mean_one = jnp.mean(scaled, axis=-1, keepdims=True)
    mean_two = jnp.mean(scaled * unit, axis=-1, keepdims=True)
    return inverse * (scaled - mean_one - unit * mean_two)


def dot(left_side, right_side):
    return jnp.dot(left_side, right_side, preferred_element_type=jnp.float32)


def column_sum(values):
    return jnp.sum(values.astype(jnp.float32), axis=0, keepdims=True)


def project_kernel(path, rows, me_ref, own_ref, other_ref, *refs):
    parts = refs[:2]
    qkv_ref, a_ref, w_ref, vec_ref, small, sems = refs[2:]
    seq = me_ref[1]
    piece, width = own_ref.shape
    third = w_ref.shape[1] // 3
    copies = start_place(
        path,
        rows,
        parts,
        me_ref,
        [(small, 3 * third, 128, 0, 0), (w_ref, 0, 3 * third, 0, 0)],
        sems,
    )
    units = []
    for part in range(2):
        values = jnp.where(seq == part, own_ref[...], other_ref[...]).astype(jnp.float32)
        units.append(normed(values)[0])
    wait_all(copies[: len(copies) // 2])
    vec_ref[...] = small[...].astype(jnp.float32).T[: vec_ref.shape[0]]
    for part in range(2):
        a_ref[part * piece : (part + 1) * piece, :] = (
            units[part] * vec_ref[0:1, :] + vec_ref[1:2, :]
        ).astype(jnp.bfloat16)
    wait_all(copies[len(copies) // 2 :])
    own_cols = pl.ds(pl.multiple_of(seq * third, 128), third)
    for k in range(3):
        cols = slice(k * third, (k + 1) * third)
        for part in range(2):
            at = slice(part * piece, (part + 1) * piece)
            product = dot(a_ref[at, :], w_ref[:, cols])
            if k != 1:
                product = product + vec_ref[2 + k // 2 : 3 + k // 2, own_cols]
            qkv_ref[at, cols] = product.astype(jnp.bfloat16)


def in_vmem(count):
    return [pl.BlockSpec(memory_space=pltpu.VMEM)] * count


def in_any(count):
    return [pl.BlockSpec(memory_space=pl.ANY)] * count


def shaped(dtype, *shape):
    return jax.ShapeDtypeStruct(shape, dtype)


def local_call(kernel, pair, vmem_args, any_args, vmem_outs, any_outs, scratch, flops):
    outs = list(vmem_outs) + list(any_outs)
    moved = sum(a.size * a.dtype.itemsize for a in [*vmem_args, *any_args, *outs])
    return pl.pallas_call(
        kernel,
        out_shape=outs,
        in_specs=[pl.BlockSpec(memory_space=pltpu.SMEM)]
        + in_vmem(len(vmem_args))
        + in_any(len(any_args)),
        out_specs=in_vmem(len(vmem_outs)) + in_any(len(any_outs)),
        scratch_shapes=scratch,
        compiler_params=pltpu.CompilerParams(vmem_limit_bytes=VMEM_LIMIT),
        cost_estimate=COST,
    )(pair, *vmem_args, *any_args)


def gelu_both(values):
    square = values * values
    angle = jnp.tanh(0.7978845608028654 * values * (1.0 + 0.044715 * square))
    half = 0.5 * (1.0 + angle)
    slope = half + 0.5 * values * (1.0 - angle * angle) * (
        0.7978845608028654 * (1.0 + 3.0 * 0.044715 * square)
    )
    return values * half, slope


def place_up(paths, rows, cut, out_cols, parts, me_ref, w_up, sems):
    up_cols = w_up.shape[1] // 2
    left = cut - out_cols
    return start_place(
        paths[0], rows, parts[:4], me_ref, [(w_up, out_cols, left, up_cols, 0)], sems
    ) + start_place(
        paths[1], rows, parts[4:], me_ref, [(w_up, 0, up_cols - left, up_cols, left)], sems.at[1:2]
    )


def place_down(paths, rows, cut, parts, me_ref, w_down, sems):
    cols = w_down.shape[1] // 2
    return start_place(
        paths[0], rows, parts[:4], me_ref, [(w_down, 0, cut, cols, 0)], sems
    ) + start_place(
        paths[1], rows, parts[4:], me_ref, [(w_down, 0, cols - cut, cols, cut)], sems.at[1:2]
    )


def hidden_kernel(paths, rows, cut, chunk, me_ref, *refs):
    mine_ref, other_ref, x_ref, vec_ref, bias_ref = refs[:5]
    parts = refs[5:13]
    h_ref, a_ref, g_ref, slope_ref = refs[13:17]
    w_out, w_up, sems = refs[17:]
    left_first = me_ref[1] == 0
    half = mine_ref.shape[1]
    out_cols = w_out.shape[1] // 2
    out_copies = start_place(
        paths[0], rows, parts[:4], me_ref, [(w_out, 0, out_cols, out_cols, 0)], sems
    )
    up_copies = place_up(paths, rows, cut, out_cols, parts, me_ref, w_up, sems.at[1:3])
    left = jnp.where(left_first, mine_ref[...], other_ref[...])
    right = jnp.where(left_first, other_ref[...], mine_ref[...])
    wait_all(out_copies)
    branch = dot(left, w_out[:half, :]) + dot(right, w_out[half:, :]) + vec_ref[4:5, :]
    middle = x_ref[...].astype(jnp.float32) + branch
    h_ref[...] = middle
    a_ref[...] = (normed(middle)[0] * vec_ref[5:6, :] + vec_ref[6:7, :]).astype(jnp.bfloat16)
    wait_all(up_copies)

    def step(k, carry):
        cols = pl.ds(pl.multiple_of(k * chunk, chunk), chunk)
        act = dot(a_ref[...], w_up[:, cols]) + bias_ref[:, cols]
        value, slope = gelu_both(act)
        g_ref[:, cols] = value.astype(jnp.bfloat16)
        slope_ref[:, cols] = slope.astype(jnp.bfloat16)
        return carry

    lax.fori_loop(0, w_up.shape[1] // chunk, step, 0)


def down_grad_kernel(paths, rows, cut, chunk, me_ref, *refs):
    g_ref, dy_ref, keep_ref, send_ref, grad, dy_t, sems = refs
    dy_t[...] = dy_ref[...].T

    def step(k, carry):
        cols = pl.ds(pl.multiple_of(k * chunk, chunk), chunk)
        grad[:, cols] = dot(dy_t[...], g_ref[:, cols]).astype(jnp.bfloat16)
        return carry

    lax.fori_loop(0, grad.shape[1] // chunk, step, 0)
    cols = grad.shape[1] // 2
    pieces = [
        (paths[0], grad, cols, 0, cut, 0),
        (paths[1], grad, cols, cut, cols - cut, cut),
    ]
    wait_all(start_split(rows, me_ref, pieces, keep_ref, send_ref, sems))


def mlp_back_kernel(paths, rows, cut, down_cut, out_cols, chunk, me_ref, *refs):
    slope_ref, dy_ref = refs[:2]
    parts, down_parts = refs[2:10], refs[10:18]
    du_ref, acc, bias_sum_ref = refs[18:21]
    w_up, w_down, sems, down_sems = refs[21:]
    down_copies = place_down(paths, rows, down_cut, down_parts, me_ref, w_down, down_sems)
    up_copies = place_up(paths, rows, cut, out_cols, parts, me_ref, w_up, sems)
    acc[...] = jnp.zeros_like(acc)
    wait_all(down_copies)
    wait_all(up_copies)

    def step(k, carry):
        cols = pl.ds(pl.multiple_of(k * chunk, chunk), chunk)
        up_grad = (
            dot(dy_ref[...], w_down[:, cols]) * slope_ref[:, cols].astype(jnp.float32)
        ).astype(jnp.bfloat16)
        du_ref[:, cols] = up_grad
        bias_sum_ref[0:1, cols] = column_sum(up_grad)
        acc[...] += contract_last(up_grad, w_up[:, cols])
        return carry

    lax.fori_loop(0, w_up.shape[1] // chunk, step, 0)


def middle_back_kernel(paths, rows, out_cols, me_ref, *refs):
    acc_ref, h_ref, dy_ref, vec_ref = refs[:4]
    parts = refs[4:8]
    dh_ref, dz_ref, do_keep_ref, do_send_ref, sum_ref = refs[8:13]
    w_out, sems = refs[13:]
    left_first = me_ref[1] == 0
    copies = start_place(
        paths[0], rows, parts, me_ref, [(w_out, 0, out_cols, out_cols, 0)], sems
    )
    out_grad = dy_ref[...].astype(jnp.float32)
    unit, inverse = normed(h_ref[...])
    grads = acc_ref[...]
    middle_grad = out_grad + normed_back(grads, unit, inverse, vec_ref[5:6, :])
    dh_ref[...] = middle_grad
    attn_grad = middle_grad.astype(jnp.bfloat16)
    dz_ref[...] = attn_grad
    wait_all(copies)
    half = do_keep_ref.shape[1]
    left = contract_last(attn_grad, w_out[:half, :])
    right = contract_last(attn_grad, w_out[half:, :])
    do_keep_ref[...] = jnp.where(left_first, left, right).astype(jnp.bfloat16)
    do_send_ref[...] = jnp.where(left_first, right, left).astype(jnp.bfloat16)
    sum_ref[...] = jnp.concatenate(
        [
            column_sum(attn_grad),
            column_sum(grads * unit),
            column_sum(grads),
            column_sum(out_grad),
            jnp.zeros((4, out_grad.shape[1]), jnp.float32),
        ],
        axis=0,
    )


def result_kernel(paths, rows, down_cut, me_ref, *refs):
    g_ref, h_ref, vec_ref = refs[:3]
    parts = refs[3:11]
    res_ref, w_down, sems = refs[11:]
    wait_all(place_down(paths, rows, down_cut, parts, me_ref, w_down, sems))
    for first in range(0, w_down.shape[0], 256):
        cols = slice(first, first + 256)
        res_ref[:, cols] = (
            h_ref[:, cols] + contract_last(g_ref[...], w_down[cols, :]) + vec_ref[7:8, cols]
        ).astype(jnp.bfloat16)


def up_grad_kernel(paths, rows, cut, chunk, me_ref, *refs):
    a_ref, du_ref, mine_ref, other_ref, dz_ref, keep_ref, send_ref = refs[:7]
    grad_up, grad_out, left_t, sems = refs[7:]
    left_first = me_ref[1] == 0
    half = mine_ref.shape[1]
    left_t[...] = a_ref[...].T

    def step(k, carry):
        cols = pl.ds(pl.multiple_of(k * chunk, chunk), chunk)
        grad_up[:, cols] = dot(left_t[...], du_ref[:, cols]).astype(jnp.bfloat16)
        return carry

    lax.fori_loop(0, du_ref.shape[1] // chunk, step, 0)
    left = jnp.where(left_first, mine_ref[...], other_ref[...])
    right = jnp.where(left_first, other_ref[...], mine_ref[...])
    grad_out[:half, :] = contract_first(left, dz_ref[...]).astype(jnp.bfloat16)
    grad_out[half:, :] = contract_first(right, dz_ref[...]).astype(jnp.bfloat16)
    up_cols, out_cols = grad_up.shape[1] // 2, grad_out.shape[1] // 2
    pieces = [
        (paths[0], grad_up, up_cols, 0, cut, 0),
        (paths[1], grad_up, up_cols, cut, up_cols - cut, cut),
        (paths[1], grad_out, out_cols, 0, out_cols, up_cols),
    ]
    wait_all(start_split(rows, me_ref, pieces, keep_ref, send_ref, sems))


def project_back_kernel(path, rows, pairs, me_ref, *refs):
    grad_refs = refs[: 3 * pairs]
    w_ref, a_ref, own_ref, other_ref, vec_ref, sum_ref, bias_ref = refs[3 * pairs : 3 * pairs + 7]
    da_own_ref, da_send_ref, keep_ref, send_ref = refs[3 * pairs + 7 : 3 * pairs + 11]
    grads_all, grad, parts, small, a_t, sems = refs[3 * pairs + 11 :]
    seq = me_ref[1]
    piece = own_ref.shape[0]
    third = grads_all.shape[1] // 3
    small[...] = jnp.zeros_like(small)
    a_t[...] = a_ref[...].T
    for k in range(3):
        for pair in range(pairs):
            at = k * third + pair * 128
            grads_all[:, at : at + 128] = grad_refs[3 * pair + k][...]
        cols = slice(k * third, (k + 1) * third)
        grad[:, cols] = dot(a_t[...], grads_all[:, cols]).astype(jnp.bfloat16)
    for part in range(2):
        at = slice(part * piece, (part + 1) * piece)
        grads = contract_last(grads_all[at, :], w_ref[...])
        parts[part] = grads
        values = jnp.where(seq == part, own_ref[...], other_ref[...]).astype(jnp.float32)
        small[0:1, :] += column_sum(grads * normed(values)[0])
        small[1:2, :] += column_sum(grads)
    da_own_ref[...] = parts[seq]
    da_send_ref[...] = parts[1 - seq].astype(jnp.bfloat16)
    own_cols = pl.ds(pl.multiple_of(seq * third, 128), third)
    small[2:3, own_cols] = column_sum(grads_all[:, :third])
    small[3:4, own_cols] = column_sum(grads_all[:, 2 * third :])
    small[4:8, :] = sum_ref[0:4, :]
    bias_rows = bias_ref.shape[0]
    small[8 : 8 + bias_rows, :] = bias_ref[...]
    grad[:, 3 * third :] = small[...].T.astype(jnp.bfloat16)
    pieces = [(path, grad, 0, 0, grad.shape[1], 0)]
    wait_all(start_split(rows, me_ref, pieces, keep_ref, send_ref, sems))


def add_kernel(cuts, count, *refs):
    ins, outs = refs[: 2 * count], refs[2 * count :]
    for pair, first, last, left, right, out, at in cuts:
        keep, other = ins[2 * pair], ins[2 * pair + 1]
        total = keep[first:last, :, left:right].astype(jnp.float32) + other[
            first:last, :, left:right
        ].astype(jnp.float32)
        outs[out][:, :, at : at + right - left] = total.astype(outs[out].dtype)


def add_pairs(pairs, cuts, shapes):
    ins = [array for pair in pairs for array in pair]
    return pl.pallas_call(
        functools.partial(add_kernel, cuts, len(pairs)),
        out_shape=[jax.ShapeDtypeStruct(shape, jnp.bfloat16) for shape in shapes],
        in_specs=in_vmem(len(ins)),
        out_specs=in_vmem(len(shapes)),
        compiler_params=pltpu.CompilerParams(vmem_limit_bytes=VMEM_LIMIT),
    )(*ins)


def halves(pairs):
    cuts, shapes = [], []
    for k, (keep, _) in enumerate(pairs):
        slots, rows, cols = keep.shape
        for part in range(2):
            cuts.append((k, part * slots // 2, (part + 1) * slots // 2, 0, cols, len(shapes), 0))
            shapes.append((slots // 2, rows, cols))
    return add_pairs(pairs, cuts, shapes)


def quarters(keep, other, cut):
    slots, rows, cols = keep.shape
    cuts, shapes = [], []
    for left, right in ((0, cut), (cut, cols)):
        for part in range(2):
            cuts.append(
                (0, part * slots // 2, (part + 1) * slots // 2, left, right, len(shapes), 0)
            )
            shapes.append((slots // 2, rows, right - left))
    return add_pairs([(keep, other)], cuts, shapes)


def rejoin(pairs):
    slots, rows, left_cols = pairs[0][0].shape
    right_cols = pairs[1][0].shape[2]
    cuts, shapes = [], []
    for part in range(2):
        first, last = part * slots // 2, (part + 1) * slots // 2
        cuts.append((0, first, last, 0, left_cols, part, 0))
        cuts.append((1, first, last, 0, right_cols, part, left_cols))
        shapes.append((slots // 2, rows, left_cols + right_cols))
    return add_pairs(pairs, cuts, shapes)


def head_lanes(values, head, width):
    lane = lax.broadcasted_iota(jnp.int32, values.shape, 1)
    return jnp.where(lane // width == head, values, jnp.zeros_like(values))


def later_keys(block):
    key_at = lax.broadcasted_iota(jnp.int32, (block, block), 0)
    query_at = lax.broadcasted_iota(jnp.int32, (block, block), 1)
    return key_at > query_at


def scores_of(keys, query, hidden_keys, block):
    scores = contract_last(keys, query)
    last = jnp.where(hidden_keys, MASKED, scores[-block:])
    if scores.shape[0] == block:
        return last
    return jnp.concatenate([scores[:-block], last], axis=0)


def attend_kernel(block, width, q_ref, k_ref, v_ref, out_ref, lse_ref):
    length, lanes = q_ref.shape
    scale = jnp.bfloat16(width ** (-0.5))
    hidden_keys = later_keys(block)
    values_t = v_ref[...].T
    for first in range(0, length, block):
        last = first + block
        queries = q_ref[first:last, :] * scale
        outs = []
        for head in range(lanes // width):
            scores = scores_of(k_ref[:last, :], head_lanes(queries, head, width), hidden_keys, block)
            top = jnp.max(scores, axis=0, keepdims=True)
            probs = jnp.exp(scores - top)
            total = jnp.sum(probs, axis=0, keepdims=True)
            mixed = jnp.dot(
                values_t[head * width : (head + 1) * width, :last],
                probs.astype(jnp.bfloat16),
                preferred_element_type=jnp.float32,
            )
            outs.append(mixed / total)
            lse_ref[head : head + 1, first:last] = top + jnp.log(total)
        out_ref[first:last, :] = jnp.concatenate(outs, axis=0).T.astype(jnp.bfloat16)


def attend_back_kernel(
    block, width, q_ref, k_ref, v_ref, g_ref, o_ref, lse_ref, dq_ref, dk_ref, dv_ref, dk_acc, dv_acc
):
    length, lanes = q_ref.shape
    heads = lanes // width
    scale = jnp.bfloat16(width ** (-0.5))
    hidden_keys = later_keys(block)
    keys_t = k_ref[...].T
    for first in reversed(range(0, length, block)):
        last = first + block
        queries = q_ref[first:last, :] * scale
        grads = g_ref[first:last, :]
        products = (grads.astype(jnp.float32) * o_ref[first:last, :].astype(jnp.float32)).T
        key_part = value_part = None
        query_parts = []
        for head in range(heads):
            query = head_lanes(queries, head, width)
            grad = head_lanes(grads, head, width)
            scores = scores_of(k_ref[:last, :], query, hidden_keys, block)
            probs = jnp.exp(scores - lse_ref[head : head + 1, first:last])
            delta = jnp.sum(products[head * width : (head + 1) * width], axis=0, keepdims=True)
            prob_grad = contract_last(v_ref[:last, :], grad)
            score_grad = (probs * (prob_grad - delta)).astype(jnp.bfloat16)
            key_term = jnp.dot(score_grad, query, preferred_element_type=jnp.float32)
            value_term = jnp.dot(
                probs.astype(jnp.bfloat16), grad, preferred_element_type=jnp.float32
            )
            key_part = key_term if key_part is None else key_part + key_term
            value_part = value_term if value_part is None else value_part + value_term
            query_parts.append(
                jnp.dot(
                    keys_t[head * width : (head + 1) * width, :last],
                    score_grad,
                    preferred_element_type=jnp.float32,
                )
            )
        query_grad = jnp.concatenate(query_parts, axis=0).T * width ** (-0.5)
        dq_ref[first:last, :] = query_grad.astype(jnp.bfloat16)
        if last == length:
            dk_acc[...] = key_part
            dv_acc[...] = value_part
        else:
            dk_acc[:last, :] += key_part
            dv_acc[:last, :] += value_part
    dk_ref[...] = dk_acc[...].astype(jnp.bfloat16)
    dv_ref[...] = dv_acc[...].astype(jnp.bfloat16)


def pair_spec(length, first):
    return pl.BlockSpec((length, 128), lambda pair: (0, first + pair))


def attend(qkv):
    length, cols = qkv.shape
    pairs = cols // 3 // 128
    return pl.pallas_call(
        functools.partial(attend_kernel, 256, HEAD_DIM),
        grid=(pairs,),
        out_shape=[
            jax.ShapeDtypeStruct((length, cols // 3), jnp.bfloat16),
            jax.ShapeDtypeStruct((8 * pairs, length), jnp.float32),
        ],
        in_specs=[pair_spec(length, k * pairs) for k in range(3)],
        out_specs=[pair_spec(length, 0), pl.BlockSpec((8, length), lambda pair: (pair, 0))],
        compiler_params=pltpu.CompilerParams(vmem_limit_bytes=VMEM_LIMIT),
        cost_estimate=COST,
    )(qkv, qkv, qkv)


def attend_back(qkv, grads, attended, lse, pair):
    length, cols = qkv.shape
    pairs = cols // 3 // 128
    column = functools.partial(pair_spec, length)
    return pl.pallas_call(
        functools.partial(attend_back_kernel, 256, HEAD_DIM),
        grid=(1,),
        out_shape=[jax.ShapeDtypeStruct((length, 128), jnp.bfloat16)] * 3,
        in_specs=[column(k * pairs + pair) for k in range(3)]
        + [column(pair)] * 2
        + [pl.BlockSpec((8, length), lambda step: (pair, 0))],
        out_specs=[column(0)] * 3,
        scratch_shapes=[pltpu.VMEM((length, 128), jnp.float32)] * 2,
        compiler_params=pltpu.CompilerParams(vmem_limit_bytes=VMEM_LIMIT),
        cost_estimate=COST,
    )(qkv, qkv, qkv, grads, attended, lse)


def in_order(seq_index, mine, other, axis):
    return jnp.where(
        seq_index == 0,
        jnp.concatenate([mine, other], axis=axis),
        jnp.concatenate([other, mine], axis=axis),
    )


def on_device(inputs, vectors, w_qkv, w_out, w_up, w_down, up_bias, cotangent):
    _, piece_len, model_width = inputs.shape
    sizes = {"dp": lax.axis_size("dp"), "seq": lax.axis_size("seq")}
    seq_index = lax.axis_index("seq")
    pair = jnp.stack([lax.axis_index("dp"), seq_index])
    swap = ("seq", 1)
    half_width = model_width // 2
    dp_masks = bit_masks(sizes["dp"])
    core, row_hop = ("dp", dp_masks[0]), ("dp", dp_masks[1])
    far = [("dp", mask) for mask in reversed(dp_masks[2:])]
    path_dp = far + [row_hop, core]
    paths = (far + [swap, row_hop, core], far + [row_hop, swap, core])
    rows = w_qkv.shape[0]
    per_row = up_bias.shape[0] // rows

    bias_cols = up_bias.reshape(per_row, rows).T
    small_own = jnp.concatenate(
        [vectors, bias_cols, jnp.zeros((rows, 128 - 8 - per_row), vectors.dtype)], axis=1
    )
    blocks = [w_qkv[:, k * half_width : (k + 1) * half_width] for k in range(3)]
    arrived = exchange(jnp.concatenate([blocks[1], small_own], axis=1), swap, sizes)
    head_cols = jnp.where(
        seq_index == 0,
        jnp.concatenate([blocks[0], blocks[2], arrived[:, :half_width]], axis=1),
        jnp.concatenate([arrived[:, :half_width], blocks[0], blocks[2]], axis=1),
    )
    bias_other = arrived[:, half_width + 8 : half_width + 8 + per_row]
    small_cols = jnp.concatenate(
        [
            vectors,
            in_order(seq_index, bias_cols, bias_other, 1),
            jnp.zeros((rows, 128 - 8 - 2 * per_row), vectors.dtype),
        ],
        axis=1,
    )
    x_own = inputs.reshape(piece_len, model_width)
    x_other = exchange(x_own, swap, sizes)
    first = jnp.concatenate([head_cols, small_cols], axis=1)[None]
    a_held = jnp.concatenate([w_out, w_up], axis=1)[None]
    b_held = w_down[None]
    up_cols = w_up.shape[1]
    cut, down_cut = 8 * a_held.shape[2] // 15 // 128 * 128, up_cols // 2
    for hop in far:
        a_held = grow(a_held, hop, sizes)
        first = grow(first, hop, sizes)
    b_held = grow(after(b_held, first), far[0], sizes)
    a_halves = [a_held[:, :, :cut], a_held[:, :, cut:]]
    a_next = [exchange(part, paths[k][len(far)], sizes) for k, part in enumerate(a_halves)]
    first = grow(first, row_hop, sizes)
    b_next = exchange(b_held, far[1], sizes)
    first_parts = [first, exchange(first, core, sizes)]

    bf16, f32 = jnp.bfloat16, jnp.float32
    seq_len, ff = 2 * piece_len, 2 * w_up.shape[1]
    head_width = 3 * half_width
    dense = 2 * piece_len * model_width
    dma = pltpu.SemaphoreType.DMA
    qkv_rows, normed_one, qkv_full, vec_rows = local_call(
        functools.partial(project_kernel, path_dp, rows),
        pair,
        [x_own, x_other],
        first_parts,
        [
            shaped(bf16, seq_len, head_width),
            shaped(bf16, seq_len, model_width),
            shaped(bf16, model_width, head_width),
            shaped(f32, 16, model_width),
        ],
        [],
        [pltpu.VMEM((model_width, 128), bf16), dma((2, sizes["dp"]))],
        2 * dense * head_width,
    )
    bias_row = jnp.transpose(
        vec_rows[8 : 8 + 2 * per_row].reshape(2 * per_row, sizes["dp"], rows), (1, 0, 2)
    ).reshape(1, ff)
    a_halves = [
        jnp.concatenate([a_halves[k], after(a_next[k], qkv_rows)], axis=0) for k in range(2)
    ]
    a_more = [exchange(part, paths[k][len(far) + 1], sizes) for k, part in enumerate(a_halves)]
    b_held = jnp.concatenate([b_held, after(b_next, qkv_rows)], axis=0)
    b_halves = [b_held[:, :, :down_cut], b_held[:, :, down_cut:]]
    b_next = [exchange(part, paths[k][len(far)], sizes) for k, part in enumerate(b_halves)]
    attended, lse = attend(after(qkv_rows, *a_halves, *b_halves))

    def crossed(parts, more):
        pieces = []
        for k in range(2):
            both = (parts[k], more[k])
            pieces += [*both, *[exchange(part, core, sizes) for part in both]]
        return pieces

    def tokens_of(values, index):
        return lax.dynamic_slice_in_dim(values, index * piece_len, piece_len, 0)

    attended_own = tokens_of(attended, seq_index)
    attended_other = exchange(tokens_of(attended, 1 - seq_index), swap, sizes)
    a_parts = crossed(a_halves, [after(part, attended) for part in a_more])
    b_halves = [
        jnp.concatenate([b_halves[k], after(b_next[k], attended)], axis=0) for k in range(2)
    ]
    b_more = [exchange(part, paths[k][len(far) + 1], sizes) for k, part in enumerate(b_halves)]
    mlp_grad = cotangent.reshape(piece_len, model_width)
    slots = sizes["dp"] * sizes["seq"]
    chunk = math.gcd(ff, 1024)
    weight_scratch = [
        pltpu.VMEM((model_width, model_width), bf16),
        pltpu.VMEM((model_width, ff), bf16),
    ]
    middle, normed_two, hidden, slope = local_call(
        functools.partial(hidden_kernel, paths, rows, cut, chunk),
        pair,
        [attended_own, attended_other, after(x_own, *b_halves), vec_rows, bias_row],
        a_parts,
        [
            shaped(f32, piece_len, model_width),
            shaped(bf16, piece_len, model_width),
            shaped(bf16, piece_len, ff),
            shaped(bf16, piece_len, ff),
        ],
        [],
        weight_scratch + [dma((3, slots))],
        dense * (model_width + ff),
    )
    b_parts = crossed(b_halves, [after(part, hidden) for part in b_more])
    down_keep, down_send = local_call(
        functools.partial(down_grad_kernel, paths, rows, down_cut, chunk),
        pair,
        [hidden, mlp_grad],
        [],
        [],
        [shaped(bf16, slots // 2, rows, ff // 2)] * 2,
        [
            pltpu.VMEM((model_width, ff), bf16),
            pltpu.VMEM((model_width, piece_len), bf16),
            dma((2, slots)),
        ],
        dense * ff,
    )

    down_other = exchange(down_send, core, sizes)
    up_grad, norm_two_grad, bias_sums = local_call(
        functools.partial(
            mlp_back_kernel, paths, rows, cut, down_cut, w_out.shape[1], chunk
        ),
        pair,
        [slope, after(mlp_grad, down_keep)],
        a_parts + b_parts,
        [
            shaped(bf16, piece_len, ff),
            shaped(f32, piece_len, model_width),
            shaped(f32, 8, ff),
        ],
        [],
        [pltpu.VMEM((model_width, ff), bf16)] * 2 + [dma((2, slots)), dma((2, slots))],
        2 * dense * ff,
    )
    down_keeps, down_sends = [None] * 2, [None] * 2
    down_keeps[0], down_sends[0], down_keeps[1], down_sends[1] = quarters(
        down_keep, after(down_other, norm_two_grad), down_cut
    )
    down_others = [exchange(down_sends[k], (swap, row_hop)[1 - k], sizes) for k in range(2)]
    middle_grad, attn_out_grad, grads_own, grads_send, sums = local_call(
        functools.partial(middle_back_kernel, paths, rows, w_out.shape[1]),
        pair,
        [after(norm_two_grad, *down_keeps), middle, mlp_grad, vec_rows],
        a_parts[:4],
        [
            shaped(f32, piece_len, model_width),
            shaped(bf16, piece_len, model_width),
            shaped(bf16, piece_len, half_width),
            shaped(bf16, piece_len, half_width),
            shaped(f32, 8, model_width),
        ],
        [],
        [weight_scratch[0], dma((1, slots))],
        dense * model_width,
    )
    grads_other = exchange(grads_send, swap, sizes)
    back_cut = 8 * (up_cols + w_out.shape[1]) // 15 // 128 * 128
    up_keep, up_send = local_call(
        functools.partial(up_grad_kernel, paths, rows, back_cut, chunk),
        pair,
        [normed_two, up_grad, attended_own, attended_other, attn_out_grad],
        [],
        [],
        [shaped(bf16, slots // 2, rows, (ff + model_width) // 2)] * 2,
        [
            pltpu.VMEM((model_width, ff), bf16),
            pltpu.VMEM((model_width, model_width), bf16),
            pltpu.VMEM((model_width, piece_len), bf16),
            dma((3, slots)),
        ],
        dense * (model_width + ff),
    )
    up_other = exchange(up_send, core, sizes)
    grad_heads = in_order(seq_index, grads_own, after(grads_other, up_keep), 0)
    down_others = [after(part, up_keep) for part in down_others]
    down_sums = halves([(down_keeps[k], down_others[k]) for k in range(2)])
    down_keeps, down_sends = down_sums[0::2], down_sums[1::2]
    down_others = [exchange(down_sends[k], (swap, row_hop)[k], sizes) for k in range(2)]

    def head_pair_back(at, *earlier):
        return attend_back(qkv_rows, grad_heads, attended, lse, at)

    pair_grads = [head_pair_back(0)]
    up_keeps, up_sends = [None] * 2, [None] * 2
    up_keeps[0], up_sends[0], up_keeps[1], up_sends[1] = quarters(
        up_keep, after(up_other, pair_grads[0][0]), back_cut
    )
    down_keep, down_send = rejoin(
        [(down_keeps[k], after(down_others[k], pair_grads[0][0])) for k in range(2)]
    )
    up_others = [exchange(up_sends[k], (swap, row_hop)[1 - k], sizes) for k in range(2)]
    down_other = exchange(down_send, far[1], sizes)
    pair_grads += [head_pair_back(at) for at in range(1, half_width // 128)]
    down_keep, down_send = halves([(down_keep, down_other)])
    down_other = exchange(down_send, far[0], sizes)
    bias_rows = jnp.transpose(
        bias_sums[0].reshape(sizes["dp"], 2 * per_row, rows), (1, 0, 2)
    ).reshape(2 * per_row, model_width)
    da_own, da_send, last_keep, last_send = local_call(
        functools.partial(project_back_kernel, path_dp, rows, half_width // 128),
        pair,
        [
            *[grad for group in pair_grads for grad in group],
            qkv_full,
            normed_one,
            x_own,
            x_other,
            vec_rows,
            sums,
            bias_rows,
        ],
        [],
        [shaped(f32, piece_len, model_width), shaped(bf16, piece_len, model_width)],
        [shaped(bf16, sizes["dp"] // 2, rows, head_width + 128)] * 2,
        [
            pltpu.VMEM((seq_len, head_width), bf16),
            pltpu.VMEM((model_width, head_width + 128), bf16),
            pltpu.VMEM((2, piece_len, model_width), f32),
            pltpu.VMEM((128, model_width), f32),
            pltpu.VMEM((model_width, seq_len), bf16),
            dma((1, sizes["dp"])),
        ],
        4 * dense * head_width,
    )
    last_other = exchange(last_send, core, sizes)
    up_sums = halves([(up_keeps[k], after(up_others[k], da_own)) for k in range(2)])
    up_keeps, up_sends = up_sums[0::2], up_sums[1::2]
    up_others = [exchange(up_sends[k], (swap, row_hop)[k], sizes) for k in range(2)]
    da_other = exchange(da_send, swap, sizes)
    last_keep, last_send = halves([(last_keep, last_other)])
    last_other = exchange(last_send, row_hop, sizes)
    up_keep, up_send = rejoin([(up_keeps[k], after(up_others[k], last_send)) for k in range(2)])
    up_other = exchange(up_send, far[1], sizes)
    grad_down = down_keep[0].astype(f32) + after(down_other, last_send)[0].astype(f32)
    (result,) = local_call(
        functools.partial(result_kernel, paths, rows, down_cut),
        pair,
        [hidden, after(middle, last_send, up_send), vec_rows],
        b_parts,
        [shaped(bf16, piece_len, model_width)],
        [],
        [pltpu.VMEM((model_width, ff), bf16), dma((2, slots))],
        dense * ff,
    )
    last_keep, last_send = halves([(last_keep, after(last_other, result))])
    last_other = exchange(last_send, far[1], sizes)
    up_keep, up_send = halves([(up_keep, after(up_other, last_send))])
    up_other = exchange(up_send, far[0], sizes)
    norm_one_own = da_own + after(da_other, last_send).astype(f32)
    unit, inverse = normed(x_own.astype(f32))
    input_grad = middle_grad + normed_back(norm_one_own, unit, inverse, vec_rows[0:1])
    last_keep, last_send = halves([(last_keep, after(last_other, input_grad))])
    last_other = exchange(last_send, far[0], sizes)
    up_other = after(up_other, last_send)
    grad_up_out = up_keep[0].astype(f32) + up_other[0].astype(f32)
    grad_up, grad_out = grad_up_out[:, :up_cols], grad_up_out[:, up_cols:]
    last = last_keep[0].astype(f32) + last_other[0].astype(f32)
    small_last = last[:, 3 * half_width :]
    sent = jnp.where(
        seq_index == 0, last[:, 2 * half_width :],
        jnp.concatenate([last[:, :half_width], small_last], axis=1)
    )
    arrived_last = exchange(sent.astype(jnp.bfloat16), swap, sizes).astype(jnp.float32)
    middle_block = arrived_last[:, :half_width]
    kept = jnp.where(seq_index == 0, last[:, : 2 * half_width], last[:, half_width : 3 * half_width])
    grad_qkv = jnp.concatenate([kept[:, :half_width], middle_block, kept[:, half_width:]], axis=1)
    small_sum = small_last + arrived_last[:, half_width:]
    grad_vectors = small_sum[:, :8]
    bias_own = lax.dynamic_slice_in_dim(small_sum, 8 + seq_index * per_row, per_row, 1)
    grad_up_bias = bias_own.T.reshape(-1)
    return (
        result.reshape(1, piece_len, model_width),
        input_grad.reshape(1, piece_len, model_width),
        grad_qkv,
        grad_out,
        grad_up,
        grad_down,
        grad_up_bias,
        grad_vectors,
    )


def block(*arrays):
    n_dp, n_seq = lax.axis_size("dp"), lax.axis_size("seq")
    rows = arrays[2].shape[0]
    whole_tiles = rows % 16 == 0 and all(weight.shape[1] % 384 == 0 for weight in arrays[2:6])
    powers = n_dp == 16
    if n_seq == 2 and powers and whole_tiles and arrays[0].shape[0] == 1:
        return on_device(*arrays)
    return on_device_general(*arrays)


def solution(mesh):
    placed = (
        P("dp", "seq", None),
        P("dp", None),
        P("dp", "seq"),
        P("dp", "seq"),
        P("dp", "seq"),
        P("dp", "seq"),
        P(("dp", "seq")),
        P("dp", "seq", None),
    )
    return jax.shard_map(
        block,
        mesh=mesh,
        in_specs=placed,
        out_specs=(
            P("dp", "seq", None),
            P("dp", "seq", None),
            P("dp", "seq"),
            P("dp", "seq"),
            P("dp", "seq"),
            P("dp", "seq"),
            P(("dp", "seq")),
            P("dp", None),
        ),
        check_vma=False,
    )
```

```python
import functools
import math

import jax
import jax.numpy as jnp
from jax import lax
from jax.experimental import pallas as pl
from jax.experimental.pallas import tpu as pltpu
from jax.sharding import PartitionSpec as P

HEADS = 12
HEAD_DIM = 64
VMEM_LIMIT = 28 * 1024 * 1024
COST = pl.CostEstimate(flops=10**11, bytes_accessed=10**7, transcendentals=0)


EPSILON = 1e-05
MASKED = -1e30


def norm_rows(values, scale_row, shift_row):
    row_mean = jnp.mean(values, axis=-1, keepdims=True)
    centered = values - row_mean
    variance = jnp.mean(centered * centered, axis=-1, keepdims=True)
    return centered * lax.rsqrt(variance + EPSILON) * scale_row + shift_row


def gelu_tanh(values):
    return (
        0.5
        * values
        * (1.0 + jnp.tanh(0.7978845608028654 * (values + 0.044715 * values * values * values)))
    )


def contract_last(left_side, right_side):
    return lax.dot_general(
        left_side, right_side, (((1,), (1,)), ((), ())), preferred_element_type=jnp.float32
    )


def contract_first(left_side, right_side):
    return lax.dot_general(
        left_side, right_side, (((0,), (0,)), ((), ())), preferred_element_type=jnp.float32
    )


def on_device_general(inputs, vectors, w_qkv, w_out, w_up, w_down, up_bias, cotangent):
    seq_count, piece_len, model_width = inputs.shape
    row_count = seq_count * piece_len
    score_scale = HEAD_DIM ** (-0.5)
    seq_index = lax.axis_index("seq")
    query_pos = seq_index * piece_len + jnp.arange(piece_len)
    qkv_cols, out_cols, up_cols, down_cols, upb_cols = (
        lax.all_gather(w_qkv, "seq", axis=1, tiled=True),
        lax.all_gather(w_out, "seq", axis=1, tiled=True),
        lax.all_gather(w_up, "seq", axis=1, tiled=True),
        lax.all_gather(w_down, "seq", axis=1, tiled=True),
        lax.all_gather(up_bias, "seq", axis=0, tiled=True),
    )
    full_fwd = (
        lax.all_gather(qkv_cols, "dp", axis=0, tiled=True),
        lax.all_gather(out_cols, "dp", axis=0, tiled=True),
        lax.all_gather(up_cols, "dp", axis=0, tiled=True),
        lax.all_gather(down_cols, "dp", axis=0, tiled=True),
        lax.all_gather(upb_cols, "dp", axis=0, tiled=True),
        lax.all_gather(vectors, "dp", axis=0, tiled=True),
    )
    qkv_full, out_full, up_full, down_full, upb_full, vec_full = full_fwd
    vec_values = vec_full.astype(jnp.float32)
    resid_in = inputs.reshape(row_count, model_width).astype(jnp.float32)
    normed_one = norm_rows(resid_in, vec_values[:, 0], vec_values[:, 1]).astype(jnp.bfloat16)
    qkv_bias = jnp.concatenate(
        [vec_values[:, 2], jnp.zeros_like(vec_values[:, 2]), vec_values[:, 3]]
    )
    qkv_rows = (
        jnp.dot(normed_one, qkv_full, preferred_element_type=jnp.float32) + qkv_bias
    ).astype(jnp.bfloat16)
    queries = qkv_rows[:, :model_width].reshape(seq_count, piece_len, HEADS, HEAD_DIM)
    key_vals = qkv_rows[:, model_width:].reshape(seq_count, piece_len, 2 * model_width)

    def block_scores(key_block, first_row):
        key_rows = key_block.shape[1]
        keys_part = key_block[..., :model_width].reshape(seq_count, key_rows, HEADS, HEAD_DIM)
        scores = (
            jnp.einsum("bqhd,bkhd->bhqk", queries, keys_part, preferred_element_type=jnp.float32)
            * score_scale
        )
        causal = (first_row + jnp.arange(key_rows))[None, :] <= query_pos[:, None]
        return jnp.where(causal, scores, MASKED)

    key_block = lax.all_gather(key_vals, "seq", axis=1, tiled=True)
    run_max = jnp.full((seq_count, HEADS, piece_len), MASKED, jnp.float32)
    key_rows = key_block.shape[1]
    values_part = key_block[..., model_width:].reshape(seq_count, key_rows, HEADS, HEAD_DIM)
    scores = block_scores(key_block, jnp.int32(0))
    new_max = jnp.maximum(run_max, jnp.max(scores, axis=-1))
    exp_scores = jnp.exp(scores - new_max[..., None])
    run_total = jnp.sum(exp_scores, axis=-1)
    added_part = jnp.einsum(
        "bhqk,bkhd->bqhd",
        exp_scores.astype(jnp.bfloat16),
        values_part,
        preferred_element_type=jnp.float32,
    )
    run_acc = added_part
    run_max, run_total, run_acc = (new_max, run_total, run_acc)
    attended = run_acc / jnp.transpose(run_total, (0, 2, 1))[..., None]
    log_total = run_max + jnp.log(run_total)
    attended_lo = attended.reshape(row_count, model_width).astype(jnp.bfloat16)
    branch_attn = (
        jnp.dot(attended_lo, out_full, preferred_element_type=jnp.float32) + vec_values[:, 4]
    )
    middle = resid_in + branch_attn
    normed_two = norm_rows(middle, vec_values[:, 5], vec_values[:, 6]).astype(jnp.bfloat16)
    up_act = jnp.dot(normed_two, up_full, preferred_element_type=jnp.float32) + upb_full.astype(
        jnp.float32
    )
    hidden = gelu_tanh(up_act).astype(jnp.bfloat16)
    branch_mlp = contract_last(hidden, down_full) + vec_values[:, 7]
    result = middle + branch_mlp
    qkv_back, out_back, up_back, down_back = (qkv_full, out_full, up_full, down_full)
    out_grad = cotangent.reshape(row_count, model_width).astype(jnp.float32)
    mlp_grad = out_grad.astype(jnp.bfloat16)
    hidden_grad = jnp.dot(mlp_grad, down_back, preferred_element_type=jnp.float32)
    gelu_pull = jax.vjp(gelu_tanh, up_act)[1]
    up_grad = gelu_pull(hidden_grad)[0].astype(jnp.bfloat16)
    norm_two_grad = contract_last(up_grad, up_back)
    ln_two_pull = jax.vjp(norm_rows, middle, vec_values[:, 5], vec_values[:, 6])[1]
    middle_part, scale_two, shift_two = ln_two_pull(norm_two_grad)
    middle_grad = out_grad + middle_part
    attn_out_grad = middle_grad.astype(jnp.bfloat16)
    attended_grad = contract_last(attn_out_grad, out_back).astype(jnp.bfloat16)
    grad_heads = attended_grad.reshape(seq_count, piece_len, HEADS, HEAD_DIM)
    row_delta = jnp.transpose(
        jnp.sum(grad_heads.astype(jnp.float32) * attended, axis=-1), (0, 2, 1)
    )
    key_vals_all = lax.all_gather(key_vals, "seq", axis=1, tiled=True)
    total_len = key_vals_all.shape[1]
    key_block_len = math.gcd(total_len, 512)

    def back_step(query_acc, block_index):
        first_row = block_index * key_block_len
        key_block = lax.dynamic_slice_in_dim(key_vals_all, first_row, key_block_len, 1)
        keys_part = key_block[..., :model_width].reshape(seq_count, key_block_len, HEADS, HEAD_DIM)
        values_part = key_block[..., model_width:].reshape(
            seq_count, key_block_len, HEADS, HEAD_DIM
        )
        scores = block_scores(key_block, first_row)
        attn_probs = jnp.exp(scores - log_total[..., None])
        prob_grad = jnp.einsum(
            "bqhd,bkhd->bhqk", grad_heads, values_part, preferred_element_type=jnp.float32
        )
        score_grad = (attn_probs * (prob_grad - row_delta[..., None])).astype(jnp.bfloat16)
        step_part = jnp.einsum(
            "bhqk,bkhd->bqhd", score_grad, keys_part, preferred_element_type=jnp.float32
        )
        key_grad = (
            jnp.einsum("bhqk,bqhd->bkhd", score_grad, queries, preferred_element_type=jnp.float32)
            * score_scale
        )
        value_grad = jnp.einsum(
            "bhqk,bqhd->bkhd",
            attn_probs.astype(jnp.bfloat16),
            grad_heads,
            preferred_element_type=jnp.float32,
        )
        key_value = jnp.concatenate(
            [
                key_grad.reshape(seq_count, key_block_len, model_width),
                value_grad.reshape(seq_count, key_block_len, model_width),
            ],
            axis=-1,
        )
        return (query_acc + step_part * score_scale, key_value)

    query_grad, kv_blocks = lax.scan(
        back_step,
        jnp.zeros((seq_count, piece_len, HEADS, HEAD_DIM), jnp.float32),
        jnp.arange(total_len // key_block_len),
    )
    kv_terms = jnp.moveaxis(kv_blocks, 0, 1).reshape(seq_count, total_len, 2 * model_width)
    key_val_grad = lax.psum_scatter(
        kv_terms.astype(jnp.bfloat16), "seq", scatter_dimension=1, tiled=True
    ).astype(jnp.float32)
    key_val_grad = key_val_grad.reshape(row_count, 2 * model_width)
    qkv_grad = jnp.concatenate(
        [query_grad.reshape(row_count, model_width), key_val_grad], axis=1
    ).astype(jnp.bfloat16)
    norm_one_grad = contract_last(qkv_grad, qkv_back)
    ln_one_pull = jax.vjp(norm_rows, resid_in, vec_values[:, 0], vec_values[:, 1])[1]
    input_part, scale_one, shift_one = ln_one_pull(norm_one_grad)
    input_grad = middle_grad + input_part
    whole_qkv = contract_first(normed_one, qkv_grad)
    whole_out = contract_first(attended_lo, attn_out_grad)
    whole_up = contract_first(normed_two, up_grad)
    whole_down = contract_first(mlp_grad, hidden)
    row_qkv, row_out, row_up, row_down = (
        lax.psum_scatter(
            whole_qkv.astype(jnp.bfloat16), "dp", scatter_dimension=0, tiled=True
        ).astype(jnp.float32),
        lax.psum_scatter(
            whole_out.astype(jnp.bfloat16), "dp", scatter_dimension=0, tiled=True
        ).astype(jnp.float32),
        lax.psum_scatter(
            whole_up.astype(jnp.bfloat16), "dp", scatter_dimension=0, tiled=True
        ).astype(jnp.float32),
        lax.psum_scatter(
            whole_down.astype(jnp.bfloat16), "dp", scatter_dimension=0, tiled=True
        ).astype(jnp.float32),
    )
    grad_qkv, grad_out, grad_up, grad_down = (
        lax.psum_scatter(
            row_qkv.astype(jnp.bfloat16), "seq", scatter_dimension=1, tiled=True
        ).astype(jnp.float32),
        lax.psum_scatter(
            row_out.astype(jnp.bfloat16), "seq", scatter_dimension=1, tiled=True
        ).astype(jnp.float32),
        lax.psum_scatter(
            row_up.astype(jnp.bfloat16), "seq", scatter_dimension=1, tiled=True
        ).astype(jnp.float32),
        lax.psum_scatter(
            row_down.astype(jnp.bfloat16), "seq", scatter_dimension=1, tiled=True
        ).astype(jnp.float32),
    )
    vec_term = jnp.stack(
        [
            scale_one,
            shift_one,
            jnp.sum(qkv_grad[:, :model_width].astype(jnp.float32), axis=0),
            jnp.sum(qkv_grad[:, 2 * model_width :].astype(jnp.float32), axis=0),
            jnp.sum(attn_out_grad.astype(jnp.float32), axis=0),
            scale_two,
            shift_two,
            jnp.sum(mlp_grad.astype(jnp.float32), axis=0),
        ],
        axis=1,
    )
    upb_term = jnp.sum(up_grad.astype(jnp.float32), axis=0)
    vec_sum, upb_sum = lax.psum((vec_term, upb_term), ("dp", "seq"))
    vec_rows = vectors.shape[0]
    grad_vectors = lax.dynamic_slice_in_dim(vec_sum, lax.axis_index("dp") * vec_rows, vec_rows, 0)
    upb_rows = up_bias.shape[0]
    upb_start = (lax.axis_index("dp") * lax.axis_size("seq") + seq_index) * upb_rows
    grad_up_bias = lax.dynamic_slice_in_dim(upb_sum, upb_start, upb_rows, 0)
    return (
        result.reshape(seq_count, piece_len, model_width).astype(jnp.bfloat16),
        input_grad.reshape(seq_count, piece_len, model_width),
        grad_qkv,
        grad_out,
        grad_up,
        grad_down,
        grad_up_bias,
        grad_vectors,
    )


def bit_masks(count):
    return [1 << k for k in range(count.bit_length() - 1)]


def exchange(values, hop, sizes):
    axis, mask = hop
    return lax.ppermute(values, axis, [(i, i ^ mask) for i in range(sizes[axis])])


def slot_owner(slot, path):
    offset = {"dp": 0, "seq": 0}
    for k, (axis, mask) in enumerate(path):
        if slot >> k & 1:
            offset[axis] ^= mask
    return offset["dp"], offset["seq"]


def after(values, *earlier):
    return lax.optimization_barrier((values, *earlier))[0]


def grow(held, hop, sizes):
    return jnp.concatenate([held, exchange(held, hop, sizes)], axis=0)


def start_place(path, rows, parts, me_ref, targets, sems):
    total = 1 << len(path)
    each = total // len(parts)
    copies = []
    for k, (target, first, cols, stride, at) in enumerate(targets):
        for slot in range(total):
            off_dp, off_seq = slot_owner(slot, path)
            row = pl.multiple_of((me_ref[0] ^ off_dp) * rows, 16)
            col = pl.multiple_of((me_ref[1] ^ off_seq) * stride + at, 128)
            src = parts[slot // each].at[slot % each, :, pl.ds(first, cols)]
            dst = target.at[pl.ds(row, rows), pl.ds(col, cols)]
            copy = pltpu.make_async_copy(src, dst, sems.at[k, slot])
            copy.start()
            copies.append(copy)
    return copies


def start_split(rows, me_ref, pieces, keep_ref, send_ref, sems):
    copies = []
    for k, (path, whole, stride, first, cols, at) in enumerate(pieces):
        half = 1 << (len(path) - 1)
        for slot in range(2 * half):
            off_dp, off_seq = slot_owner(slot, path)
            row = pl.multiple_of((me_ref[0] ^ off_dp) * rows, 16)
            col = pl.multiple_of((me_ref[1] ^ off_seq) * stride + first, 128)
            target = keep_ref if slot < half else send_ref
            copy = pltpu.make_async_copy(
                whole.at[pl.ds(row, rows), pl.ds(col, cols)],
                target.at[slot % half, :, pl.ds(at, cols)],
                sems.at[k, slot],
            )
            copy.start()
            copies.append(copy)
    return copies


def wait_all(copies):
    for copy in copies:
        copy.wait()


def normed(values):
    centered = values - jnp.mean(values, axis=-1, keepdims=True)
    inverse = lax.rsqrt(jnp.mean(centered * centered, axis=-1, keepdims=True) + EPSILON)
    return centered * inverse, inverse


def normed_back(grads, unit, inverse, scale_row):
    scaled = grads * scale_row
    mean_one = jnp.mean(scaled, axis=-1, keepdims=True)
    mean_two = jnp.mean(scaled * unit, axis=-1, keepdims=True)
    return inverse * (scaled - mean_one - unit * mean_two)


def dot(left_side, right_side):
    return jnp.dot(left_side, right_side, preferred_element_type=jnp.float32)


def column_sum(values):
    return jnp.sum(values.astype(jnp.float32), axis=0, keepdims=True)


def project_kernel(path, rows, me_ref, own_ref, other_ref, *refs):
    parts = refs[:2]
    qkv_ref, a_ref, w_ref, vec_ref, small, sems = refs[2:]
    seq = me_ref[1]
    piece, width = own_ref.shape
    third = w_ref.shape[1] // 3
    copies = start_place(
        path,
        rows,
        parts,
        me_ref,
        [(small, 3 * third, 128, 0, 0), (w_ref, 0, 3 * third, 0, 0)],
        sems,
    )
    units = []
    for part in range(2):
        values = jnp.where(seq == part, own_ref[...], other_ref[...]).astype(jnp.float32)
        units.append(normed(values)[0])
    wait_all(copies[: len(copies) // 2])
    vec_ref[...] = small[...].astype(jnp.float32).T[: vec_ref.shape[0]]
    for part in range(2):
        a_ref[part * piece : (part + 1) * piece, :] = (
            units[part] * vec_ref[0:1, :] + vec_ref[1:2, :]
        ).astype(jnp.bfloat16)
    wait_all(copies[len(copies) // 2 :])
    own_cols = pl.ds(pl.multiple_of(seq * third, 128), third)
    for k in range(3):
        cols = slice(k * third, (k + 1) * third)
        for part in range(2):
            at = slice(part * piece, (part + 1) * piece)
            product = dot(a_ref[at, :], w_ref[:, cols])
            if k != 1:
                product = product + vec_ref[2 + k // 2 : 3 + k // 2, own_cols]
            qkv_ref[at, cols] = product.astype(jnp.bfloat16)


def in_vmem(count):
    return [pl.BlockSpec(memory_space=pltpu.VMEM)] * count


def in_any(count):
    return [pl.BlockSpec(memory_space=pl.ANY)] * count


def shaped(dtype, *shape):
    return jax.ShapeDtypeStruct(shape, dtype)


def local_call(kernel, pair, vmem_args, any_args, vmem_outs, any_outs, scratch, flops):
    outs = list(vmem_outs) + list(any_outs)
    moved = sum(a.size * a.dtype.itemsize for a in [*vmem_args, *any_args, *outs])
    return pl.pallas_call(
        kernel,
        out_shape=outs,
        in_specs=[pl.BlockSpec(memory_space=pltpu.SMEM)]
        + in_vmem(len(vmem_args))
        + in_any(len(any_args)),
        out_specs=in_vmem(len(vmem_outs)) + in_any(len(any_outs)),
        scratch_shapes=scratch,
        compiler_params=pltpu.CompilerParams(vmem_limit_bytes=VMEM_LIMIT),
        cost_estimate=COST,
    )(pair, *vmem_args, *any_args)


def gelu_both(values):
    square = values * values
    angle = jnp.tanh(0.7978845608028654 * values * (1.0 + 0.044715 * square))
    half = 0.5 * (1.0 + angle)
    slope = half + 0.5 * values * (1.0 - angle * angle) * (
        0.7978845608028654 * (1.0 + 3.0 * 0.044715 * square)
    )
    return values * half, slope


def place_up(paths, rows, cut, out_cols, parts, me_ref, w_up, sems):
    up_cols = w_up.shape[1] // 2
    left = cut - out_cols
    return start_place(
        paths[0], rows, parts[:4], me_ref, [(w_up, out_cols, left, up_cols, 0)], sems
    ) + start_place(
        paths[1], rows, parts[4:], me_ref, [(w_up, 0, up_cols - left, up_cols, left)], sems.at[1:2]
    )


def place_down(paths, rows, cut, parts, me_ref, w_down, sems):
    cols = w_down.shape[1] // 2
    return start_place(
        paths[0], rows, parts[:4], me_ref, [(w_down, 0, cut, cols, 0)], sems
    ) + start_place(
        paths[1], rows, parts[4:], me_ref, [(w_down, 0, cols - cut, cols, cut)], sems.at[1:2]
    )


def hidden_kernel(paths, rows, cut, chunk, me_ref, *refs):
    mine_ref, other_ref, x_ref, vec_ref, bias_ref = refs[:5]
    parts = refs[5:13]
    h_ref, a_ref, g_ref, slope_ref = refs[13:17]
    w_out, w_up, sems = refs[17:]
    left_first = me_ref[1] == 0
    half = mine_ref.shape[1]
    out_cols = w_out.shape[1] // 2
    out_copies = start_place(
        paths[0], rows, parts[:4], me_ref, [(w_out, 0, out_cols, out_cols, 0)], sems
    )
    up_copies = place_up(paths, rows, cut, out_cols, parts, me_ref, w_up, sems.at[1:3])
    left = jnp.where(left_first, mine_ref[...], other_ref[...])
    right = jnp.where(left_first, other_ref[...], mine_ref[...])
    wait_all(out_copies)
    branch = dot(left, w_out[:half, :]) + dot(right, w_out[half:, :]) + vec_ref[4:5, :]
    middle = x_ref[...].astype(jnp.float32) + branch
    h_ref[...] = middle
    a_ref[...] = (normed(middle)[0] * vec_ref[5:6, :] + vec_ref[6:7, :]).astype(jnp.bfloat16)
    wait_all(up_copies)

    def step(k, carry):
        cols = pl.ds(pl.multiple_of(k * chunk, chunk), chunk)
        act = dot(a_ref[...], w_up[:, cols]) + bias_ref[:, cols]
        value, slope = gelu_both(act)
        g_ref[:, cols] = value.astype(jnp.bfloat16)
        slope_ref[:, cols] = slope.astype(jnp.bfloat16)
        return carry

    lax.fori_loop(0, w_up.shape[1] // chunk, step, 0)


def down_grad_kernel(paths, rows, cut, chunk, me_ref, *refs):
    g_ref, dy_ref, keep_ref, send_ref, grad, dy_t, sems = refs
    dy_t[...] = dy_ref[...].T

    def step(k, carry):
        cols = pl.ds(pl.multiple_of(k * chunk, chunk), chunk)
        grad[:, cols] = dot(dy_t[...], g_ref[:, cols]).astype(jnp.bfloat16)
        return carry

    lax.fori_loop(0, grad.shape[1] // chunk, step, 0)
    cols = grad.shape[1] // 2
    pieces = [
        (paths[0], grad, cols, 0, cut, 0),
        (paths[1], grad, cols, cut, cols - cut, cut),
    ]
    wait_all(start_split(rows, me_ref, pieces, keep_ref, send_ref, sems))


def mlp_back_kernel(paths, rows, cut, down_cut, out_cols, chunk, me_ref, *refs):
    slope_ref, dy_ref = refs[:2]
    parts, down_parts = refs[2:10], refs[10:18]
    du_ref, acc, bias_sum_ref = refs[18:21]
    w_up, w_down, sems, down_sems = refs[21:]
    down_copies = place_down(paths, rows, down_cut, down_parts, me_ref, w_down, down_sems)
    up_copies = place_up(paths, rows, cut, out_cols, parts, me_ref, w_up, sems)
    acc[...] = jnp.zeros_like(acc)
    wait_all(down_copies)
    wait_all(up_copies)

    def step(k, carry):
        cols = pl.ds(pl.multiple_of(k * chunk, chunk), chunk)
        up_grad = (
            dot(dy_ref[...], w_down[:, cols]) * slope_ref[:, cols].astype(jnp.float32)
        ).astype(jnp.bfloat16)
        du_ref[:, cols] = up_grad
        bias_sum_ref[0:1, cols] = column_sum(up_grad)
        acc[...] += contract_last(up_grad, w_up[:, cols])
        return carry

    lax.fori_loop(0, w_up.shape[1] // chunk, step, 0)


def middle_back_kernel(paths, rows, out_cols, me_ref, *refs):
    acc_ref, h_ref, dy_ref, vec_ref = refs[:4]
    parts = refs[4:8]
    dh_ref, dz_ref, do_keep_ref, do_send_ref, sum_ref = refs[8:13]
    w_out, sems = refs[13:]
    left_first = me_ref[1] == 0
    copies = start_place(
        paths[0], rows, parts, me_ref, [(w_out, 0, out_cols, out_cols, 0)], sems
    )
    out_grad = dy_ref[...].astype(jnp.float32)
    unit, inverse = normed(h_ref[...])
    grads = acc_ref[...]
    middle_grad = out_grad + normed_back(grads, unit, inverse, vec_ref[5:6, :])
    dh_ref[...] = middle_grad
    attn_grad = middle_grad.astype(jnp.bfloat16)
    dz_ref[...] = attn_grad
    wait_all(copies)
    half = do_keep_ref.shape[1]
    left = contract_last(attn_grad, w_out[:half, :])
    right = contract_last(attn_grad, w_out[half:, :])
    do_keep_ref[...] = jnp.where(left_first, left, right).astype(jnp.bfloat16)
    do_send_ref[...] = jnp.where(left_first, right, left).astype(jnp.bfloat16)
    sum_ref[...] = jnp.concatenate(
        [
            column_sum(attn_grad),
            column_sum(grads * unit),
            column_sum(grads),
            column_sum(out_grad),
            jnp.zeros((4, out_grad.shape[1]), jnp.float32),
        ],
        axis=0,
    )


def result_kernel(paths, rows, down_cut, me_ref, *refs):
    g_ref, h_ref, vec_ref = refs[:3]
    parts = refs[3:11]
    res_ref, w_down, sems = refs[11:]
    wait_all(place_down(paths, rows, down_cut, parts, me_ref, w_down, sems))
    for first in range(0, w_down.shape[0], 256):
        cols = slice(first, first + 256)
        res_ref[:, cols] = (
            h_ref[:, cols] + contract_last(g_ref[...], w_down[cols, :]) + vec_ref[7:8, cols]
        ).astype(jnp.bfloat16)


def up_grad_kernel(paths, rows, cut, chunk, me_ref, *refs):
    a_ref, du_ref, mine_ref, other_ref, dz_ref, keep_ref, send_ref = refs[:7]
    grad_up, grad_out, left_t, sems = refs[7:]
    left_first = me_ref[1] == 0
    half = mine_ref.shape[1]
    left_t[...] = a_ref[...].T

    def step(k, carry):
        cols = pl.ds(pl.multiple_of(k * chunk, chunk), chunk)
        grad_up[:, cols] = dot(left_t[...], du_ref[:, cols]).astype(jnp.bfloat16)
        return carry

    lax.fori_loop(0, du_ref.shape[1] // chunk, step, 0)
    left = jnp.where(left_first, mine_ref[...], other_ref[...])
    right = jnp.where(left_first, other_ref[...], mine_ref[...])
    grad_out[:half, :] = contract_first(left, dz_ref[...]).astype(jnp.bfloat16)
    grad_out[half:, :] = contract_first(right, dz_ref[...]).astype(jnp.bfloat16)
    up_cols, out_cols = grad_up.shape[1] // 2, grad_out.shape[1] // 2
    pieces = [
        (paths[0], grad_up, up_cols, 0, cut, 0),
        (paths[1], grad_up, up_cols, cut, up_cols - cut, cut),
        (paths[1], grad_out, out_cols, 0, out_cols, up_cols),
    ]
    wait_all(start_split(rows, me_ref, pieces, keep_ref, send_ref, sems))


def project_back_kernel(path, rows, pairs, me_ref, *refs):
    grad_refs = refs[: 3 * pairs]
    w_ref, a_ref, own_ref, other_ref, vec_ref, sum_ref, bias_ref = refs[3 * pairs : 3 * pairs + 7]
    da_own_ref, da_send_ref, keep_ref, send_ref = refs[3 * pairs + 7 : 3 * pairs + 11]
    grads_all, grad, parts, small, small_out, a_t, sems = refs[3 * pairs + 11 :]
    seq = me_ref[1]
    piece = own_ref.shape[0]
    third = grads_all.shape[1] // 3
    small[...] = jnp.zeros_like(small)
    a_t[...] = a_ref[...].T
    for k in range(3):
        for pair in range(pairs):
            at = k * third + pair * 128
            grads_all[:, at : at + 128] = grad_refs[3 * pair + k][...]
        cols = slice(k * third, (k + 1) * third)
        grad[:, cols] = dot(a_t[...], grads_all[:, cols]).astype(jnp.bfloat16)
    pieces = [(path, grad, 0, 0, 3 * third, 0)]
    copies = start_split(rows, me_ref, pieces, keep_ref, send_ref, sems.at[0:1])
    for part in range(2):
        at = slice(part * piece, (part + 1) * piece)
        grads = contract_last(grads_all[at, :], w_ref[...])
        parts[part] = grads
        values = jnp.where(seq == part, own_ref[...], other_ref[...]).astype(jnp.float32)
        small[0:1, :] += column_sum(grads * normed(values)[0])
        small[1:2, :] += column_sum(grads)
    da_own_ref[...] = parts[seq]
    da_send_ref[...] = parts[1 - seq].astype(jnp.bfloat16)
    own_cols = pl.ds(pl.multiple_of(seq * third, 128), third)
    small[2:3, own_cols] = column_sum(grads_all[:, :third])
    small[3:4, own_cols] = column_sum(grads_all[:, 2 * third :])
    small[4:8, :] = sum_ref[0:4, :]
    bias_rows = bias_ref.shape[0]
    small[8 : 8 + bias_rows, :] = bias_ref[...]
    small_out[...] = small[...].T.astype(jnp.bfloat16)
    pieces = [(path, small_out, 0, 0, 128, 3 * third)]
    copies += start_split(rows, me_ref, pieces, keep_ref, send_ref, sems.at[1:2])
    wait_all(copies)


def add_kernel(cuts, count, *refs):
    ins, outs = refs[: 2 * count], refs[2 * count :]
    for pair, first, last, left, right, out, at in cuts:
        keep, other = ins[2 * pair], ins[2 * pair + 1]
        total = keep[first:last, :, left:right].astype(jnp.float32) + other[
            first:last, :, left:right
        ].astype(jnp.float32)
        outs[out][:, :, at : at + right - left] = total.astype(outs[out].dtype)


def add_pairs(pairs, cuts, shapes):
    ins = [array for pair in pairs for array in pair]
    return pl.pallas_call(
        functools.partial(add_kernel, cuts, len(pairs)),
        out_shape=[jax.ShapeDtypeStruct(shape, jnp.bfloat16) for shape in shapes],
        in_specs=in_vmem(len(ins)),
        out_specs=in_vmem(len(shapes)),
        compiler_params=pltpu.CompilerParams(vmem_limit_bytes=VMEM_LIMIT),
    )(*ins)


def halves(pairs):
    cuts, shapes = [], []
    for k, (keep, _) in enumerate(pairs):
        slots, rows, cols = keep.shape
        for part in range(2):
            cuts.append((k, part * slots // 2, (part + 1) * slots // 2, 0, cols, len(shapes), 0))
            shapes.append((slots // 2, rows, cols))
    return add_pairs(pairs, cuts, shapes)


def quarters(keep, other, cut):
    slots, rows, cols = keep.shape
    cuts, shapes = [], []
    for left, right in ((0, cut), (cut, cols)):
        for part in range(2):
            cuts.append(
                (0, part * slots // 2, (part + 1) * slots // 2, left, right, len(shapes), 0)
            )
            shapes.append((slots // 2, rows, right - left))
    return add_pairs([(keep, other)], cuts, shapes)


def rejoin(pairs):
    slots, rows, left_cols = pairs[0][0].shape
    right_cols = pairs[1][0].shape[2]
    cuts, shapes = [], []
    for part in range(2):
        first, last = part * slots // 2, (part + 1) * slots // 2
        cuts.append((0, first, last, 0, left_cols, part, 0))
        cuts.append((1, first, last, 0, right_cols, part, left_cols))
        shapes.append((slots // 2, rows, left_cols + right_cols))
    return add_pairs(pairs, cuts, shapes)


def head_lanes(values, head, width):
    lane = lax.broadcasted_iota(jnp.int32, values.shape, 1)
    return jnp.where(lane // width == head, values, jnp.zeros_like(values))


def later_keys(block):
    key_at = lax.broadcasted_iota(jnp.int32, (block, block), 0)
    query_at = lax.broadcasted_iota(jnp.int32, (block, block), 1)
    return key_at > query_at


def scores_of(keys, query, hidden_keys, block):
    scores = contract_last(keys, query)
    last = jnp.where(hidden_keys, MASKED, scores[-block:])
    if scores.shape[0] == block:
        return last
    return jnp.concatenate([scores[:-block], last], axis=0)


def attend_kernel(block, width, q_ref, k_ref, v_ref, out_ref, lse_ref):
    length, lanes = q_ref.shape
    scale = jnp.bfloat16(width ** (-0.5))
    hidden_keys = later_keys(block)
    values_t = v_ref[...].T
    for first in range(0, length, block):
        last = first + block
        queries = q_ref[first:last, :] * scale
        outs = []
        for head in range(lanes // width):
            scores = scores_of(k_ref[:last, :], head_lanes(queries, head, width), hidden_keys, block)
            top = jnp.max(scores, axis=0, keepdims=True)
            probs = jnp.exp(scores - top)
            total = jnp.sum(probs, axis=0, keepdims=True)
            mixed = jnp.dot(
                values_t[head * width : (head + 1) * width, :last],
                probs.astype(jnp.bfloat16),
                preferred_element_type=jnp.float32,
            )
            outs.append(mixed / total)
            lse_ref[head : head + 1, first:last] = top + jnp.log(total)
        out_ref[first:last, :] = jnp.concatenate(outs, axis=0).T.astype(jnp.bfloat16)


def attend_back_kernel(
    block, width, q_ref, k_ref, v_ref, g_ref, o_ref, lse_ref, dq_ref, dk_ref, dv_ref, dk_acc, dv_acc
):
    length, lanes = q_ref.shape
    heads = lanes // width
    scale = jnp.bfloat16(width ** (-0.5))
    hidden_keys = later_keys(block)
    keys_t = k_ref[...].T
    for first in reversed(range(0, length, block)):
        last = first + block
        queries = q_ref[first:last, :] * scale
        grads = g_ref[first:last, :]
        products = (grads.astype(jnp.float32) * o_ref[first:last, :].astype(jnp.float32)).T
        key_part = value_part = None
        query_parts = []
        for head in range(heads):
            query = head_lanes(queries, head, width)
            grad = head_lanes(grads, head, width)
            scores = scores_of(k_ref[:last, :], query, hidden_keys, block)
            probs = jnp.exp(scores - lse_ref[head : head + 1, first:last])
            delta = jnp.sum(products[head * width : (head + 1) * width], axis=0, keepdims=True)
            prob_grad = contract_last(v_ref[:last, :], grad)
            score_grad = (probs * (prob_grad - delta)).astype(jnp.bfloat16)
            key_term = jnp.dot(score_grad, query, preferred_element_type=jnp.float32)
            value_term = jnp.dot(
                probs.astype(jnp.bfloat16), grad, preferred_element_type=jnp.float32
            )
            key_part = key_term if key_part is None else key_part + key_term
            value_part = value_term if value_part is None else value_part + value_term
            query_parts.append(
                jnp.dot(
                    keys_t[head * width : (head + 1) * width, :last],
                    score_grad,
                    preferred_element_type=jnp.float32,
                )
            )
        query_grad = jnp.concatenate(query_parts, axis=0).T * width ** (-0.5)
        dq_ref[first:last, :] = query_grad.astype(jnp.bfloat16)
        if last == length:
            dk_acc[...] = key_part
            dv_acc[...] = value_part
        else:
            dk_acc[:last, :] += key_part
            dv_acc[:last, :] += value_part
    dk_ref[...] = dk_acc[...].astype(jnp.bfloat16)
    dv_ref[...] = dv_acc[...].astype(jnp.bfloat16)


def pair_spec(length, first):
    return pl.BlockSpec((length, 128), lambda pair: (0, first + pair))


def attend(qkv):
    length, cols = qkv.shape
    pairs = cols // 3 // 128
    return pl.pallas_call(
        functools.partial(attend_kernel, 256, HEAD_DIM),
        grid=(pairs,),
        out_shape=[
            jax.ShapeDtypeStruct((length, cols // 3), jnp.bfloat16),
            jax.ShapeDtypeStruct((8 * pairs, length), jnp.float32),
        ],
        in_specs=[pair_spec(length, k * pairs) for k in range(3)],
        out_specs=[pair_spec(length, 0), pl.BlockSpec((8, length), lambda pair: (pair, 0))],
        compiler_params=pltpu.CompilerParams(vmem_limit_bytes=VMEM_LIMIT),
        cost_estimate=COST,
    )(qkv, qkv, qkv)


def attend_back(qkv, grads, attended, lse, pair):
    length, cols = qkv.shape
    pairs = cols // 3 // 128
    column = functools.partial(pair_spec, length)
    return pl.pallas_call(
        functools.partial(attend_back_kernel, 256, HEAD_DIM),
        grid=(1,),
        out_shape=[jax.ShapeDtypeStruct((length, 128), jnp.bfloat16)] * 3,
        in_specs=[column(k * pairs + pair) for k in range(3)]
        + [column(pair)] * 2
        + [pl.BlockSpec((8, length), lambda step: (pair, 0))],
        out_specs=[column(0)] * 3,
        scratch_shapes=[pltpu.VMEM((length, 128), jnp.float32)] * 2,
        compiler_params=pltpu.CompilerParams(vmem_limit_bytes=VMEM_LIMIT),
        cost_estimate=COST,
    )(qkv, qkv, qkv, grads, attended, lse)


def in_order(seq_index, mine, other, axis):
    return jnp.where(
        seq_index == 0,
        jnp.concatenate([mine, other], axis=axis),
        jnp.concatenate([other, mine], axis=axis),
    )


def on_device(inputs, vectors, w_qkv, w_out, w_up, w_down, up_bias, cotangent):
    _, piece_len, model_width = inputs.shape
    sizes = {"dp": lax.axis_size("dp"), "seq": lax.axis_size("seq")}
    seq_index = lax.axis_index("seq")
    pair = jnp.stack([lax.axis_index("dp"), seq_index])
    swap = ("seq", 1)
    half_width = model_width // 2
    dp_masks = bit_masks(sizes["dp"])
    core, row_hop = ("dp", dp_masks[0]), ("dp", dp_masks[1])
    far = [("dp", mask) for mask in reversed(dp_masks[2:])]
    path_dp = far + [row_hop, core]
    paths = (far + [swap, row_hop, core], far + [row_hop, swap, core])
    rows = w_qkv.shape[0]
    per_row = up_bias.shape[0] // rows

    bias_cols = up_bias.reshape(per_row, rows).T
    small_own = jnp.concatenate(
        [vectors, bias_cols, jnp.zeros((rows, 128 - 8 - per_row), vectors.dtype)], axis=1
    )
    blocks = [w_qkv[:, k * half_width : (k + 1) * half_width] for k in range(3)]
    arrived = exchange(jnp.concatenate([blocks[1], small_own], axis=1), swap, sizes)
    head_cols = jnp.where(
        seq_index == 0,
        jnp.concatenate([blocks[0], blocks[2], arrived[:, :half_width]], axis=1),
        jnp.concatenate([arrived[:, :half_width], blocks[0], blocks[2]], axis=1),
    )
    bias_other = arrived[:, half_width + 8 : half_width + 8 + per_row]
    small_cols = jnp.concatenate(
        [
            vectors,
            in_order(seq_index, bias_cols, bias_other, 1),
            jnp.zeros((rows, 128 - 8 - 2 * per_row), vectors.dtype),
        ],
        axis=1,
    )
    x_own = inputs.reshape(piece_len, model_width)
    x_other = exchange(x_own, swap, sizes)
    first = jnp.concatenate([head_cols, small_cols], axis=1)[None]
    a_held = jnp.concatenate([w_out, w_up], axis=1)[None]
    b_held = w_down[None]
    up_cols = w_up.shape[1]
    cut, down_cut = 8 * a_held.shape[2] // 15 // 128 * 128, up_cols // 2
    for hop in far:
        a_held = grow(a_held, hop, sizes)
        first = grow(first, hop, sizes)
    b_held = grow(after(b_held, first), far[0], sizes)
    a_halves = [a_held[:, :, :cut], a_held[:, :, cut:]]
    a_next = [exchange(part, paths[k][len(far)], sizes) for k, part in enumerate(a_halves)]
    first = grow(first, row_hop, sizes)
    b_next = exchange(b_held, far[1], sizes)
    first_parts = [first, exchange(first, core, sizes)]

    bf16, f32 = jnp.bfloat16, jnp.float32
    seq_len, ff = 2 * piece_len, 2 * w_up.shape[1]
    head_width = 3 * half_width
    dense = 2 * piece_len * model_width
    dma = pltpu.SemaphoreType.DMA
    qkv_rows, normed_one, qkv_full, vec_rows = local_call(
        functools.partial(project_kernel, path_dp, rows),
        pair,
        [x_own, x_other],
        first_parts,
        [
            shaped(bf16, seq_len, head_width),
            shaped(bf16, seq_len, model_width),
            shaped(bf16, model_width, head_width),
            shaped(f32, 16, model_width),
        ],
        [],
        [pltpu.VMEM((model_width, 128), bf16), dma((2, sizes["dp"]))],
        2 * dense * head_width,
    )
    bias_row = jnp.transpose(
        vec_rows[8 : 8 + 2 * per_row].reshape(2 * per_row, sizes["dp"], rows), (1, 0, 2)
    ).reshape(1, ff)
    a_halves = [
        jnp.concatenate([a_halves[k], after(a_next[k], qkv_rows)], axis=0) for k in range(2)
    ]
    a_more = [exchange(part, paths[k][len(far) + 1], sizes) for k, part in enumerate(a_halves)]
    b_held = jnp.concatenate([b_held, after(b_next, qkv_rows)], axis=0)
    b_halves = [b_held[:, :, :down_cut], b_held[:, :, down_cut:]]
    b_next = [exchange(part, paths[k][len(far)], sizes) for k, part in enumerate(b_halves)]
    attended, lse = attend(after(qkv_rows, *a_halves, *b_halves))

    def crossed(parts, more):
        pieces = []
        for k in range(2):
            both = (parts[k], more[k])
            pieces += [*both, *[exchange(part, core, sizes) for part in both]]
        return pieces

    def tokens_of(values, index):
        return lax.dynamic_slice_in_dim(values, index * piece_len, piece_len, 0)

    attended_own = tokens_of(attended, seq_index)
    attended_other = exchange(tokens_of(attended, 1 - seq_index), swap, sizes)
    a_parts = crossed(a_halves, [after(part, attended) for part in a_more])
    b_halves = [
        jnp.concatenate([b_halves[k], after(b_next[k], attended)], axis=0) for k in range(2)
    ]
    b_more = [exchange(part, paths[k][len(far) + 1], sizes) for k, part in enumerate(b_halves)]
    mlp_grad = cotangent.reshape(piece_len, model_width)
    slots = sizes["dp"] * sizes["seq"]
    chunk = math.gcd(ff, 1024)
    weight_scratch = [
        pltpu.VMEM((model_width, model_width), bf16),
        pltpu.VMEM((model_width, ff), bf16),
    ]
    middle, normed_two, hidden, slope = local_call(
        functools.partial(hidden_kernel, paths, rows, cut, chunk),
        pair,
        [attended_own, attended_other, after(x_own, *b_halves), vec_rows, bias_row],
        a_parts,
        [
            shaped(f32, piece_len, model_width),
            shaped(bf16, piece_len, model_width),
            shaped(bf16, piece_len, ff),
            shaped(bf16, piece_len, ff),
        ],
        [],
        weight_scratch + [dma((3, slots))],
        dense * (model_width + ff),
    )
    b_parts = crossed(b_halves, [after(part, hidden) for part in b_more])
    down_keep, down_send = local_call(
        functools.partial(down_grad_kernel, paths, rows, down_cut, chunk),
        pair,
        [hidden, mlp_grad],
        [],
        [],
        [shaped(bf16, slots // 2, rows, ff // 2)] * 2,
        [
            pltpu.VMEM((model_width, ff), bf16),
            pltpu.VMEM((model_width, piece_len), bf16),
            dma((2, slots)),
        ],
        dense * ff,
    )

    down_other = exchange(down_send, core, sizes)
    up_grad, norm_two_grad, bias_sums = local_call(
        functools.partial(
            mlp_back_kernel, paths, rows, cut, down_cut, w_out.shape[1], chunk
        ),
        pair,
        [slope, after(mlp_grad, down_keep)],
        a_parts + b_parts,
        [
            shaped(bf16, piece_len, ff),
            shaped(f32, piece_len, model_width),
            shaped(f32, 8, ff),
        ],
        [],
        [pltpu.VMEM((model_width, ff), bf16)] * 2 + [dma((2, slots)), dma((2, slots))],
        2 * dense * ff,
    )
    down_keeps, down_sends = [None] * 2, [None] * 2
    down_keeps[0], down_sends[0], down_keeps[1], down_sends[1] = quarters(
        down_keep, after(down_other, norm_two_grad), down_cut
    )
    down_others = [exchange(down_sends[k], (swap, row_hop)[1 - k], sizes) for k in range(2)]
    middle_grad, attn_out_grad, grads_own, grads_send, sums = local_call(
        functools.partial(middle_back_kernel, paths, rows, w_out.shape[1]),
        pair,
        [after(norm_two_grad, *down_keeps), middle, mlp_grad, vec_rows],
        a_parts[:4],
        [
            shaped(f32, piece_len, model_width),
            shaped(bf16, piece_len, model_width),
            shaped(bf16, piece_len, half_width),
            shaped(bf16, piece_len, half_width),
            shaped(f32, 8, model_width),
        ],
        [],
        [weight_scratch[0], dma((1, slots))],
        dense * model_width,
    )
    grads_other = exchange(grads_send, swap, sizes)
    back_cut = 8 * (up_cols + w_out.shape[1]) // 15 // 128 * 128
    up_keep, up_send = local_call(
        functools.partial(up_grad_kernel, paths, rows, back_cut, chunk),
        pair,
        [normed_two, up_grad, attended_own, attended_other, attn_out_grad],
        [],
        [],
        [shaped(bf16, slots // 2, rows, (ff + model_width) // 2)] * 2,
        [
            pltpu.VMEM((model_width, ff), bf16),
            pltpu.VMEM((model_width, model_width), bf16),
            pltpu.VMEM((model_width, piece_len), bf16),
            dma((3, slots)),
        ],
        dense * (model_width + ff),
    )
    up_other = exchange(up_send, core, sizes)
    grad_heads = in_order(seq_index, grads_own, after(grads_other, up_keep), 0)
    down_others = [after(part, up_keep) for part in down_others]
    down_sums = halves([(down_keeps[k], down_others[k]) for k in range(2)])
    down_keeps, down_sends = down_sums[0::2], down_sums[1::2]
    down_others = [exchange(down_sends[k], (swap, row_hop)[k], sizes) for k in range(2)]

    def head_pair_back(at, *earlier):
        return attend_back(qkv_rows, grad_heads, attended, lse, at)

    pair_grads = [head_pair_back(0)]
    up_keeps, up_sends = [None] * 2, [None] * 2
    up_keeps[0], up_sends[0], up_keeps[1], up_sends[1] = quarters(
        up_keep, after(up_other, pair_grads[0][0]), back_cut
    )
    down_keep, down_send = rejoin(
        [(down_keeps[k], after(down_others[k], pair_grads[0][0])) for k in range(2)]
    )
    up_others = [exchange(up_sends[k], (swap, row_hop)[1 - k], sizes) for k in range(2)]
    down_other = exchange(down_send, far[1], sizes)
    pair_grads += [head_pair_back(at) for at in range(1, half_width // 128)]
    down_keep, down_send = halves([(down_keep, down_other)])
    down_other = exchange(down_send, far[0], sizes)
    bias_rows = jnp.transpose(
        bias_sums[0].reshape(sizes["dp"], 2 * per_row, rows), (1, 0, 2)
    ).reshape(2 * per_row, model_width)
    da_own, da_send, last_keep, last_send = local_call(
        functools.partial(project_back_kernel, path_dp, rows, half_width // 128),
        pair,
        [
            *[grad for group in pair_grads for grad in group],
            qkv_full,
            normed_one,
            x_own,
            x_other,
            vec_rows,
            sums,
            bias_rows,
        ],
        [],
        [shaped(f32, piece_len, model_width), shaped(bf16, piece_len, model_width)],
        [shaped(bf16, sizes["dp"] // 2, rows, head_width + 128)] * 2,
        [
            pltpu.VMEM((seq_len, head_width), bf16),
            pltpu.VMEM((model_width, head_width), bf16),
            pltpu.VMEM((2, piece_len, model_width), f32),
            pltpu.VMEM((128, model_width), f32),
            pltpu.VMEM((model_width, 128), bf16),
            pltpu.VMEM((model_width, seq_len), bf16),
            dma((2, sizes["dp"])),
        ],
        4 * dense * head_width,
    )
    last_other = exchange(last_send, core, sizes)
    up_sums = halves([(up_keeps[k], after(up_others[k], da_own)) for k in range(2)])
    up_keeps, up_sends = up_sums[0::2], up_sums[1::2]
    up_others = [exchange(up_sends[k], (swap, row_hop)[k], sizes) for k in range(2)]
    da_other = exchange(da_send, swap, sizes)
    last_keep, last_send = halves([(last_keep, last_other)])
    last_other = exchange(last_send, row_hop, sizes)
    up_keep, up_send = rejoin([(up_keeps[k], after(up_others[k], last_send)) for k in range(2)])
    up_other = exchange(up_send, far[1], sizes)
    grad_down = down_keep[0].astype(f32) + after(down_other, last_send)[0].astype(f32)
    (result,) = local_call(
        functools.partial(result_kernel, paths, rows, down_cut),
        pair,
        [hidden, after(middle, last_send, up_send), vec_rows],
        b_parts,
        [shaped(bf16, piece_len, model_width)],
        [],
        [pltpu.VMEM((model_width, ff), bf16), dma((2, slots))],
        dense * ff,
    )
    last_keep, last_send = halves([(last_keep, after(last_other, result))])
    last_other = exchange(last_send, far[1], sizes)
    up_keep, up_send = halves([(up_keep, after(up_other, last_send))])
    up_other = exchange(up_send, far[0], sizes)
    norm_one_own = da_own + after(da_other, last_send).astype(f32)
    unit, inverse = normed(x_own.astype(f32))
    input_grad = middle_grad + normed_back(norm_one_own, unit, inverse, vec_rows[0:1])
    last_keep, last_send = halves([(last_keep, after(last_other, input_grad))])
    last_other = exchange(last_send, far[0], sizes)
    up_other = after(up_other, last_send)
    grad_up_out = up_keep[0].astype(f32) + up_other[0].astype(f32)
    grad_up, grad_out = grad_up_out[:, :up_cols], grad_up_out[:, up_cols:]
    last = last_keep[0].astype(f32) + last_other[0].astype(f32)
    small_last = last[:, 3 * half_width :]
    sent = jnp.where(
        seq_index == 0, last[:, 2 * half_width :],
        jnp.concatenate([last[:, :half_width], small_last], axis=1)
    )
    arrived_last = exchange(sent.astype(jnp.bfloat16), swap, sizes).astype(jnp.float32)
    middle_block = arrived_last[:, :half_width]
    kept = jnp.where(seq_index == 0, last[:, : 2 * half_width], last[:, half_width : 3 * half_width])
    grad_qkv = jnp.concatenate([kept[:, :half_width], middle_block, kept[:, half_width:]], axis=1)
    small_sum = small_last + arrived_last[:, half_width:]
    grad_vectors = small_sum[:, :8]
    bias_own = lax.dynamic_slice_in_dim(small_sum, 8 + seq_index * per_row, per_row, 1)
    grad_up_bias = bias_own.T.reshape(-1)
    return (
        result.reshape(1, piece_len, model_width),
        input_grad.reshape(1, piece_len, model_width),
        grad_qkv,
        grad_out,
        grad_up,
        grad_down,
        grad_up_bias,
        grad_vectors,
    )


def block(*arrays):
    n_dp, n_seq = lax.axis_size("dp"), lax.axis_size("seq")
    rows = arrays[2].shape[0]
    whole_tiles = rows % 16 == 0 and all(weight.shape[1] % 384 == 0 for weight in arrays[2:6])
    powers = n_dp == 16
    if n_seq == 2 and powers and whole_tiles and arrays[0].shape[0] == 1:
        return on_device(*arrays)
    return on_device_general(*arrays)


def solution(mesh):
    placed = (
        P("dp", "seq", None),
        P("dp", None),
        P("dp", "seq"),
        P("dp", "seq"),
        P("dp", "seq"),
        P("dp", "seq"),
        P(("dp", "seq")),
        P("dp", "seq", None),
    )
    return jax.shard_map(
        block,
        mesh=mesh,
        in_specs=placed,
        out_specs=(
            P("dp", "seq", None),
            P("dp", "seq", None),
            P("dp", "seq"),
            P("dp", "seq"),
            P("dp", "seq"),
            P("dp", "seq"),
            P(("dp", "seq")),
            P("dp", None),
        ),
        check_vma=False,
    )
```
